32 devices in a mesh: rows: 2 (over core), seq: 4 (over y, x), tensor: 4 (over z).
Axes of the slice: x: 2, y: 2, z: 4, core: 2. Of those that a mesh axis runs over, the one named last changes fastest.
Arguments:
- activations: bfloat16 [2, 1280, 2048], P('rows', 'seq'), may hold values from -6 to 6
- doc_lengths: int32 [2, 4], P('rows'), may hold values from 1 to 1276, as said below
- w_query: bfloat16 [2048, 2048], P(None, 'tensor'), may hold values from -0.125 to 0.125
- key_matrix: bfloat16 [2048, 512], P(None, 'tensor'), may hold values from -0.125 to 0.125
- value_matrix: bfloat16 [2048, 512], P(None, 'tensor'), may hold values from -0.125 to 0.125
- w_output: bfloat16 [2048, 2048], P('tensor'), may hold values from -0.75 to 0.75
- w_gate: bfloat16 [2048, 8192], P(None, 'tensor'), may hold values from -0.125 to 0.125
- w_up: bfloat16 [2048, 8192], P(None, 'tensor'), may hold values from -0.125 to 0.125
- w_down: bfloat16 [8192, 2048], P('tensor'), may hold values from -0.0625 to 0.0625
- gain_attn: float32 [2048], replicated, may hold values from 0.5 to 1.5
- gain_ffn: float32 [2048], replicated, may hold values from 0.5 to 1.5
- cotangent: bfloat16 [2, 1280, 2048], P('rows', 'seq'), may hold values from -6 to 6
Outputs:
- block_output: bfloat16 [2, 1280, 2048], P('rows', 'seq')
- grad_activations: bfloat16 [2, 1280, 2048], P('rows', 'seq')
- grad_w_query: float32 [2048, 2048], P(None, 'tensor')
- grad_w_key: float32 [2048, 512], P(None, 'tensor')
- grad_w_value: float32 [2048, 512], P(None, 'tensor')
- grad_w_output: float32 [2048, 2048], P('tensor')
- grad_w_gate: float32 [2048, 8192], P(None, 'tensor')
- grad_w_up: float32 [2048, 8192], P(None, 'tensor')
- grad_w_down: float32 [8192, 2048], P('tensor')
- grad_gain_attn: float32 [2048], replicated
- grad_gain_ffn: float32 [2048], replicated
The draws below stay inside these ranges and needn't reach their ends.
Inputs may be any that keep to these rules, and one draw needn't show every extreme that they name: `doc_lengths`: each row's lengths sum to less than 1280; the rest of the row is padding. In every row one document starts within the first 320 places and ends within the last 320.
All inputs are finite; a program needn't handle non-finite values.
Results may differ from the reference program's by a relative error of at most 0.023.
Values may be sent and summed in bfloat16 or wider, within the bound.
No kernel may reach another device: no remote copies, remote signals or barrier semaphores. Data moves between devices by JAX's collectives and lax.ppermute only.
A program may use at most 256 MiB of HBM per device.

```python
import jax
import jax.numpy as jnp
from jax import lax

MODEL_WIDTH = 2048
QUERY_HEADS = 32
KEY_VALUE_HEADS = 8
HEAD_SIZE = 64
FF = 8192
SPAN = 320
DOCS = 4
PACKED_LENGTH = 1280
ROWS = 2


def draw_doc_lengths(key, part):
    key = jax.random.fold_in(key, 7)
    short_key, pad_key, pick_key = jax.random.split(key, 3)
    shorts = jax.random.randint(short_key, (ROWS, DOCS), 1, SPAN // DOCS)
    padding = jax.random.randint(pad_key, (ROWS, 1), 1, SPAN // DOCS)
    longest = jax.random.randint(pick_key, (ROWS, 1), 0, DOCS)
    chosen = jnp.arange(DOCS, dtype=jnp.int32)[None, :] == longest
    others = jnp.sum(jnp.where(chosen, 0, shorts), axis=1, keepdims=True)
    return jnp.where(chosen, PACKED_LENGTH - padding - others, shorts).astype(jnp.int32)


def shard_levels(rng, dims, shards, smallest, top_value):
    gain = 1.0
    for dim, blocks in shards:
        steps = jax.random.uniform(jax.random.fold_in(jax.random.fold_in(rng, 6), dim), (blocks,), jnp.float32, smallest / len(shards), top_value / len(shards))
        gain = gain * jnp.repeat(jnp.exp(steps), dims[dim] // blocks).reshape((-1,) + (1,) * (len(dims) - 1 - dim))
    return gain


def scatter_about(rng, dims, width, limit, cuts=(), kind=jnp.bfloat16):
    values = jax.random.normal(rng, dims, jnp.float32) * width
    if len(cuts) > 0:
        values = shard_levels(rng, dims, cuts, -0.22, 0.18) * values
    return jnp.clip(values, min=-limit, max=limit).astype(kind)


def setup_inputs(seed: int = 0) -> dict:
    keys = jax.random.split(jax.random.key(seed), 13)
    return {
        "activations": scatter_about(keys[0], (ROWS, PACKED_LENGTH, MODEL_WIDTH), 1.0, 6.0, ((0, 2), (1, 4))),
        "doc_lengths": draw_doc_lengths(jax.random.fold_in(keys[12], 71), 0),
        "w_query": scatter_about(keys[2], (MODEL_WIDTH, QUERY_HEADS * HEAD_SIZE), MODEL_WIDTH ** -0.5, 0.125, ((1, 4),)),
        "key_matrix": scatter_about(keys[3], (MODEL_WIDTH, KEY_VALUE_HEADS * HEAD_SIZE), MODEL_WIDTH ** -0.5, 0.125, ((1, 4),)),
        "value_matrix": scatter_about(keys[4], (MODEL_WIDTH, KEY_VALUE_HEADS * HEAD_SIZE), MODEL_WIDTH ** -0.5, 0.125, ((1, 4),)),
        "w_output": scatter_about(keys[5], (QUERY_HEADS * HEAD_SIZE, MODEL_WIDTH), (QUERY_HEADS * HEAD_SIZE // 32) ** -0.5, 0.75, ((0, 4),)),
        "w_gate": scatter_about(keys[6], (MODEL_WIDTH, FF), MODEL_WIDTH ** -0.5, 0.125, ((1, 4),)),
        "w_up": scatter_about(keys[7], (MODEL_WIDTH, FF), MODEL_WIDTH ** -0.5, 0.125, ((1, 4),)),
        "w_down": scatter_about(keys[8], (FF, MODEL_WIDTH), FF ** -0.5, 0.0625, ((0, 4),)),
        "gain_attn": jnp.clip(1.0 + 0.1 * jax.random.normal(keys[9], (MODEL_WIDTH,), jnp.float32), 0.5, 1.5),
        "gain_ffn": jnp.clip(1.0 + 0.1 * jax.random.normal(keys[10], (MODEL_WIDTH,), jnp.float32), 0.5, 1.5),
        "cotangent": scatter_about(keys[11], (ROWS, PACKED_LENGTH, MODEL_WIDTH), 1.0, 6.0, ((0, 2), (1, 4))),
    }


@jax.custom_vjp
def lower_precision(v):
    return lax.optimization_barrier(v.astype(jnp.bfloat16)).astype(jnp.float32)

@jax.custom_vjp
def lower_backward(v):
    return v

def low_keep(v):
    return (lower_precision(v), None)

def low_pass(kept, grad):
    return (grad,)

def back_keep(v):
    return (v, None)

def back_low(kept, grad):
    return (lower_precision(grad),)
lower_precision.defvjp(low_keep, low_pass)
lower_backward.defvjp(back_keep, back_low)

def rope_tables(positions):
    half = HEAD_SIZE // 2
    expo = jnp.arange(half, dtype=jnp.float32) * 2.0 / HEAD_SIZE
    inverse = 1.0 / 500000.0 ** expo
    wavelength = 2.0 * jnp.pi / inverse
    smooth = (8192.0 / wavelength - 1.0) / 3.0
    middle = (1.0 - smooth) * inverse / 32.0 + smooth * inverse
    scaled = jnp.where(wavelength < 2048.0, inverse, jnp.where(wavelength > 8192.0, inverse / 32.0, middle))
    angles = positions.astype(jnp.float32)[:, None] * scaled[None, :]
    return (jnp.cos(angles), jnp.sin(angles))

def apply_rotation(values, cosine_table, sine_table):
    half = values.shape[-1] // 2
    first = values[..., :half]
    second = values[..., half:]
    cosine_table = cosine_table[:, None, :]
    sine_table = sine_table[:, None, :]
    return jnp.concatenate([first * cosine_table - second * sine_table, second * cosine_table + first * sine_table], axis=-1)

def layout(row_lengths, places):
    ends = jnp.cumsum(row_lengths).astype(jnp.int32)
    starts = (ends - row_lengths).astype(jnp.int32)
    segment = lax.optimization_barrier(jnp.sum((places[:, None] >= ends[None, :]).astype(jnp.int32), axis=1)).astype(jnp.int32)
    labels = jnp.arange(row_lengths.shape[0], dtype=jnp.int32)
    begin = lax.optimization_barrier(jnp.sum(jnp.where(segment[:, None] == labels[None, :], starts[None, :], 0), axis=1)).astype(jnp.int32)
    begin = begin + jnp.where(segment == row_lengths.shape[0], ends[-1], 0).astype(jnp.int32)
    return (segment, (places - begin).astype(jnp.int32))

def rms_scale(values):
    return lax.rsqrt(lax.optimization_barrier(jnp.mean(values * values, axis=-1, keepdims=True)) + 1e-05)

def layer(stream, params, segment, places, cosine_table, sine_table):
    w_query, key_matrix, value_matrix, w_output, w_gate, w_up, w_down, gain_attn, gain_ffn = params
    highest_precision = lax.Precision.HIGHEST
    query_group = QUERY_HEADS // KEY_VALUE_HEADS
    scale = HEAD_SIZE ** (-0.5)
    first_normed = lower_precision(stream * rms_scale(stream) * gain_attn)
    query_rows = lower_backward(jnp.dot(first_normed, w_query, precision=highest_precision)).reshape(PACKED_LENGTH, QUERY_HEADS, HEAD_SIZE)
    key = lower_backward(jnp.dot(first_normed, key_matrix, precision=highest_precision)).reshape(PACKED_LENGTH, KEY_VALUE_HEADS, HEAD_SIZE)
    value_rows = lower_precision(lower_backward(jnp.dot(first_normed, value_matrix, precision=highest_precision))).reshape(PACKED_LENGTH, KEY_VALUE_HEADS, HEAD_SIZE)
    query_rows = lower_precision(apply_rotation(query_rows, cosine_table, sine_table)).reshape(PACKED_LENGTH, KEY_VALUE_HEADS, query_group, HEAD_SIZE).transpose(1, 0, 2, 3)
    key = lower_precision(apply_rotation(key, cosine_table, sine_table)).transpose(1, 0, 2)
    value_rows = value_rows.transpose(1, 0, 2)
    allowed = (segment[:, None] == segment[None, :]) & (places[:, None] >= places[None, :])

    def one_head(pack):
        query_head, key_head, value_head = pack
        scores = lower_backward(jnp.einsum('cgd,wd->gcw', query_head, key_head, precision=highest_precision) * scale)
        scores = jnp.where(allowed[None], scores, -1e+30)
        top = lax.optimization_barrier(jnp.max(scores, axis=-1, keepdims=True))
        weights = jnp.exp(scores - top)
        probs = lower_precision(weights / lax.optimization_barrier(jnp.sum(weights, axis=-1, keepdims=True)))
        return jnp.einsum('gcw,wd->cgd', probs, value_head, precision=highest_precision)
    heads = lax.map(jax.checkpoint(one_head), (query_rows, key, value_rows))
    attended = lower_precision(lower_backward(heads.transpose(1, 0, 2, 3).reshape(PACKED_LENGTH, QUERY_HEADS * HEAD_SIZE)))
    middle = stream + lower_backward(jnp.dot(attended, w_output, precision=highest_precision))
    normed_two = lower_precision(middle * rms_scale(middle) * gain_ffn)
    gate = lower_backward(jnp.dot(normed_two, w_gate, precision=highest_precision))
    up = lower_backward(jnp.dot(normed_two, w_up, precision=highest_precision))
    hidden = lower_precision(jax.nn.silu(gate) * up)
    return middle + lower_backward(jnp.dot(hidden, w_down, precision=highest_precision))

def reference(activations, doc_lengths, w_query, key_matrix, value_matrix, w_output, w_gate, w_up, w_down, gain_attn, gain_ffn, cotangent):
    params = (w_query.astype(jnp.float32), key_matrix.astype(jnp.float32), value_matrix.astype(jnp.float32), w_output.astype(jnp.float32), w_gate.astype(jnp.float32), w_up.astype(jnp.float32), w_down.astype(jnp.float32), gain_attn.astype(jnp.float32), gain_ffn.astype(jnp.float32))
    places = jnp.arange(PACKED_LENGTH, dtype=jnp.int32)

    def one_row(totals, pack):
        row_input, row_lengths, row_cotangent = pack
        segment, position = layout(row_lengths.astype(jnp.int32), places)
        cosine_table, sine_table = rope_tables(position)
        valid = (segment < DOCS).astype(jnp.float32)

        def forward(stream, weights):
            return layer(stream, weights, segment, places, cosine_table, sine_table)
        result, pull = jax.vjp(forward, row_input.astype(jnp.float32), params)
        grad_stream, grad_params = pull(row_cotangent.astype(jnp.float32) * valid[:, None])
        totals = tuple((a + b for a, b in zip(totals, grad_params)))
        return (totals, (result.astype(jnp.bfloat16), grad_stream.astype(jnp.bfloat16)))
    start_totals = tuple((jnp.zeros(w.shape, jnp.float32) for w in params))
    totals, (outputs, grad_inputs) = lax.scan(one_row, start_totals, (activations, doc_lengths, cotangent))
    return (outputs, grad_inputs, totals[0], totals[1], totals[2], totals[3], totals[4], totals[5], totals[6], totals[7], totals[8])
```

```python
import functools

import jax
import jax.numpy as jnp
from jax import lax
from jax.experimental import pallas as pl
from jax.experimental.pallas import tpu as pltpu
from jax.sharding import PartitionSpec as P

HEAD_SIZE = 64
DOCS = 4
EPSILON = 1e-05
BF = jnp.bfloat16
F32 = jnp.float32


MIB = 1 << 20


def kernel_params(dims):
    return pltpu.CompilerParams(
        vmem_limit_bytes=56 * MIB, dimension_semantics=("arbitrary",) * dims
    )


def contract(a, b, dim_a, dim_b):
    return lax.dot_general(
        a, b, (((dim_a,), (dim_b,)), ((), ())), preferred_element_type=F32
    )


def tile(limit, size):
    while size > limit and size % 2 == 0:
        size //= 2
    return size


def cost(flops, moved, exps=0):
    return pl.CostEstimate(
        flops=flops // 64, bytes_accessed=moved // 64, transcendentals=exps // 64
    )


def hidden_half_kernel(core, upstream, weight, out):
    out[...] = contract(upstream[...], weight[...], 1, 1).astype(BF)


def grad_hidden_half(core, upstream, w_down):
    tokens, depth = upstream.shape
    half = w_down.shape[0] // 2
    rows, cols = tile(640, tokens), tile(1024, half)
    steps = half // cols
    return pl.pallas_call(
        hidden_half_kernel,
        out_shape=jax.ShapeDtypeStruct((tokens, half), BF),
        grid_spec=pltpu.PrefetchScalarGridSpec(
            num_scalar_prefetch=1,
            grid=(steps, tokens // rows),
            in_specs=[
                pl.BlockSpec((rows, depth), lambda j, i, c: (i, 0)),
                pl.BlockSpec((cols, depth), lambda j, i, c: (c[0] * steps + j, 0)),
            ],
            out_specs=pl.BlockSpec((rows, cols), lambda j, i, c: (i, j)),
        ),
        compiler_params=kernel_params(2),
        cost_estimate=cost(
            2 * tokens * depth * half, 2 * (tokens * depth + half * depth + tokens * half)
        ),
        name="grad_hidden_half",
    )(core, upstream, w_down)


def swish_grads(gate, up_proj, grad_hidden):
    sigmoid = 1.0 / (1.0 + jnp.exp(-gate))
    activated = gate * sigmoid
    hidden = (activated * up_proj).astype(BF)
    grad_gate = (grad_hidden * up_proj * (sigmoid * (1.0 + gate * (1.0 - sigmoid)))).astype(BF)
    grad_up = (grad_hidden * activated).astype(BF)
    return hidden, grad_gate, grad_up


def feed_half_kernel(core, normed, gate_w, up_w, grad_hidden, hidden, grad_gate, grad_up):
    rows = normed[...]
    hidden[...], grad_gate[...], grad_up[...] = swish_grads(
        contract(rows, gate_w[...], 1, 0),
        contract(rows, up_w[...], 1, 0),
        grad_hidden[...].astype(F32),
    )


def feed_half(core, normed, w_gate, w_up, grad_hidden):
    tokens, depth = normed.shape
    half = w_gate.shape[1] // 2
    rows, cols = tile(640, tokens), tile(512, half)
    steps = half // cols
    out = jax.ShapeDtypeStruct((tokens, half), BF)
    weight = pl.BlockSpec((depth, cols), lambda j, i, c: (0, c[0] * steps + j))
    block = pl.BlockSpec((rows, cols), lambda j, i, c: (i, j))
    return pl.pallas_call(
        feed_half_kernel,
        out_shape=(out, out, out),
        grid_spec=pltpu.PrefetchScalarGridSpec(
            num_scalar_prefetch=1,
            grid=(steps, tokens // rows),
            in_specs=[
                pl.BlockSpec((rows, depth), lambda j, i, c: (i, 0)),
                weight,
                weight,
                block,
            ],
            out_specs=(block, block, block),
        ),
        compiler_params=kernel_params(2),
        cost_estimate=cost(
            4 * tokens * depth * half,
            2 * (tokens * depth + 2 * half * depth + 4 * tokens * half),
            tokens * half,
        ),
        name="feed_half",
    )(core, normed, w_gate, w_up, grad_hidden)


def feed_own_kernel(normed, gate_w, up_w, grad_hidden, hidden, part, total):
    step = pl.program_id(0)
    rows = normed[...]
    gate_now = gate_w[...]
    up_now = up_w[...]
    hidden[...], grad_gate, grad_up = swish_grads(
        contract(rows, gate_now, 1, 0),
        contract(rows, up_now, 1, 0),
        grad_hidden[...].astype(F32),
    )
    term = contract(grad_gate, gate_now, 1, 1) + contract(grad_up, up_now, 1, 1)

    @pl.when(step == 0)
    def _():
        total[...] = term

    @pl.when(step > 0)
    def _():
        total[...] += term

    @pl.when(step == pl.num_programs(0) - 1)
    def _():
        part[...] = total[...]


def feed_own(normed, w_gate, w_up, grad_hidden):
    tokens, depth = normed.shape
    units = w_gate.shape[1]
    cols = tile(512, units)
    weight = pl.BlockSpec((depth, cols), lambda j: (0, j))
    block = pl.BlockSpec((tokens, cols), lambda j: (0, j))
    rows = pl.BlockSpec((tokens, depth), lambda j: (0, 0))
    return pl.pallas_call(
        feed_own_kernel,
        out_shape=(
            jax.ShapeDtypeStruct((tokens, units), BF),
            jax.ShapeDtypeStruct((tokens, depth), F32),
        ),
        grid=(units // cols,),
        in_specs=[rows, weight, weight, block],
        out_specs=(block, rows),
        scratch_shapes=[pltpu.VMEM((tokens, depth), F32)],
        compiler_params=kernel_params(1),
        cost_estimate=cost(8 * tokens * depth * units, 4 * depth * units, tokens * units),
        name="feed_own",
    )(normed, w_gate, w_up, grad_hidden)


def weight_grad_kernel(count, core, *refs):
    lefts, rights = refs[:count], refs[count : 2 * count]
    wide, low = refs[2 * count :]
    total = contract(lefts[0][...], rights[0][...], 0, 0)
    for left, right in zip(lefts[1:], rights[1:]):
        total = total + contract(left[...], right[...], 0, 0)
    wide[...] = total
    low[...] = total.astype(BF)


def weight_grad(core, lefts, rights, dim):
    tokens, m = lefts[0].shape
    n = rights[0].shape[1]
    count = len(lefts)
    rows, cols = tile(512, m), tile(1024, n)
    down, across = m // rows, n // cols
    if dim == 0:
        full = (2 * m, n)
        place = lambda j, i, c: (c[0] * down + i, j)
    else:
        full = (m, 2 * n)
        place = lambda j, i, c: (i, c[0] * across + j)
    return pl.pallas_call(
        functools.partial(weight_grad_kernel, count),
        out_shape=(jax.ShapeDtypeStruct(full, F32), jax.ShapeDtypeStruct((m, n), BF)),
        grid_spec=pltpu.PrefetchScalarGridSpec(
            num_scalar_prefetch=1,
            grid=(across, down),
            in_specs=[pl.BlockSpec((tokens, rows), lambda j, i, c: (0, i))] * count
            + [pl.BlockSpec((tokens, cols), lambda j, i, c: (0, j))] * count,
            out_specs=(
                pl.BlockSpec((rows, cols), place),
                pl.BlockSpec((rows, cols), lambda j, i, c: (i, j)),
            ),
        ),
        compiler_params=kernel_params(2),
        cost_estimate=cost(
            2 * tokens * count * m * n, 2 * tokens * count * (m + n) + 6 * m * n
        ),
        name="weight_grad",
    )(core, *lefts, *rights)


def fill_other_kernel(core, other, held, out):
    out[...] = other[...].astype(F32)


def fill_other(core, other, held, dim):
    m, n = other.shape
    rows = tile(256, m)
    down = m // rows
    if dim == 0:
        place = lambda i, c: ((1 - c[0]) * down + i, 0)
    else:
        place = lambda i, c: (i, 1 - c[0])
    return pl.pallas_call(
        fill_other_kernel,
        out_shape=jax.ShapeDtypeStruct(held.shape, F32),
        grid_spec=pltpu.PrefetchScalarGridSpec(
            num_scalar_prefetch=1,
            grid=(down,),
            in_specs=[
                pl.BlockSpec((rows, n), lambda i, c: (i, 0)),
                pl.BlockSpec(memory_space=pl.ANY),
            ],
            out_specs=pl.BlockSpec((rows, n), place),
        ),
        input_output_aliases={2: 0},
        compiler_params=kernel_params(1),
        cost_estimate=cost(m * n, 6 * m * n),
        name="fill_other",
    )(core, other, held)


def rope_tables(positions):
    half = HEAD_SIZE // 2
    expo = jnp.arange(half, dtype=F32) * 2.0 / HEAD_SIZE
    inverse = 1.0 / 500000.0**expo
    wavelength = 2.0 * jnp.pi / inverse
    smooth = (8192.0 / wavelength - 1.0) / 3.0
    middle = (1.0 - smooth) * inverse / 32.0 + smooth * inverse
    scaled = jnp.where(
        wavelength < 2048.0, inverse, jnp.where(wavelength > 8192.0, inverse / 32.0, middle)
    )
    angles = positions.astype(F32)[:, None] * scaled[None, :]
    return (jnp.cos(angles), jnp.sin(angles))


def apply_rotation(values, cosine_table, sine_table):
    half = values.shape[-1] // 2
    first = values[..., :half]
    second = values[..., half:]
    cosine_table = cosine_table[:, None, :]
    sine_table = sine_table[:, None, :]
    return jnp.concatenate(
        [first * cosine_table - second * sine_table, second * cosine_table + first * sine_table],
        axis=-1,
    )


def layout(row_lengths, places):
    ends = jnp.cumsum(row_lengths)
    starts = ends - row_lengths
    segment = jnp.sum((places[:, None] >= ends[None, :]).astype(jnp.int32), axis=1)
    labels = jnp.arange(row_lengths.shape[0], dtype=jnp.int32)
    begin = jnp.sum(jnp.where(segment[:, None] == labels[None, :], starts[None, :], 0), axis=1)
    begin = begin + jnp.where(segment == row_lengths.shape[0], ends[-1], 0)
    return (segment, places - begin)


def rms_back(grad_normed, gain, values, inverse):
    scaled = grad_normed * gain
    product = jnp.mean(scaled * values, axis=-1, keepdims=True)
    return inverse * scaled - values * inverse * inverse * inverse * product


def dot(a, b):
    return jnp.dot(a, b, preferred_element_type=F32)


def dot_right(a, b):
    return jnp.einsum("cf,df->cd", a, b, preferred_element_type=F32)


def dot_left(a, b):
    return jnp.einsum("cd,cf->df", a, b, preferred_element_type=F32)


def flip(value, axis, mask):
    return lax.ppermute(value, axis, [(i, i ^ mask) for i in range(lax.axis_size(axis))])


def reorder(value, axis):
    n = lax.axis_size(axis)
    me = lax.axis_index(axis)
    chunk = value.shape[0] // n
    return jnp.concatenate(
        [lax.dynamic_slice_in_dim(value, (me ^ k) * chunk, chunk, 0) for k in range(n)], axis=0
    )


def scatter_sum(part, axis):
    n = lax.axis_size(axis)
    chunk = part.shape[0] // n
    total = part[:chunk]
    low = part.astype(BF)
    for k in reversed(range(1, n)):
        total = total + flip(low[k * chunk : (k + 1) * chunk], axis, k).astype(F32)
    return total


def spread(chunk, axis):
    return jnp.concatenate(
        [chunk] + [flip(chunk, axis, k) for k in range(1, lax.axis_size(axis))], axis=0
    )


def after(value, *others):
    return lax.optimization_barrier((value,) + others)[0]


def gather_halves(value):
    half = value.shape[0] // 2
    return [
        lax.all_gather(value[:half], ("rows", "seq"), axis=0, tiled=True),
        lax.all_gather(value[half:], ("seq", "rows"), axis=0, tiled=True),
    ]


def total_over(value, axes):
    for axis in axes:
        n = lax.axis_size(axis)
        for b in range(n.bit_length() - 1):
            value = value + flip(value, axis, 1 << b)
    return value


def per_device(
    activations,
    doc_lengths,
    w_query,
    key_matrix,
    value_matrix,
    w_output,
    w_gate,
    w_up,
    w_down,
    gain_attn,
    gain_ffn,
    cotangent,
):
    span = activations.shape[1]
    blocks = lax.axis_size("seq")
    whole = span * blocks
    chunk = span // lax.axis_size("tensor")
    heads_kv = key_matrix.shape[1] // HEAD_SIZE
    query_group = w_query.shape[1] // key_matrix.shape[1]
    width = heads_kv * HEAD_SIZE
    scale = HEAD_SIZE ** (-0.5)
    row_lengths = doc_lengths[0]
    block_here = lax.axis_index("seq")
    order = reorder(jnp.arange(span, dtype=jnp.int32), "tensor")
    places = block_here * span + order
    segment, position = layout(row_lengths, places)
    key_places = jnp.concatenate([(block_here ^ j) * span + order for j in range(blocks)])
    key_segment = layout(row_lengths, key_places)[0]
    allowed = (segment[:, None] == key_segment[None, :]) & (places[:, None] >= key_places[None, :])
    cosine_table, sine_table = rope_tables(position)

    stream = reorder(activations[0], "tensor").astype(F32)
    valid = (segment < DOCS).astype(F32)
    upstream_low = (reorder(cotangent[0], "tensor").astype(F32) * valid[:, None]).astype(BF)
    stream_chunk = stream[:chunk]
    upstream_chunk = upstream_low[:chunk].astype(F32)

    inverse_one = lax.rsqrt(jnp.mean(stream * stream, axis=-1, keepdims=True) + EPSILON)
    first_normed = (stream * inverse_one * gain_attn).astype(BF)
    key_lin = dot(first_normed, key_matrix)
    value_lin = dot(first_normed, value_matrix)
    keys = apply_rotation(
        key_lin.reshape(span, heads_kv, HEAD_SIZE), cosine_table, sine_table
    ).astype(BF)
    packed = jnp.concatenate([keys.reshape(span, width), value_lin.astype(BF)], axis=1)
    gathered = spread(packed, "seq")
    upstream_all = gather_halves(upstream_low)

    query_lin = dot(first_normed, w_query)
    queries = apply_rotation(
        query_lin.reshape(span, heads_kv * query_group, HEAD_SIZE), cosine_table, sine_table
    ).astype(BF)
    query_four = queries.reshape(span, heads_kv, query_group, HEAD_SIZE)

    def score_block(key_full):
        raw = (
            jnp.einsum("chgd,whd->hgcw", query_four, key_full, preferred_element_type=F32) * scale
        )
        return jnp.where(allowed[None, None], raw, -1e30)

    key_full = gathered[:, :width].reshape(whole, heads_kv, HEAD_SIZE)
    value_full = gathered[:, width:].reshape(whole, heads_kv, HEAD_SIZE)
    masked = score_block(key_full)
    top = jnp.max(masked, axis=-1, keepdims=True)
    weights = jnp.exp(masked - top)
    total = jnp.sum(weights, axis=-1, keepdims=True)
    probs = (weights / total).astype(BF)
    mixed = jnp.einsum("hgcw,whd->chgd", probs, value_full, preferred_element_type=F32)
    attended = mixed.reshape(span, width * query_group).astype(BF)

    core = lax.axis_index("rows").astype(jnp.int32).reshape(1)
    attn_part = dot(attended, w_output)
    attn_sum = scatter_sum(attn_part, "tensor")
    grad_hidden = dot_right(after(upstream_low, attn_part), w_down).astype(BF)
    attn_sum, grad_hidden = lax.optimization_barrier((attn_sum, grad_hidden))
    middle = stream_chunk + attn_sum
    inverse_two = lax.rsqrt(jnp.mean(middle * middle, axis=-1, keepdims=True) + EPSILON)
    normed_chunk = (middle * inverse_two * gain_ffn).astype(BF)
    normed_here = spread(normed_chunk, "tensor")
    grad_hidden_all = [grad_hidden_half(core, after(u, attn_sum), w_down) for u in upstream_all]
    normed_here, *grad_hidden_all = lax.optimization_barrier((normed_here, *grad_hidden_all))
    normed_all = gather_halves(normed_here)

    hidden, part_two = feed_own(normed_here, w_gate, w_up, grad_hidden)
    grad_normed_two = scatter_sum(part_two, "tensor")
    down_part = dot(after(hidden, part_two), w_down)
    grad_normed_two, down_part = lax.optimization_barrier((grad_normed_two, down_part))
    gain_two = jnp.sum(grad_normed_two * middle * inverse_two, axis=0)
    grad_middle = upstream_chunk + rms_back(grad_normed_two, gain_ffn, middle, inverse_two)
    grad_middle_here = spread(grad_middle.astype(BF), "tensor")
    first_feed = feed_half(
        core, after(normed_all[0], grad_normed_two), w_gate, w_up, grad_hidden_all[0]
    )
    grad_middle_here, *first_feed = lax.optimization_barrier((grad_middle_here, *first_feed))
    grad_wo = lax.psum(dot_left(attended, grad_middle_here).astype(BF), ("rows", "seq"))
    block_sum = scatter_sum(after(down_part, grad_middle_here), "tensor")

    grad_attended = (
        dot_right(grad_middle_here, w_output)
        .astype(BF)
        .reshape(span, heads_kv, query_group, HEAD_SIZE)
    )
    renewed = jnp.exp(score_block(key_full) - top) / total
    renewed_low = renewed.astype(BF)
    grad_probs = jnp.einsum(
        "chgd,whd->hgcw", grad_attended, value_full, preferred_element_type=F32
    )
    inner = jnp.sum(renewed * grad_probs, axis=-1, keepdims=True)
    grad_scores = (renewed * (grad_probs - inner)).astype(BF)
    grad_query_rot = (
        jnp.einsum("hgcw,whd->chgd", grad_scores, key_full, preferred_element_type=F32) * scale
    )
    grad_key_term = (
        jnp.einsum("hgcw,chgd->whd", grad_scores, query_four, preferred_element_type=F32) * scale
    )
    grad_value_term = jnp.einsum(
        "hgcw,chgd->whd", renewed_low, grad_attended, preferred_element_type=F32
    )
    kv_term = jnp.concatenate(
        [grad_key_term.reshape(whole, width), grad_value_term.reshape(whole, width)], axis=1
    )
    kv_term, block_sum = lax.optimization_barrier((kv_term, block_sum))
    kv_grad = scatter_sum(kv_term, "seq")
    second_feed = feed_half(
        core, after(normed_all[1], kv_term), w_gate, w_up, grad_hidden_all[1]
    )
    kv_grad, *second_feed = lax.optimization_barrier((kv_grad, *second_feed))
    block_chunk = middle + block_sum
    block_output = reorder(spread(block_chunk.astype(BF), "tensor"), "tensor")
    grad_query_lin = apply_rotation(
        grad_query_rot.reshape(span, heads_kv * query_group, HEAD_SIZE), cosine_table, -sine_table
    )
    grad_query_lin = grad_query_lin.reshape(span, width * query_group).astype(BF)
    grad_key_lin = apply_rotation(
        kv_grad[:, :width].reshape(span, heads_kv, HEAD_SIZE), cosine_table, -sine_table
    )
    grad_key_lin = grad_key_lin.reshape(span, width).astype(BF)
    grad_value_lin = kv_grad[:, width:].astype(BF)

    lin = jnp.concatenate([grad_query_lin, grad_key_lin, grad_value_lin], axis=1)
    lin_part = dot_left(after(first_normed, grad_wo), lin).astype(BF)
    grad_query_lin, lin_part = lax.optimization_barrier((grad_query_lin, lin_part))
    grad_lin = lax.psum(lin_part, ("rows", "seq"))
    part_one = (
        dot_right(grad_query_lin, w_query)
        + dot_right(grad_key_lin, key_matrix)
        + dot_right(grad_value_lin, value_matrix)
    )
    grad_normed_one = scatter_sum(part_one, "tensor")
    hidden_all, grad_gate_all, grad_up_all = zip(first_feed, second_feed)
    grad_down = weight_grad(
        core, [after(h, part_one) for h in hidden_all], upstream_all, 0
    )
    down_other = flip(grad_down[1], "rows", 1)
    grad_gate_w = weight_grad(
        core, [after(n, grad_down[1]) for n in normed_all], grad_gate_all, 1
    )
    gate_other = flip(grad_gate_w[1], "rows", 1)
    grad_normed_one, wide, down_other = lax.optimization_barrier(
        (grad_normed_one, grad_gate_w[0], down_other)
    )
    grad_gate_w = (wide, grad_gate_w[1])
    inverse_chunk = inverse_one[:chunk]
    gain_one = jnp.sum(grad_normed_one * stream_chunk * inverse_chunk, axis=0)
    grad_input = grad_middle + rms_back(grad_normed_one, gain_attn, stream_chunk, inverse_chunk)
    grad_input = spread(grad_input.astype(BF), "tensor")
    grad_up_w = weight_grad(
        core, [after(n, grad_normed_one) for n in normed_all], grad_up_all, 1
    )
    up_other = flip(grad_up_w[1], "rows", 1)
    grad_down = fill_other(core, after(down_other, grad_up_w[1]), grad_down[0], 0)
    grad_gate_w = fill_other(core, after(gate_other, grad_down), grad_gate_w[0], 1)
    grad_up_w = fill_other(core, up_other, grad_up_w[0], 1)
    grad_input = reorder(grad_input, "tensor")
    grad_wq = grad_lin[:, : width * query_group].astype(F32)
    grad_wkv = grad_lin[:, width * query_group :].astype(F32)
    gains = total_over(jnp.stack([gain_one, gain_two]), ("rows", "seq", "tensor"))
    return (
        block_output[None],
        grad_input[None],
        grad_wq,
        grad_wkv[:, :width],
        grad_wkv[:, width:],
        grad_wo.astype(F32),
        grad_gate_w,
        grad_up_w,
        grad_down,
        gains[0],
        gains[1],
    )


def solution(mesh):
    placed = (
        P("rows", "seq", None),
        P("rows", None),
        P(None, "tensor"),
        P(None, "tensor"),
        P(None, "tensor"),
        P("tensor", None),
        P(None, "tensor"),
        P(None, "tensor"),
        P("tensor", None),
        P(),
        P(),
        P("rows", "seq", None),
    )
    return jax.shard_map(
        per_device,
        mesh=mesh,
        in_specs=placed,
        out_specs=(
            P("rows", "seq", None),
            P("rows", "seq", None),
            P(None, "tensor"),
            P(None, "tensor"),
            P(None, "tensor"),
            P("tensor", None),
            P(None, "tensor"),
            P(None, "tensor"),
            P("tensor", None),
            P(),
            P(),
        ),
        check_vma=False,
    )
```

```python
import functools

import jax
import jax.numpy as jnp
from jax import lax
from jax.experimental import pallas as pl
from jax.experimental.pallas import tpu as pltpu
import numpy as np
from jax.sharding import PartitionSpec as P

HEAD_SIZE = 64
DOCS = 4
EPSILON = 1e-05
BF = jnp.bfloat16
F32 = jnp.float32


MIB = 1 << 20


def kernel_params(dims, mib=63):
    return pltpu.CompilerParams(
        vmem_limit_bytes=mib * MIB, dimension_semantics=("arbitrary",) * dims
    )


def contract(a, b, dim_a, dim_b):
    return lax.dot_general(
        a, b, (((dim_a,), (dim_b,)), ((), ())), preferred_element_type=F32
    )


def tile(limit, size):
    while size > limit and size % 2 == 0:
        size //= 2
    return size


SMALL = pl.CostEstimate(flops=1, bytes_accessed=1, transcendentals=0)


def spent(us):
    return pl.CostEstimate(flops=us * 10**9, bytes_accessed=1, transcendentals=0)


def whole_spec(array):
    shape = array.shape
    return pl.BlockSpec(shape, lambda *_: (0,) * len(shape))


def join(refs):
    if refs[0].shape[0] % 16 == 0:
        return jnp.concatenate([r[...] for r in refs], axis=0)
    return jnp.concatenate([r[...].astype(F32) for r in refs], axis=0).astype(refs[0].dtype)


def unread(deps):
    return [pl.BlockSpec(memory_space=pl.ANY)] * len(deps)


def times_transposed_kernel(core, left, weight, *refs):
    refs[-1][...] = contract(left[...], weight[...], 1, 1).astype(BF)


def grad_hidden_of(core, upstream, w_down, shares, deps=()):
    tokens, depth = upstream.shape
    units = w_down.shape[0] // shares
    rows, cols = tile(640, tokens), tile(1024 // (3 - shares), units)
    steps = units // cols
    offset = steps * (shares - 1)
    return pl.pallas_call(
        times_transposed_kernel,
        out_shape=jax.ShapeDtypeStruct((tokens, units), BF),
        grid_spec=pltpu.PrefetchScalarGridSpec(
            num_scalar_prefetch=1,
            grid=(steps, tokens // rows),
            in_specs=[
                pl.BlockSpec((rows, depth), lambda j, i, c: (i, 0)),
                pl.BlockSpec((cols, depth), lambda j, i, c: (c[0] * offset + j, 0)),
            ]
            + unread(deps),
            out_specs=pl.BlockSpec((rows, cols), lambda j, i, c: (i, j)),
        ),
        compiler_params=kernel_params(2),
        cost_estimate=SMALL,
        name="grad_hidden_of",
    )(core, upstream, w_down, *deps)


def swish_grads(gate, up_proj, grad_hidden):
    sigmoid = 1.0 / (1.0 + jnp.exp(-gate))
    activated = gate * sigmoid
    hidden = (activated * up_proj).astype(BF)
    grad_gate = (grad_hidden * up_proj * (sigmoid * (1.0 + gate * (1.0 - sigmoid)))).astype(BF)
    grad_up = (grad_hidden * activated).astype(BF)
    return hidden, grad_gate, grad_up


def feed_half_kernel(core, normed, gate_w, up_w, grad_hidden, *refs):
    hidden, grad_gate, grad_up = refs[-3:]
    rows = normed[...]
    hidden[...], grad_gate[...], grad_up[...] = swish_grads(
        contract(rows, gate_w[...], 1, 0),
        contract(rows, up_w[...], 1, 0),
        grad_hidden[...].astype(F32),
    )


def feed_half(core, normed, w_gate, w_up, grad_hidden, deps=()):
    tokens, depth = normed.shape
    half = w_gate.shape[1] // 2
    rows, cols = tile(640, tokens), tile(512, half)
    steps = half // cols
    out = jax.ShapeDtypeStruct((tokens, half), BF)
    weight = pl.BlockSpec((depth, cols), lambda j, i, c: (0, c[0] * steps + j))
    block = pl.BlockSpec((rows, cols), lambda j, i, c: (i, j))
    return pl.pallas_call(
        feed_half_kernel,
        out_shape=(out, out, out),
        grid_spec=pltpu.PrefetchScalarGridSpec(
            num_scalar_prefetch=1,
            grid=(steps, tokens // rows),
            in_specs=[
                pl.BlockSpec((rows, depth), lambda j, i, c: (i, 0)),
                weight,
                weight,
                block,
            ]
            + unread(deps),
            out_specs=(block, block, block),
        ),
        compiler_params=kernel_params(2),
        cost_estimate=SMALL,
        name="feed_half",
    )(core, normed, w_gate, w_up, grad_hidden, *deps)


def feed_own_kernel(pieces, chunks, gate_w, up_w, grad_hidden, *refs):
    normed = refs[:pieces]
    hidden, parts = refs[-chunks - 3], refs[-chunks - 2 : -2]
    rows, total = refs[-2:]
    step = pl.program_id(0)
    size = total.shape[0] // chunks

    @pl.when(step == 0)
    def _():
        rows[...] = join(normed)

    gate_now = gate_w[...]
    up_now = up_w[...]
    hidden[...], grad_gate, grad_up = swish_grads(
        contract(rows[...], gate_now, 1, 0),
        contract(rows[...], up_now, 1, 0),
        grad_hidden[...].astype(F32),
    )
    term = contract(grad_gate, gate_now, 1, 1) + contract(grad_up, up_now, 1, 1)

    @pl.when(step == 0)
    def _():
        total[...] = term

    @pl.when(step > 0)
    def _():
        total[...] += term

    @pl.when(step == pl.num_programs(0) - 1)
    def _():
        for k, part in enumerate(parts):
            part[...] = total[k * size : (k + 1) * size].astype(BF)


def feed_own(normed, w_gate, w_up, grad_hidden, chunks, deps=()):
    tokens, units = grad_hidden.shape
    depth = w_gate.shape[0]
    size = tokens // chunks
    cols = tile(512, units)
    weight = pl.BlockSpec((depth, cols), lambda j: (0, j))
    block = pl.BlockSpec((tokens, cols), lambda j: (0, j))
    rows = pl.BlockSpec((size, depth), lambda j: (0, 0))
    out = pl.pallas_call(
        functools.partial(feed_own_kernel, len(normed), chunks),
        out_shape=(jax.ShapeDtypeStruct((tokens, units), BF),)
        + (jax.ShapeDtypeStruct((size, depth), BF),) * chunks,
        grid=(units // cols,),
        in_specs=[weight, weight, block] + [whole_spec(n) for n in normed] + unread(deps),
        out_specs=(block,) + (rows,) * chunks,
        scratch_shapes=[pltpu.VMEM((tokens, depth), BF), pltpu.VMEM((tokens, depth), F32)],
        compiler_params=kernel_params(1),
        cost_estimate=SMALL,
        name="feed_own",
    )(w_gate, w_up, grad_hidden, *normed, *deps)
    return out[0], list(out[1:])


def down_kernel(chunks, hidden, weight, *refs):
    parts = refs[-chunks:]
    part = contract(hidden[...], weight[...], 1, 0)
    rows = part.shape[0] // chunks
    for k, out in enumerate(parts):
        out[...] = part[k * rows : (k + 1) * rows].astype(BF)


def down_projection(hidden, w_down, chunks, deps=()):
    tokens, units = hidden.shape
    depth = w_down.shape[1]
    cols = tile(512, depth)
    return list(
        pl.pallas_call(
            functools.partial(down_kernel, chunks),
            out_shape=(jax.ShapeDtypeStruct((tokens // chunks, depth), BF),) * chunks,
            grid=(depth // cols,),
            in_specs=[whole_spec(hidden), pl.BlockSpec((units, cols), lambda j: (0, j))]
            + unread(deps),
            out_specs=(pl.BlockSpec((tokens // chunks, cols), lambda j: (0, j)),) * chunks,
            compiler_params=kernel_params(1),
            cost_estimate=SMALL,
                name="down_projection",
        )(hidden, w_down, *deps)
    )


PIECES = 4


def weight_grad_kernel(count, core, *refs):
    lefts, rights = refs[:count], refs[count : 2 * count]
    wide, lows = refs[-1 - PIECES], refs[-PIECES:]
    total = contract(lefts[0][...], rights[0][...], 0, 0)
    for left, right in zip(lefts[1:], rights[1:]):
        total = total + contract(left[...], right[...], 0, 0)
    wide[...] = total
    for k, low in enumerate(lows):

        @pl.when(pl.program_id(1) == k)
        def _():
            low[...] = total.astype(BF)


def weight_grad(core, lefts, rights, dim, deps=()):
    tokens, m = lefts[0].shape
    n = rights[0].shape[1]
    count = len(lefts)
    rows, cols = m // PIECES, tile(1024, n)
    across = n // cols
    if dim == 0:
        full = (2 * m, n)
        place = lambda j, i, c: (c[0] * PIECES + i, j)
    else:
        full = (m, 2 * n)
        place = lambda j, i, c: (i, c[0] * across + j)
    piece = pl.BlockSpec((rows, cols), lambda j, i, c: (0, j))
    out = pl.pallas_call(
        functools.partial(weight_grad_kernel, count),
        out_shape=(jax.ShapeDtypeStruct(full, F32),)
        + (jax.ShapeDtypeStruct((rows, n), BF),) * PIECES,
        grid_spec=pltpu.PrefetchScalarGridSpec(
            num_scalar_prefetch=1,
            grid=(across, PIECES),
            in_specs=[pl.BlockSpec((tokens, rows), lambda j, i, c: (0, i))] * count
            + [pl.BlockSpec((tokens, cols), lambda j, i, c: (0, j))] * count
            + unread(deps),
            out_specs=(pl.BlockSpec((rows, cols), place),) + (piece,) * PIECES,
        ),
        compiler_params=kernel_params(2),
        cost_estimate=SMALL,
        name="weight_grad",
    )(core, *lefts, *rights, *deps)
    return out[0], list(out[1:])


def left_product_kernel(count, left, *refs):
    right = join(refs[:count])
    refs[-1][...] = contract(left[...], right, 0, 0).astype(BF)


def left_product(left, pieces, deps=()):
    tokens, m = left.shape
    n = pieces[0].shape[1]
    rows, cols = tile(1024, m), tile(512, n)
    return pl.pallas_call(
        functools.partial(left_product_kernel, len(pieces)),
        out_shape=jax.ShapeDtypeStruct((m, n), BF),
        grid=(m // rows, n // cols),
        in_specs=[pl.BlockSpec((tokens, rows), lambda i, j: (0, i))]
        + [pl.BlockSpec((p.shape[0], cols), lambda i, j: (0, j)) for p in pieces]
        + unread(deps),
        out_specs=pl.BlockSpec((rows, cols), lambda i, j: (i, j)),
        compiler_params=kernel_params(2),
        cost_estimate=SMALL,
        name="left_product",
    )(left, *pieces, *deps)


def kv_product_kernel(left, right, gain_one, gain_two, *refs):
    out = refs[-1]
    width = right.shape[1]
    rows = left.shape[1]
    out[:, :width] = contract(left[...], right[...], 0, 0).astype(BF)
    gains = jnp.concatenate([gain_one[...], gain_two[...], jnp.zeros((126, rows), F32)], axis=0)
    out[:, width:] = jnp.transpose(gains).astype(BF)


def kv_product(left, right, gain_one, gain_two, deps=()):
    tokens, m = left.shape
    width = right.shape[1]
    rows = tile(1024, m)
    gain = pl.BlockSpec((1, rows), lambda i: (0, i))
    return pl.pallas_call(
        kv_product_kernel,
        out_shape=jax.ShapeDtypeStruct((m, width + 128), BF),
        grid=(m // rows,),
        in_specs=[pl.BlockSpec((tokens, rows), lambda i: (0, i)), whole_spec(right), gain, gain]
        + unread(deps),
        out_specs=pl.BlockSpec((rows, width + 128), lambda i: (i, 0)),
        compiler_params=kernel_params(1),
        cost_estimate=SMALL,
        name="kv_product",
    )(left, right, gain_one, gain_two, *deps)


def mask_kernel(chunks, scalars, place, *refs):
    value = join(refs[:chunks]).astype(F32)
    masked = jnp.where(place[...] < scalars[1], value, 0.0).astype(BF)
    half = masked.shape[0] // 2
    refs[-3][...] = masked
    refs[-2][...] = masked[:half]
    refs[-1][...] = masked[half:]


def mask_padding(scalars, value, place, chunks, deps=()):
    span, depth = value.shape
    half = jax.ShapeDtypeStruct((span // 2, depth), BF)
    outs = (jax.ShapeDtypeStruct(value.shape, BF), half, half)
    return pl.pallas_call(
        functools.partial(mask_kernel, chunks),
        out_shape=outs,
        grid_spec=pltpu.PrefetchScalarGridSpec(
            num_scalar_prefetch=1,
            grid=(1,),
            in_specs=[whole_spec(place)]
            + [chunk_spec(value, chunks, k) for k in range(chunks)]
            + unread(deps),
            out_specs=tuple(whole_spec(a) for a in outs),
        ),
        compiler_params=kernel_params(1),
        cost_estimate=SMALL,
        name="mask_padding",
    )(scalars, place, *[value] * chunks, *deps)


def gain_rows_kernel(value, out):
    out[...] = jnp.transpose(value[...].astype(F32))[:8]


def gain_rows(value):
    rows, width = value.shape
    return pl.pallas_call(
        gain_rows_kernel,
        out_shape=jax.ShapeDtypeStruct((8, rows), F32),
        grid=(1,),
        in_specs=[pl.BlockSpec((rows, 128), lambda i: (0, width // 128 - 1))],
        out_specs=pl.BlockSpec((8, rows), lambda i: (0, 0)),
        compiler_params=kernel_params(1),
        cost_estimate=SMALL,
        name="gain_rows",
    )(value)


def fill_other_kernel(core, *refs):
    step = pl.program_id(0)
    for k in range(PIECES):

        @pl.when(step == k)
        def _():
            refs[-1][...] = refs[k][...].astype(F32)


def fill_other(core, others, held, dim, deps=()):
    rows, n = others[0].shape
    if dim == 0:
        place = lambda i, c: ((1 - c[0]) * PIECES + i, 0)
    else:
        place = lambda i, c: (i, 1 - c[0])
    return pl.pallas_call(
        fill_other_kernel,
        out_shape=jax.ShapeDtypeStruct(held.shape, F32),
        grid_spec=pltpu.PrefetchScalarGridSpec(
            num_scalar_prefetch=1,
            grid=(PIECES,),
            in_specs=[whole_spec(o) for o in others]
            + [pl.BlockSpec(memory_space=pl.ANY)]
            + unread(deps),
            out_specs=pl.BlockSpec((rows, n), place),
        ),
        input_output_aliases={1 + PIECES: 0},
        compiler_params=kernel_params(1),
        cost_estimate=spent(50),
        name="fill_other",
    )(core, *others, held, *deps)


def rotate_block(values, cosine, sine):
    width = values.shape[1]
    column = lax.broadcasted_iota(jnp.int32, values.shape, 1)
    other = jnp.where(
        column % HEAD_SIZE < HEAD_SIZE // 2,
        pltpu.roll(values, width - HEAD_SIZE // 2, 1),
        pltpu.roll(values, HEAD_SIZE // 2, 1),
    )
    return values * cosine + other * sine


def pack_rotated(keys, values, cosine, sine):
    width = keys.shape[1]
    if width % 128 == 0:
        turned = [
            rotate_block(keys[:, i : i + 128], cosine, sine) for i in range(0, width, 128)
        ]
        return jnp.concatenate(turned + [values], axis=1)
    both = jnp.concatenate([keys, values], axis=1)
    column = lax.broadcasted_iota(jnp.int32, both.shape, 1)
    return jnp.where(column < width, rotate_block(both, cosine, sine), both)


def chunk_spec(array, chunks, k):
    block = (array.shape[0] // chunks, array.shape[1])
    return pl.BlockSpec(block, lambda *a: (a[-1][0] ^ k, 0))


def project_kv_kernel(chunks, waits, me, *refs):
    gain, key_w, value_w, cosine, sine = refs[chunks : chunks + 5]
    normed, inverse, packed = refs[-3:]
    stream = join(refs[:chunks]).astype(F32)
    scale = lax.rsqrt(jnp.mean(stream * stream, axis=1, keepdims=True) + EPSILON)
    low = (stream * scale * gain[...]).astype(BF)
    normed[...] = low
    inverse[...] = jnp.broadcast_to(scale, inverse.shape)
    packed[...] = pack_rotated(
        contract(low, key_w[...], 1, 0), contract(low, value_w[...], 1, 0), cosine[...], sine[...]
    ).astype(BF)


def project_kv(me, x, gain, key_matrix, value_matrix, cosine, sine, chunks, deps=()):
    span, depth = x.shape
    args = (gain, key_matrix, value_matrix, cosine, sine)
    outs = (
        jax.ShapeDtypeStruct((span, depth), BF),
        jax.ShapeDtypeStruct((span, 128), F32),
        jax.ShapeDtypeStruct((span, 2 * key_matrix.shape[1]), BF),
    )
    return pl.pallas_call(
        functools.partial(project_kv_kernel, chunks, len(deps)),
        out_shape=outs,
        grid_spec=pltpu.PrefetchScalarGridSpec(
            num_scalar_prefetch=1,
            grid=(1,),
            in_specs=[chunk_spec(x, chunks, k) for k in range(chunks)]
            + [whole_spec(a) for a in args]
            + unread(deps),
            out_specs=tuple(whole_spec(a) for a in outs),
        ),
        compiler_params=kernel_params(1),
        cost_estimate=SMALL,
        name="project_kv",
    )(me, *[x] * chunks, *args, *deps)


def project_query_kernel(normed, weight, cosine, sine, *refs):
    out = refs[-1]
    lin = contract(normed[...], weight[...], 1, 0)
    for i in range(0, lin.shape[1], 128):
        turned = rotate_block(lin[:, i : i + 128], cosine[...], sine[...])
        out[:, i : i + 128] = (turned * HEAD_SIZE**-0.5).astype(BF)


def project_query(normed, w_query, cosine, sine, deps=()):
    span, depth = normed.shape
    width = w_query.shape[1]
    cols = 256
    return pl.pallas_call(
        project_query_kernel,
        out_shape=jax.ShapeDtypeStruct((span, width), BF),
        grid=(width // cols,),
        in_specs=[
            whole_spec(normed),
            pl.BlockSpec((depth, cols), lambda j: (0, j)),
            whole_spec(cosine),
            whole_spec(sine),
        ]
        + unread(deps),
        out_specs=pl.BlockSpec((span, cols), lambda j: (0, j)),
        compiler_params=kernel_params(1),
        cost_estimate=SMALL,
        name="project_query",
    )(normed, w_query, cosine, sine, *deps)


def head_columns(array, index):
    return array[:, index * HEAD_SIZE : (index + 1) * HEAD_SIZE]


def stack_heads(array, heads):
    return jnp.concatenate([head_columns(array, h) for h in heads], axis=0)


def store_heads(out, turned, first, span, finish):
    for i in range(0, turned.shape[1] // span, 2):
        pair = jnp.concatenate(
            [turned[:, (i + e) * span : (i + e + 1) * span] for e in range(2)], axis=0
        )
        at = (first + i) * HEAD_SIZE
        out[:, at : at + 128] = finish(jnp.transpose(pair)).astype(BF)


def attend_kernel(blocks, chunks, shift, query, place, place_row, begin_row, w_output, *refs):
    packed = refs[:blocks]
    attended, stats, *parts = refs[-2 - chunks :]
    span, width = query.shape
    heads_kv = packed[0].shape[1] // (2 * HEAD_SIZE)
    group = width // HEAD_SIZE // heads_kv
    last = jnp.concatenate([place_row[...]] * group, axis=1)
    first = jnp.concatenate([begin_row[...]] * group, axis=1)
    for g in range(heads_kv):
        q = stack_heads(query, range(g * group, (g + 1) * group))
        top = total = mixed = None
        for j in range(blocks):
            keys = head_columns(packed[j], g)
            values = head_columns(packed[j], heads_kv + g)
            key_place = place[...] + shift[j]
            allowed = (key_place >= first) & (key_place <= last)
            masked = jnp.where(allowed, contract(keys, q, 1, 1), -1e30)
            peak = jnp.max(masked, axis=0, keepdims=True)
            peak = peak if j == 0 else jnp.maximum(top, peak)
            terms = jnp.exp(masked - peak)
            amount = jnp.sum(terms, axis=0, keepdims=True)
            term = contract(values, terms.astype(BF), 0, 0)
            if j == 0:
                total, mixed = amount, term
            else:
                fade = jnp.exp(top - peak)
                total, mixed = total * fade + amount, mixed * fade + term
            top = peak
        stats[g : g + 1, :] = top + jnp.log(total)
        store_heads(attended, mixed * (1.0 / total), g * group, span, lambda v: v)
    part = contract(attended[...], w_output[...], 1, 0)
    chunk = span // len(parts)
    for k, out in enumerate(parts):
        out[...] = part[k * chunk : (k + 1) * chunk].astype(BF)


def attend(shift, query, packed, places, w_output, chunks, deps=()):
    span, width = query.shape
    depth = w_output.shape[1]
    blocks = len(packed)
    heads_kv = packed[0].shape[1] // (2 * HEAD_SIZE)
    args = (
        query,
        *places,
        w_output,
        *packed,
    )
    outs = (
        jax.ShapeDtypeStruct((span, width), BF),
        jax.ShapeDtypeStruct((heads_kv, width // HEAD_SIZE // heads_kv * span), F32),
    )
    outs += (jax.ShapeDtypeStruct((span // chunks, depth), BF),) * chunks
    out = pl.pallas_call(
        functools.partial(attend_kernel, blocks, chunks),
        out_shape=outs,
        grid_spec=pltpu.PrefetchScalarGridSpec(
            num_scalar_prefetch=1,
            grid=(1,),
            in_specs=[whole_spec(a) for a in args] + unread(deps),
            out_specs=tuple(whole_spec(a) for a in outs),
        ),
        compiler_params=kernel_params(1),
        cost_estimate=spent(87),
        name="attend",
    )(shift, *args, *deps)
    return out[0], out[1], list(out[2:])


def sum_chunks(refs):
    total = refs[0][...].astype(F32)
    for ref in refs[1:]:
        total = total + ref[...].astype(F32)
    return total


def middle_kernel(count, me, x, gain, *refs):
    chunks, (middle, inverse, normed) = refs[:count], refs[-3:]
    stream = x[...].astype(F32) + sum_chunks(chunks)
    scale = lax.rsqrt(jnp.mean(stream * stream, axis=1, keepdims=True) + EPSILON)
    middle[...] = stream
    inverse[...] = jnp.broadcast_to(scale, inverse.shape)
    normed[...] = (stream * scale * gain[...]).astype(BF)


def middle_norm(me, x, gain, chunks, deps=()):
    rows, depth = chunks[0].shape
    outs = (
        jax.ShapeDtypeStruct((rows, depth), F32),
        jax.ShapeDtypeStruct((rows, 128), F32),
        jax.ShapeDtypeStruct((rows, depth), BF),
    )
    return pl.pallas_call(
        functools.partial(middle_kernel, len(chunks)),
        out_shape=outs,
        grid_spec=pltpu.PrefetchScalarGridSpec(
            num_scalar_prefetch=1,
            grid=(1,),
            in_specs=[chunk_spec(x, len(chunks), 0)]
            + [whole_spec(a) for a in (gain, *chunks)]
            + unread(deps),
            out_specs=tuple(whole_spec(a) for a in outs),
        ),
        compiler_params=kernel_params(1),
        cost_estimate=SMALL,
        name="middle_norm",
    )(me, x, gain, *chunks, *deps)


def halves_kernel(count, *refs):
    half = count // 2
    refs[-2][...] = join(refs[:half])
    refs[-1][...] = join(refs[half:count])


def join_halves(chunks, deps=()):
    rows, depth = chunks[0].shape
    outs = (jax.ShapeDtypeStruct((rows * len(chunks) // 2, depth), BF),) * 2
    return pl.pallas_call(
        functools.partial(halves_kernel, len(chunks)),
        out_shape=outs,
        grid=(1,),
        in_specs=[whole_spec(a) for a in chunks] + unread(deps),
        out_specs=tuple(whole_spec(a) for a in outs),
        compiler_params=kernel_params(1),
        cost_estimate=SMALL,
        name="join_halves",
    )(*chunks, *deps)


def norm_gradient(grad, rows, scale, gain):
    scaled = grad * gain
    product = jnp.mean(scaled * rows, axis=1, keepdims=True)
    gain_grad = jnp.sum(grad * rows * scale, axis=0, keepdims=True)
    return scale * scaled - rows * (scale * scale * scale * product), gain_grad


def norm_back_kernel(count, upstream, middle, inverse, gain, *refs):
    chunks, (wide, low, gain_grad) = refs[:count], refs[-3:]
    grad, gain_grad[...] = norm_gradient(
        sum_chunks(chunks), middle[...], inverse[:, :1], gain[...]
    )
    total = upstream[...].astype(F32) + grad
    wide[...] = total
    low[...] = total.astype(BF)


def norm_back(upstream, middle, inverse, gain, chunks, deps=()):
    rows, depth = middle.shape
    args = (middle, inverse, gain, *chunks)
    outs = (
        jax.ShapeDtypeStruct((rows, depth), F32),
        jax.ShapeDtypeStruct((rows, depth), BF),
        jax.ShapeDtypeStruct((1, depth), F32),
    )
    return pl.pallas_call(
        functools.partial(norm_back_kernel, len(chunks)),
        out_shape=outs,
        grid=(1,),
        in_specs=[pl.BlockSpec((rows, depth), lambda i: (0, 0))]
        + [whole_spec(a) for a in args]
        + unread(deps),
        out_specs=tuple(whole_spec(a) for a in outs),
        compiler_params=kernel_params(1),
        cost_estimate=SMALL,
        name="norm_back",
    )(upstream, *args, *deps)


def finish_kernel(count, me, x, inverse, gain, grad_middle, *refs):
    grad, _ = norm_gradient(
        sum_chunks(refs[:count]), x[...].astype(F32), inverse[:, :1], gain[...]
    )
    refs[-1][...] = (grad_middle[...] + grad).astype(BF)


def finish(me, x, inverse, gain, grad_middle, chunks, deps=()):
    rows, depth = grad_middle.shape
    args = (gain, grad_middle, *chunks)
    outs = jax.ShapeDtypeStruct((rows, depth), BF)
    return pl.pallas_call(
        functools.partial(finish_kernel, len(chunks)),
        out_shape=outs,
        grid_spec=pltpu.PrefetchScalarGridSpec(
            num_scalar_prefetch=1,
            grid=(1,),
            in_specs=[
                chunk_spec(x, len(chunks), 0),
                pl.BlockSpec((rows, 128), lambda i, c: (0, 0)),
            ]
            + [whole_spec(a) for a in args]
            + unread(deps),
            out_specs=whole_spec(outs),
        ),
        compiler_params=kernel_params(1),
        cost_estimate=SMALL,
        name="finish",
    )(me, x, inverse, *args, *deps)


def add_kernel(count, *refs):
    refs[-1][...] = sum_chunks(refs[:count]).astype(refs[-1].dtype)


def add_up(arrays, dtype, deps=()):
    out = jax.ShapeDtypeStruct(arrays[0].shape, dtype)
    return pl.pallas_call(
        functools.partial(add_kernel, len(arrays)),
        out_shape=out,
        grid=(1,),
        in_specs=[whole_spec(a) for a in arrays] + unread(deps),
        out_specs=whole_spec(out),
        compiler_params=kernel_params(1),
        cost_estimate=SMALL,
        name="add_up",
    )(*arrays, *deps)


def restore_kernel(count, me, *refs):
    step = pl.program_id(0)
    for k in range(count):

        @pl.when(step == k)
        def _():
            refs[-1][...] = refs[k][...]


def restore(me, pieces, cost, deps=()):
    count = len(pieces)
    rows, depth = pieces[0].shape
    if rows % 16:
        return reorder(jnp.concatenate(pieces, axis=0), "tensor")
    return pl.pallas_call(
        functools.partial(restore_kernel, count),
        out_shape=jax.ShapeDtypeStruct((count * rows, depth), BF),
        grid_spec=pltpu.PrefetchScalarGridSpec(
            num_scalar_prefetch=1,
            grid=(count,),
            in_specs=[whole_spec(p) for p in pieces] + unread(deps),
            out_specs=pl.BlockSpec((rows, depth), lambda i, c: (c[0] ^ i, 0)),
        ),
        compiler_params=kernel_params(1),
        cost_estimate=cost,
        name="restore",
    )(me, *pieces, *deps)


def attend_back_kernel(blocks, count, shift, query, attended, stats, place, place_row, begin_row,
                       cosine, sine, w_output, *refs):
    packed = refs[:blocks]
    chunks = refs[blocks : blocks + count]
    grad_query = refs[-1 - blocks]
    terms = refs[-blocks:]
    span, width = query.shape
    heads_kv = packed[0].shape[1] // (2 * HEAD_SIZE)
    group = width // HEAD_SIZE // heads_kv
    grad_middle = join(chunks)
    grad_attended = contract(grad_middle, w_output[...], 1, 1).astype(BF)
    last = jnp.concatenate([place_row[...]] * group, axis=1)
    first = jnp.concatenate([begin_row[...]] * group, axis=1)
    key_terms = [[] for _ in range(blocks)]
    value_terms = [[] for _ in range(blocks)]
    for g in range(heads_kv):
        mine = range(g * group, (g + 1) * group)
        q = stack_heads(query, mine)
        grad = stack_heads(grad_attended, mine)
        norm = stats[g : g + 1, :]
        inner = lax.dot_general(
            jnp.ones((8, HEAD_SIZE), F32),
            grad.astype(F32) * stack_heads(attended, mine).astype(F32),
            (((1,), (1,)), ((), ())),
            preferred_element_type=F32,
            precision=lax.Precision.HIGHEST,
        )[:1]
        total = None
        for j in range(blocks):
            keys = head_columns(packed[j], g)
            values = head_columns(packed[j], heads_kv + g)
            key_place = place[...] + shift[j]
            allowed = (key_place >= first) & (key_place <= last)
            scores = contract(keys, q, 1, 1)
            probs = jnp.exp(jnp.where(allowed, scores - norm, -1e30))
            grad_scores = (probs * (contract(values, grad, 1, 1) - inner)).astype(BF)
            value_terms[j].append(contract(probs.astype(BF), grad, 1, 0))
            key_terms[j].append(contract(grad_scores, q, 1, 0))
            term = contract(keys, grad_scores, 0, 0)
            total = term if total is None else total + term
        store_heads(
            grad_query,
            total,
            g * group,
            span,
            lambda v: rotate_block(v * HEAD_SIZE**-0.5, cosine[...], -sine[...]),
        )
    for j in range(blocks):
        terms[j][...] = jnp.concatenate(key_terms[j] + value_terms[j], axis=1).astype(BF)


def attend_back(shift, query, attended, stats, packed, places, cosine, sine, w_output, chunks,
                deps=()):
    span, width = query.shape
    blocks = len(packed)
    args = (
        query,
        attended,
        stats,
        *places,
        cosine,
        sine,
        w_output,
        *packed,
        *chunks,
    )
    outs = (jax.ShapeDtypeStruct((span, width), BF),)
    outs += (jax.ShapeDtypeStruct(packed[0].shape, BF),) * blocks
    out = pl.pallas_call(
        functools.partial(attend_back_kernel, blocks, len(chunks)),
        out_shape=outs,
        grid_spec=pltpu.PrefetchScalarGridSpec(
            num_scalar_prefetch=1,
            grid=(1,),
            in_specs=[whole_spec(a) for a in args] + unread(deps),
            out_specs=tuple(whole_spec(a) for a in outs),
        ),
        compiler_params=kernel_params(1),
        cost_estimate=SMALL,
        name="attend_back",
    )(shift, *args, *deps)
    return out[0], list(out[1:])


def input_back_kernel(
    count, chunks, me, grad_query, w_query, key_w, value_w, cosine, sine, inverse, *refs
):
    terms, rows = refs[:count], refs[count : count + chunks]
    lin, gain_grad, *parts = refs[-2 - chunks :]
    normed = join(rows).astype(F32) * inverse[:, :1]
    width = key_w.shape[1]
    total = sum_chunks(terms)
    low = pack_rotated(total[:, :width], total[:, width:], cosine[...], -sine[...]).astype(BF)
    lin[...] = low
    part = contract(grad_query[...], w_query[...], 1, 1)
    part = part + contract(low[:, :width], key_w[...], 1, 1)
    part = part + contract(low[:, width:], value_w[...], 1, 1)
    rows = part.shape[0] // chunks
    for k, out in enumerate(parts):
        out[...] = part[k * rows : (k + 1) * rows].astype(BF)
    gain_grad[...] = jnp.sum(part * normed, axis=0, keepdims=True)


def input_back(
    me, grad_query, w_query, key_matrix, value_matrix, cosine, sine, inverse, x, terms, chunks, deps=()
):
    span = grad_query.shape[0]
    depth = w_query.shape[0]
    args = (grad_query, w_query, key_matrix, value_matrix, cosine, sine, inverse, *terms)
    outs = (
        jax.ShapeDtypeStruct(terms[0].shape, BF),
        jax.ShapeDtypeStruct((1, depth), F32),
    )
    outs += (jax.ShapeDtypeStruct((span // chunks, depth), BF),) * chunks
    out = pl.pallas_call(
        functools.partial(input_back_kernel, len(terms), chunks),
        out_shape=outs,
        grid_spec=pltpu.PrefetchScalarGridSpec(
            num_scalar_prefetch=1,
            grid=(1,),
            in_specs=[whole_spec(a) for a in args]
            + [chunk_spec(x, chunks, k) for k in range(chunks)]
            + unread(deps),
            out_specs=tuple(whole_spec(a) for a in outs),
        ),
        compiler_params=kernel_params(1),
        cost_estimate=SMALL,
        name="input_back",
    )(me, *args, *[x] * chunks, *deps)
    return out[0], out[1], list(out[2:])


def rope_tables(positions):
    expo = np.arange(HEAD_SIZE // 2, dtype=np.float64) * 2.0 / HEAD_SIZE
    inverse = 1.0 / 500000.0**expo
    wavelength = 2.0 * np.pi / inverse
    smooth = (8192.0 / wavelength - 1.0) / 3.0
    middle = (1.0 - smooth) * inverse / 32.0 + smooth * inverse
    scaled = np.where(
        wavelength < 2048.0, inverse, np.where(wavelength > 8192.0, inverse / 32.0, middle)
    )
    scaled = jnp.asarray(np.tile(scaled, 4)[None, :].astype(np.float32))
    sign = jnp.asarray(np.tile(np.repeat([-1.0, 1.0], HEAD_SIZE // 2), 2)[None, :].astype(np.float32))
    angles = positions.astype(F32)[:, None] * scaled
    return jnp.cos(angles), jnp.sin(angles) * sign


def flip(value, axis, mask):
    return lax.ppermute(value, axis, [(i, i ^ mask) for i in range(lax.axis_size(axis))])


def reorder(value, axis):
    n = lax.axis_size(axis)
    me = lax.axis_index(axis)
    chunk = value.shape[0] // n
    return jnp.concatenate(
        [lax.dynamic_slice_in_dim(value, (me ^ k) * chunk, chunk, 0) for k in range(n)], axis=0
    )


def exchange(chunks, axis):
    return chunks[:1] + [flip(chunks[k], axis, k) for k in reversed(range(1, len(chunks)))]


def spread(chunk, axis):
    return [chunk] + [flip(chunk, axis, k) for k in range(1, lax.axis_size(axis))]


def gather_halves(first, second):
    return [
        lax.all_gather(first, ("rows", "seq"), axis=0, tiled=True),
        lax.all_gather(second, ("seq", "rows"), axis=0, tiled=True),
    ]


def per_device(
    activations,
    doc_lengths,
    w_query,
    key_matrix,
    value_matrix,
    w_output,
    w_gate,
    w_up,
    w_down,
    gain_attn,
    gain_ffn,
    cotangent,
):
    span = activations.shape[1]
    blocks = lax.axis_size("seq")
    chunks = lax.axis_size("tensor")
    chunk = span // chunks
    core = lax.axis_index("rows").astype(jnp.int32).reshape(1)
    block_here = lax.axis_index("seq")
    gain_attn = gain_attn.reshape(1, -1)
    gain_ffn = gain_ffn.reshape(1, -1)
    stream, cotangent = activations[0], cotangent[0]
    me = lax.axis_index("tensor").astype(jnp.int32)
    token = jnp.arange(span, dtype=jnp.int32)
    place = block_here * span + (me ^ (token // chunk)) * chunk + token % chunk
    if chunk % 16:
        stream, cotangent = reorder(stream, "tensor"), reorder(cotangent, "tensor")
        me = jnp.zeros_like(me)
    ends = [doc_lengths[0, 0]]
    for d in range(1, DOCS):
        ends.append(ends[-1] + doc_lengths[0, d])
    begin = jnp.zeros_like(place)
    for end in ends:
        begin = jnp.where(place >= end, end, begin)
    cosine, sine = rope_tables(place - begin)
    shift = jnp.stack([((block_here ^ j) - block_here) * span for j in range(blocks)])
    shift = shift.astype(jnp.int32)
    scalars = jnp.stack([me, ends[-1].astype(jnp.int32)])
    places = (place.reshape(span, 1), place.reshape(1, span), begin.reshape(1, span))

    normed_one, inverse_one, packed = project_kv(
        scalars, stream, gain_attn, key_matrix, value_matrix, cosine, sine, chunks, (shift, *places)
    )
    packed = spread(packed, "seq")
    query = project_query(normed_one, w_query, cosine, sine)
    attended, stats, parts = attend(shift, query, packed, places, w_output, chunks)

    upstream, *upstream_halves = mask_padding(scalars, cotangent, places[0], chunks, (parts[0],))
    upstream_all = gather_halves(*upstream_halves)
    sent = exchange(parts, "tensor")
    grad_hidden = grad_hidden_of(core, upstream, w_down, 1, (parts[0],))
    middle, inverse_two, normed = middle_norm(scalars, stream, gain_ffn, sent, (grad_hidden,))

    grad_hidden_first = grad_hidden_of(core, upstream_all[0], w_down, 2, (middle,))
    normed = join_halves(spread(normed, "tensor"), (grad_hidden_first,))
    normed_all = gather_halves(*normed)
    hidden, parts = feed_own(normed, w_gate, w_up, grad_hidden, chunks)

    sent = exchange(parts, "tensor")
    grad_hidden_second = grad_hidden_of(core, upstream_all[1], w_down, 2, (parts[0],))
    grad_middle, grad_middle_low, gain_two = norm_back(
        upstream, middle, inverse_two, gain_ffn, sent, (grad_hidden_second,)
    )
    grad_middle_all = spread(grad_middle_low, "tensor")
    feed_first = feed_half(
        core, normed_all[0], w_gate, w_up, grad_hidden_first, (grad_middle,)
    )
    down_parts = down_projection(hidden, w_down, chunks, (feed_first[0],))
    grad_query, kv_terms = attend_back(
        shift,
        query,
        attended,
        stats,
        packed,
        places,
        cosine,
        sine,
        w_output,
        grad_middle_all,
        (down_parts[0],),
    )
    block_sent = exchange(down_parts, "tensor")

    kv_sent = exchange(kv_terms, "seq")
    wo_part = left_product(attended, grad_middle_all, (grad_query,))
    wq_part = left_product(normed_one, [grad_query], (wo_part,))
    grad_kv, gain_one, parts = input_back(
        scalars,
        grad_query,
        w_query,
        key_matrix,
        value_matrix,
        cosine,
        sine,
        inverse_one,
        stream,
        kv_sent,
        chunks,
        (wq_part, normed_all[1]),
    )

    sent = exchange(parts, "tensor")
    wkv_part = kv_product(normed_one, grad_kv, gain_one, gain_two, (parts[0],))
    grad_wo, grad_wq, grad_wkv = lax.psum((wo_part, wq_part, wkv_part), ("rows", "seq"))
    feed_second = feed_half(
        core, normed_all[1], w_gate, w_up, grad_hidden_second, (wkv_part,)
    )
    block_chunk = add_up([middle, *block_sent], BF, (feed_second[0],))
    block_all = spread(block_chunk, "tensor")
    hidden_all, grad_gate_all, grad_up_all = zip(feed_first, feed_second)
    grad_down, low = weight_grad(core, hidden_all, upstream_all, 0, (block_chunk,))
    down_other = [flip(v, "rows", 1) for v in low]
    grad_input = finish(
        scalars, stream, inverse_one, gain_attn, grad_middle, sent, (grad_down,)
    )
    grad_input_all = spread(grad_input, "tensor")
    grad_gate_w, low = weight_grad(core, normed_all, grad_gate_all, 1, (grad_input,))
    gate_other = [flip(v, "rows", 1) for v in low]
    block_output = restore(scalars, block_all, SMALL, (grad_gate_w,))
    grad_up_w, low = weight_grad(core, normed_all, grad_up_all, 1, (block_output,))
    up_other = [flip(v, "rows", 1) for v in low]
    grad_input = restore(scalars, grad_input_all, spent(25), (grad_up_w,))
    width_kv = key_matrix.shape[1]
    gains_sent = spread(gain_rows(grad_wkv), "tensor")
    grad_down = fill_other(core, down_other, grad_down, 0, (grad_input,))
    grad_gate_w = fill_other(core, gate_other, grad_gate_w, 1, (grad_down,))
    gains = add_up(gains_sent, F32, (grad_gate_w,))
    grad_up_w = fill_other(core, up_other, grad_up_w, 1, (gains,))
    return (
        block_output[None],
        grad_input[None],
        grad_wq.astype(F32),
        grad_wkv[:, :width_kv].astype(F32),
        grad_wkv[:, width_kv : 2 * width_kv].astype(F32),
        grad_wo.astype(F32),
        grad_gate_w,
        grad_up_w,
        grad_down,
        gains[0],
        gains[1],
    )


def solution(mesh):
    placed = (
        P("rows", "seq", None),
        P("rows", None),
        P(None, "tensor"),
        P(None, "tensor"),
        P(None, "tensor"),
        P("tensor", None),
        P(None, "tensor"),
        P(None, "tensor"),
        P("tensor", None),
        P(),
        P(),
        P("rows", "seq", None),
    )
    return jax.shard_map(
        per_device,
        mesh=mesh,
        in_specs=placed,
        out_specs=(
            P("rows", "seq", None),
            P("rows", "seq", None),
            P(None, "tensor"),
            P(None, "tensor"),
            P(None, "tensor"),
            P("tensor", None),
            P(None, "tensor"),
            P(None, "tensor"),
            P("tensor", None),
            P(),
            P(),
        ),
        check_vma=False,
    )
```

```python
import functools

import jax
import jax.numpy as jnp
from jax import lax
from jax.experimental import pallas as pl
from jax.experimental.pallas import tpu as pltpu
import numpy as np
from jax.sharding import PartitionSpec as P

HEAD_SIZE = 64
DOCS = 4
EPSILON = 1e-05
BF = jnp.bfloat16
F32 = jnp.float32


MIB = 1 << 20


def kernel_params(dims, mib=63):
    return pltpu.CompilerParams(
        vmem_limit_bytes=mib * MIB, dimension_semantics=("arbitrary",) * dims
    )


def contract(a, b, dim_a, dim_b):
    return lax.dot_general(
        a, b, (((dim_a,), (dim_b,)), ((), ())), preferred_element_type=F32
    )


def tile(limit, size):
    while size > limit and size % 2 == 0:
        size //= 2
    return size


SMALL = pl.CostEstimate(flops=1, bytes_accessed=1, transcendentals=0)


def spent(us):
    return pl.CostEstimate(flops=us * 10**9, bytes_accessed=1, transcendentals=0)


def whole_spec(array):
    shape = array.shape
    return pl.BlockSpec(shape, lambda *_: (0,) * len(shape))


def join(refs):
    if refs[0].shape[0] % 16 == 0:
        return jnp.concatenate([r[...] for r in refs], axis=0)
    return jnp.concatenate([r[...].astype(F32) for r in refs], axis=0).astype(refs[0].dtype)


def unread(deps):
    return [pl.BlockSpec(memory_space=pl.ANY)] * len(deps)


def times_transposed_kernel(core, left, weight, *refs):
    refs[-1][...] = contract(left[...], weight[...], 1, 1).astype(BF)


def grad_hidden_of(core, upstream, w_down, shares, deps=()):
    tokens, depth = upstream.shape
    units = w_down.shape[0] // shares
    rows, cols = tile(640, tokens), tile(1024 // (3 - shares), units)
    steps = units // cols
    offset = steps * (shares - 1)
    return pl.pallas_call(
        times_transposed_kernel,
        out_shape=jax.ShapeDtypeStruct((tokens, units), BF),
        grid_spec=pltpu.PrefetchScalarGridSpec(
            num_scalar_prefetch=1,
            grid=(steps, tokens // rows),
            in_specs=[
                pl.BlockSpec((rows, depth), lambda j, i, c: (i, 0)),
                pl.BlockSpec((cols, depth), lambda j, i, c: (c[0] * offset + j, 0)),
            ]
            + unread(deps),
            out_specs=pl.BlockSpec((rows, cols), lambda j, i, c: (i, j)),
        ),
        compiler_params=kernel_params(2),
        cost_estimate=spent(10),
        name="grad_hidden_of",
    )(core, upstream, w_down, *deps)


def swish_grads(gate, up_proj, grad_hidden):
    sigmoid = 1.0 / (1.0 + jnp.exp(-gate))
    activated = gate * sigmoid
    hidden = (activated * up_proj).astype(BF)
    grad_gate = (grad_hidden * up_proj * (sigmoid * (1.0 + gate * (1.0 - sigmoid)))).astype(BF)
    grad_up = (grad_hidden * activated).astype(BF)
    return hidden, grad_gate, grad_up


def feed_half_kernel(core, normed, gate_w, up_w, grad_hidden, *refs):
    hidden, grad_gate, grad_up = refs[-3:]
    rows = normed[...]
    hidden[...], grad_gate[...], grad_up[...] = swish_grads(
        contract(rows, gate_w[...], 1, 0),
        contract(rows, up_w[...], 1, 0),
        grad_hidden[...].astype(F32),
    )


def feed_half(core, normed, w_gate, w_up, grad_hidden, deps=()):
    tokens, depth = normed.shape
    half = w_gate.shape[1] // 2
    rows, cols = tile(640, tokens), tile(512, half)
    steps = half // cols
    out = jax.ShapeDtypeStruct((tokens, half), BF)
    weight = pl.BlockSpec((depth, cols), lambda j, i, c: (0, c[0] * steps + j))
    block = pl.BlockSpec((rows, cols), lambda j, i, c: (i, j))
    return pl.pallas_call(
        feed_half_kernel,
        out_shape=(out, out, out),
        grid_spec=pltpu.PrefetchScalarGridSpec(
            num_scalar_prefetch=1,
            grid=(steps, tokens // rows),
            in_specs=[
                pl.BlockSpec((rows, depth), lambda j, i, c: (i, 0)),
                weight,
                weight,
                block,
            ]
            + unread(deps),
            out_specs=(block, block, block),
        ),
        compiler_params=kernel_params(2),
        cost_estimate=spent(18),
        name="feed_half",
    )(core, normed, w_gate, w_up, grad_hidden, *deps)


def feed_own_kernel(pieces, chunks, gate_w, up_w, grad_hidden, *refs):
    normed = refs[:pieces]
    hidden, parts = refs[-chunks - 3], refs[-chunks - 2 : -2]
    rows, total = refs[-2:]
    step = pl.program_id(0)
    size = total.shape[0] // chunks

    @pl.when(step == 0)
    def _():
        rows[...] = join(normed)

    gate_now = gate_w[...]
    up_now = up_w[...]
    hidden[...], grad_gate, grad_up = swish_grads(
        contract(rows[...], gate_now, 1, 0),
        contract(rows[...], up_now, 1, 0),
        grad_hidden[...].astype(F32),
    )
    term = contract(grad_gate, gate_now, 1, 1) + contract(grad_up, up_now, 1, 1)

    @pl.when(step == 0)
    def _():
        total[...] = term

    @pl.when(step > 0)
    def _():
        total[...] += term

    @pl.when(step == pl.num_programs(0) - 1)
    def _():
        for k, part in enumerate(parts):
            part[...] = total[k * size : (k + 1) * size].astype(BF)


def feed_own(normed, w_gate, w_up, grad_hidden, chunks, deps=()):
    tokens, units = grad_hidden.shape
    depth = w_gate.shape[0]
    size = tokens // chunks
    cols = tile(512, units)
    weight = pl.BlockSpec((depth, cols), lambda j: (0, j))
    block = pl.BlockSpec((tokens, cols), lambda j: (0, j))
    rows = pl.BlockSpec((size, depth), lambda j: (0, 0))
    out = pl.pallas_call(
        functools.partial(feed_own_kernel, len(normed), chunks),
        out_shape=(jax.ShapeDtypeStruct((tokens, units), BF),)
        + (jax.ShapeDtypeStruct((size, depth), BF),) * chunks,
        grid=(units // cols,),
        in_specs=[weight, weight, block] + [whole_spec(n) for n in normed] + unread(deps),
        out_specs=(block,) + (rows,) * chunks,
        scratch_shapes=[pltpu.VMEM((tokens, depth), BF), pltpu.VMEM((tokens, depth), F32)],
        compiler_params=kernel_params(1),
        cost_estimate=spent(18),
        name="feed_own",
    )(w_gate, w_up, grad_hidden, *normed, *deps)
    return out[0], list(out[1:])


def down_kernel(hidden, weight, *refs):
    keep, send = refs[-2:]
    part = contract(hidden[...], weight[...], 1, 0).astype(BF)
    rows = keep.shape[0]
    keep[...] = part[:rows]
    send[...] = part[rows:]


def down_projection(hidden, w_down, deps=()):
    tokens, units = hidden.shape
    depth = w_down.shape[1]
    cols = tile(512, depth)
    half = jax.ShapeDtypeStruct((tokens // 2, depth), BF)
    block = pl.BlockSpec((tokens // 2, cols), lambda j: (0, j))
    return pl.pallas_call(
        down_kernel,
        out_shape=(half, half),
        grid=(depth // cols,),
        in_specs=[whole_spec(hidden), pl.BlockSpec((units, cols), lambda j: (0, j))]
        + unread(deps),
        out_specs=(block, block),
        compiler_params=kernel_params(1),
        cost_estimate=spent(7),
        name="down_projection",
    )(hidden, w_down, *deps)


def add_half_kernel(keep, came, *refs):
    total = keep[...].astype(F32) + came[...].astype(F32)
    first, second = refs[-2:]
    rows = first.shape[0]
    first[...] = total[:rows].astype(BF)
    second[...] = total[rows:].astype(BF)


def add_half(keep, came, deps=()):
    rows, depth = keep.shape
    half = jax.ShapeDtypeStruct((rows // 2, depth), BF)
    return pl.pallas_call(
        add_half_kernel,
        out_shape=(half, half),
        grid=(1,),
        in_specs=[whole_spec(keep), whole_spec(came)] + unread(deps),
        out_specs=(whole_spec(half), whole_spec(half)),
        compiler_params=kernel_params(1),
        cost_estimate=spent(2),
        name="add_half",
    )(keep, came, *deps)


STEPS = 4


def weight_grad_kernel(count, pieces, core, *refs):
    lefts, rights = refs[:count], refs[count : 2 * count]
    wide, lows = refs[-1 - pieces], refs[-pieces:]
    total = contract(lefts[0][...], rights[0][...], 0, 0)
    for left, right in zip(lefts[1:], rights[1:]):
        total = total + contract(left[...], right[...], 0, 0)
    wide[...] = total
    for k, low in enumerate(lows):

        @pl.when(pl.program_id(1) // (STEPS // pieces) == k)
        def _():
            low[...] = total.astype(BF)


def weight_grad(core, lefts, rights, dim, pieces, deps=()):
    tokens, m = lefts[0].shape
    n = rights[0].shape[1]
    count = len(lefts)
    rows, cols = m // STEPS, tile(1024, n)
    across = n // cols
    if dim == 0:
        full = (2 * m, n)
        place = lambda j, i, c: (c[0] * STEPS + i, j)
    else:
        full = (m, 2 * n)
        place = lambda j, i, c: (i, c[0] * across + j)
    share = STEPS // pieces

    def piece(k):
        last = share - 1
        return pl.BlockSpec(
            (rows, cols), lambda j, i, c: (jnp.clip(i - k * share, 0, last), j)
        )

    out = pl.pallas_call(
        functools.partial(weight_grad_kernel, count, pieces),
        out_shape=(jax.ShapeDtypeStruct(full, F32),)
        + (jax.ShapeDtypeStruct((rows * share, n), BF),) * pieces,
        grid_spec=pltpu.PrefetchScalarGridSpec(
            num_scalar_prefetch=1,
            grid=(across, STEPS),
            in_specs=[pl.BlockSpec((tokens, rows), lambda j, i, c: (0, i))] * count
            + [pl.BlockSpec((tokens, cols), lambda j, i, c: (0, j))] * count
            + unread(deps),
            out_specs=(pl.BlockSpec((rows, cols), place),)
            + tuple(piece(k) for k in range(pieces)),
        ),
        compiler_params=kernel_params(2),
        cost_estimate=spent(19),
        name="weight_grad",
    )(core, *lefts, *rights, *deps)
    return out[0], list(out[1:])


def pair_grad_kernel(count, core, *refs):
    lefts = [r[...] for r in refs[:count]]
    wides, low = refs[-3:-1], refs[-1]
    for k in range(2):
        rights = refs[count * (k + 1) : count * (k + 2)]
        total = contract(lefts[0], rights[0][...], 0, 0)
        for left, right in zip(lefts[1:], rights[1:]):
            total = total + contract(left, right[...], 0, 0)
        wides[k][...] = total
        low[k] = total.astype(BF)


def pair_grad(core, lefts, first, second, deps=()):
    tokens, m = lefts[0].shape
    n = first[0].shape[1]
    count = len(lefts)
    rows = m // STEPS
    wide = jax.ShapeDtypeStruct((m, 2 * n), F32)
    low = jax.ShapeDtypeStruct((2, m, n), BF)
    place = pl.BlockSpec((rows, n), lambda i, c: (i, c[0]))
    here = pl.BlockSpec((2, rows, n), lambda i, c: (0, i, 0))
    out = pl.pallas_call(
        functools.partial(pair_grad_kernel, count),
        out_shape=(wide, wide, low),
        grid_spec=pltpu.PrefetchScalarGridSpec(
            num_scalar_prefetch=1,
            grid=(STEPS,),
            in_specs=[pl.BlockSpec((tokens, rows), lambda i, c: (0, i))] * count
            + [whole_spec(v) for v in (*first, *second)]
            + unread(deps),
            out_specs=(place, place, here),
        ),
        compiler_params=kernel_params(1),
        cost_estimate=spent(34),
        name="pair_grad",
    )(core, *lefts, *first, *second, *deps)
    return out


def left_product_kernel(count, left, *refs):
    right = join(refs[:count])
    refs[-1][...] = contract(left[...], right, 0, 0).astype(BF)


def left_product(left, pieces, deps=()):
    tokens, m = left.shape
    n = pieces[0].shape[1]
    rows, cols = tile(1024, m), tile(512, n)
    return pl.pallas_call(
        functools.partial(left_product_kernel, len(pieces)),
        out_shape=jax.ShapeDtypeStruct((m, n), BF),
        grid=(m // rows, n // cols),
        in_specs=[pl.BlockSpec((tokens, rows), lambda i, j: (0, i))]
        + [pl.BlockSpec((p.shape[0], cols), lambda i, j: (0, j)) for p in pieces]
        + unread(deps),
        out_specs=pl.BlockSpec((rows, cols), lambda i, j: (i, j)),
        compiler_params=kernel_params(2),
        cost_estimate=spent(4),
        name="left_product",
    )(left, *pieces, *deps)


def kv_product_kernel(left, right, gain_one, gain_two, *refs):
    out = refs[-1]
    width = right.shape[1]
    out[:width, :] = contract(right[...], left[...], 0, 0).astype(BF)
    empty = jnp.zeros((14, left.shape[1]), F32)
    gains = jnp.concatenate([gain_one[...], gain_two[...], empty], axis=0)
    out[width:, :] = gains.astype(BF)


def kv_product(left, right, gain_one, gain_two, deps=()):
    tokens, m = left.shape
    width = right.shape[1]
    cols = tile(1024, m)
    gain = pl.BlockSpec((1, cols), lambda i: (0, i))
    return pl.pallas_call(
        kv_product_kernel,
        out_shape=jax.ShapeDtypeStruct((width + 16, m), BF),
        grid=(m // cols,),
        in_specs=[pl.BlockSpec((tokens, cols), lambda i: (0, i)), whole_spec(right), gain, gain]
        + unread(deps),
        out_specs=pl.BlockSpec((width + 16, cols), lambda i: (0, i)),
        compiler_params=kernel_params(1),
        cost_estimate=spent(3),
        name="kv_product",
    )(left, right, gain_one, gain_two, *deps)


def mask_kernel(chunks, scalars, place, *refs):
    value = join(refs[:chunks]).astype(F32)
    masked = jnp.where(place[...] < scalars[1], value, 0.0).astype(BF)
    half = masked.shape[0] // 2
    refs[-3][...] = masked
    refs[-2][...] = masked[:half]
    refs[-1][...] = masked[half:]


def mask_padding(scalars, value, place, chunks, deps=()):
    span, depth = value.shape
    half = jax.ShapeDtypeStruct((span // 2, depth), BF)
    outs = (jax.ShapeDtypeStruct(value.shape, BF), half, half)
    return pl.pallas_call(
        functools.partial(mask_kernel, chunks),
        out_shape=outs,
        grid_spec=pltpu.PrefetchScalarGridSpec(
            num_scalar_prefetch=1,
            grid=(1,),
            in_specs=[whole_spec(place)]
            + [chunk_spec(value, chunks, k) for k in range(chunks)]
            + unread(deps),
            out_specs=tuple(whole_spec(a) for a in outs),
        ),
        compiler_params=kernel_params(1),
        cost_estimate=spent(40),
        name="mask_padding",
    )(scalars, place, *[value] * chunks, *deps)


def corner_kernel(value, out):
    out[...] = value[...]


def corner(value):
    return pl.pallas_call(
        corner_kernel,
        out_shape=jax.ShapeDtypeStruct((16, 128), value.dtype),
        grid=(1,),
        in_specs=[pl.BlockSpec((16, 128), lambda i: (0, 0))],
        out_specs=pl.BlockSpec((16, 128), lambda i: (0, 0)),
        compiler_params=kernel_params(1),
        cost_estimate=spent(5),
        name="corner",
    )(value)


def gain_rows_kernel(value, *refs):
    refs[-1][...] = value[...].astype(F32)


def gain_rows(value, deps=()):
    rows, width = value.shape
    return pl.pallas_call(
        gain_rows_kernel,
        out_shape=jax.ShapeDtypeStruct((16, width), F32),
        grid=(1,),
        in_specs=[pl.BlockSpec((16, width), lambda i: (rows // 16 - 1, 0))] + unread(deps),
        out_specs=pl.BlockSpec((16, width), lambda i: (0, 0)),
        compiler_params=kernel_params(1),
        cost_estimate=spent(2),
        name="gain_rows",
    )(value, *deps)


def fill_other_kernel(pieces, core, *refs):
    step = pl.program_id(0)
    for k in range(pieces):

        @pl.when(step // (STEPS // pieces) == k)
        def _():
            refs[-1][...] = refs[k][...].astype(F32).reshape(refs[-1].shape)


def fill_other(core, others, index, held, dim, deps=()):
    pieces = len(others)
    share = STEPS // pieces
    rows, n = others[0].shape[1] // share, others[0].shape[2]
    if dim == 0:
        place = lambda i, c: ((1 - c[0]) * STEPS + i, 0)
    else:
        place = lambda i, c: (i, 1 - c[0])

    def piece(k):
        last = share - 1
        return pl.BlockSpec(
            (1, rows, n), lambda i, c: (index, jnp.clip(i - k * share, 0, last), 0)
        )

    return pl.pallas_call(
        functools.partial(fill_other_kernel, pieces),
        out_shape=jax.ShapeDtypeStruct(held.shape, F32),
        grid_spec=pltpu.PrefetchScalarGridSpec(
            num_scalar_prefetch=1,
            grid=(STEPS,),
            in_specs=[piece(k) for k in range(pieces)]
            + [pl.BlockSpec(memory_space=pl.ANY)]
            + unread(deps),
            out_specs=pl.BlockSpec((rows, n), place),
        ),
        input_output_aliases={1 + pieces: 0},
        compiler_params=kernel_params(1),
        cost_estimate=spent(6),
        name="fill_other",
    )(core, *others, held, *deps)


def rotate_block(values, cosine, sine):
    width = values.shape[1]
    column = lax.broadcasted_iota(jnp.int32, values.shape, 1)
    other = jnp.where(
        column % HEAD_SIZE < HEAD_SIZE // 2,
        pltpu.roll(values, width - HEAD_SIZE // 2, 1),
        pltpu.roll(values, HEAD_SIZE // 2, 1),
    )
    return values * cosine + other * sine


def pack_rotated(keys, values, cosine, sine):
    width = keys.shape[1]
    if width % 128 == 0:
        turned = [
            rotate_block(keys[:, i : i + 128], cosine, sine) for i in range(0, width, 128)
        ]
        return jnp.concatenate(turned + [values], axis=1)
    both = jnp.concatenate([keys, values], axis=1)
    column = lax.broadcasted_iota(jnp.int32, both.shape, 1)
    return jnp.where(column < width, rotate_block(both, cosine, sine), both)


def chunk_spec(array, chunks, k):
    block = (array.shape[0] // chunks, array.shape[1])
    return pl.BlockSpec(block, lambda *a: (a[-1][0] ^ k, 0))


def project_kv_kernel(chunks, waits, me, *refs):
    gain, key_w, value_w, cosine, sine = refs[chunks : chunks + 5]
    normed, inverse, packed = refs[-3:]
    stream = join(refs[:chunks]).astype(F32)
    scale = lax.rsqrt(jnp.mean(stream * stream, axis=1, keepdims=True) + EPSILON)
    low = (stream * scale * gain[...]).astype(BF)
    normed[...] = low
    inverse[...] = jnp.broadcast_to(scale, inverse.shape)
    packed[...] = pack_rotated(
        contract(low, key_w[...], 1, 0), contract(low, value_w[...], 1, 0), cosine[...], sine[...]
    ).astype(BF)


def project_kv(me, x, gain, key_matrix, value_matrix, cosine, sine, chunks, deps=()):
    span, depth = x.shape
    args = (gain, key_matrix, value_matrix, cosine, sine)
    outs = (
        jax.ShapeDtypeStruct((span, depth), BF),
        jax.ShapeDtypeStruct((span, 128), F32),
        jax.ShapeDtypeStruct((span, 2 * key_matrix.shape[1]), BF),
    )
    return pl.pallas_call(
        functools.partial(project_kv_kernel, chunks, len(deps)),
        out_shape=outs,
        grid_spec=pltpu.PrefetchScalarGridSpec(
            num_scalar_prefetch=1,
            grid=(1,),
            in_specs=[chunk_spec(x, chunks, k) for k in range(chunks)]
            + [whole_spec(a) for a in args]
            + unread(deps),
            out_specs=tuple(whole_spec(a) for a in outs),
        ),
        compiler_params=kernel_params(1),
        cost_estimate=spent(4),
        name="project_kv",
    )(me, *[x] * chunks, *args, *deps)


def project_query_kernel(normed, weight, cosine, sine, *refs):
    out = refs[-1]
    lin = contract(normed[...], weight[...], 1, 0)
    for i in range(0, lin.shape[1], 128):
        turned = rotate_block(lin[:, i : i + 128], cosine[...], sine[...])
        out[:, i : i + 128] = (turned * HEAD_SIZE**-0.5).astype(BF)


def project_query(normed, w_query, cosine, sine, deps=()):
    span, depth = normed.shape
    width = w_query.shape[1]
    cols = 256
    return pl.pallas_call(
        project_query_kernel,
        out_shape=jax.ShapeDtypeStruct((span, width), BF),
        grid=(width // cols,),
        in_specs=[
            whole_spec(normed),
            pl.BlockSpec((depth, cols), lambda j: (0, j)),
            whole_spec(cosine),
            whole_spec(sine),
        ]
        + unread(deps),
        out_specs=pl.BlockSpec((span, cols), lambda j: (0, j)),
        compiler_params=kernel_params(1),
        cost_estimate=spent(4),
        name="project_query",
    )(normed, w_query, cosine, sine, *deps)


def head_columns(array, index):
    return array[:, index * HEAD_SIZE : (index + 1) * HEAD_SIZE]


def stack_heads(array, heads):
    return jnp.concatenate([head_columns(array, h) for h in heads], axis=0)


def store_heads(out, turned, first, span, finish):
    for i in range(0, turned.shape[1] // span, 2):
        pair = jnp.concatenate(
            [turned[:, (i + e) * span : (i + e + 1) * span] for e in range(2)], axis=0
        )
        at = (first + i) * HEAD_SIZE
        out[:, at : at + 128] = finish(jnp.transpose(pair)).astype(BF)


def attend_kernel(blocks, chunks, shift, query, place, place_row, begin_row, w_output, *refs):
    packed = refs[:blocks]
    attended, stats, *parts = refs[-2 - chunks :]
    span, width = query.shape
    heads_kv = packed[0].shape[1] // (2 * HEAD_SIZE)
    group = width // HEAD_SIZE // heads_kv
    last = jnp.concatenate([place_row[...]] * group, axis=1)
    first = jnp.concatenate([begin_row[...]] * group, axis=1)
    for g in range(heads_kv):
        q = stack_heads(query, range(g * group, (g + 1) * group))
        top = total = mixed = None
        for j in range(blocks):
            keys = head_columns(packed[j], g)
            values = head_columns(packed[j], heads_kv + g)
            key_place = place[...] + shift[j]
            allowed = (key_place >= first) & (key_place <= last)
            masked = jnp.where(allowed, contract(keys, q, 1, 1), -1e30)
            peak = jnp.max(masked, axis=0, keepdims=True)
            peak = peak if j == 0 else jnp.maximum(top, peak)
            terms = jnp.exp(masked - peak)
            amount = jnp.sum(terms, axis=0, keepdims=True)
            term = contract(values, terms.astype(BF), 0, 0)
            if j == 0:
                total, mixed = amount, term
            else:
                fade = jnp.exp(top - peak)
                total, mixed = total * fade + amount, mixed * fade + term
            top = peak
        stats[g : g + 1, :] = top + jnp.log(total)
        store_heads(attended, mixed * (1.0 / total), g * group, span, lambda v: v)
    part = contract(attended[...], w_output[...], 1, 0)
    chunk = span // len(parts)
    for k, out in enumerate(parts):
        out[...] = part[k * chunk : (k + 1) * chunk].astype(BF)


def attend(shift, query, packed, places, w_output, chunks, deps=()):
    span, width = query.shape
    depth = w_output.shape[1]
    blocks = len(packed)
    heads_kv = packed[0].shape[1] // (2 * HEAD_SIZE)
    args = (
        query,
        *places,
        w_output,
        *packed,
    )
    outs = (
        jax.ShapeDtypeStruct((span, width), BF),
        jax.ShapeDtypeStruct((heads_kv, width // HEAD_SIZE // heads_kv * span), F32),
    )
    outs += (jax.ShapeDtypeStruct((span // chunks, depth), BF),) * chunks
    out = pl.pallas_call(
        functools.partial(attend_kernel, blocks, chunks),
        out_shape=outs,
        grid_spec=pltpu.PrefetchScalarGridSpec(
            num_scalar_prefetch=1,
            grid=(1,),
            in_specs=[whole_spec(a) for a in args] + unread(deps),
            out_specs=tuple(whole_spec(a) for a in outs),
        ),
        compiler_params=kernel_params(1),
        cost_estimate=spent(11),
        name="attend",
    )(shift, *args, *deps)
    return out[0], out[1], list(out[2:])


def sum_chunks(refs):
    total = refs[0][...].astype(F32)
    for ref in refs[1:]:
        total = total + ref[...].astype(F32)
    return total


def middle_kernel(count, me, x, gain, *refs):
    chunks, (middle, inverse, normed) = refs[:count], refs[-3:]
    stream = x[...].astype(F32) + sum_chunks(chunks)
    scale = lax.rsqrt(jnp.mean(stream * stream, axis=1, keepdims=True) + EPSILON)
    middle[...] = stream
    inverse[...] = jnp.broadcast_to(scale, inverse.shape)
    normed[...] = (stream * scale * gain[...]).astype(BF)


def middle_norm(me, x, gain, chunks, deps=()):
    rows, depth = chunks[0].shape
    outs = (
        jax.ShapeDtypeStruct((rows, depth), F32),
        jax.ShapeDtypeStruct((rows, 128), F32),
        jax.ShapeDtypeStruct((rows, depth), BF),
    )
    return pl.pallas_call(
        functools.partial(middle_kernel, len(chunks)),
        out_shape=outs,
        grid_spec=pltpu.PrefetchScalarGridSpec(
            num_scalar_prefetch=1,
            grid=(1,),
            in_specs=[chunk_spec(x, len(chunks), 0)]
            + [whole_spec(a) for a in (gain, *chunks)]
            + unread(deps),
            out_specs=tuple(whole_spec(a) for a in outs),
        ),
        compiler_params=kernel_params(1),
        cost_estimate=spent(3),
        name="middle_norm",
    )(me, x, gain, *chunks, *deps)


def halves_kernel(count, *refs):
    half = count // 2
    refs[-2][...] = join(refs[:half])
    refs[-1][...] = join(refs[half:count])


def join_halves(chunks, deps=()):
    rows, depth = chunks[0].shape
    outs = (jax.ShapeDtypeStruct((rows * len(chunks) // 2, depth), BF),) * 2
    return pl.pallas_call(
        functools.partial(halves_kernel, len(chunks)),
        out_shape=outs,
        grid=(1,),
        in_specs=[whole_spec(a) for a in chunks] + unread(deps),
        out_specs=tuple(whole_spec(a) for a in outs),
        compiler_params=kernel_params(1),
        cost_estimate=spent(2),
        name="join_halves",
    )(*chunks, *deps)


def norm_gradient(grad, rows, scale, gain):
    scaled = grad * gain
    product = jnp.mean(scaled * rows, axis=1, keepdims=True)
    gain_grad = jnp.sum(grad * rows * scale, axis=0, keepdims=True)
    return scale * scaled - rows * (scale * scale * scale * product), gain_grad


def norm_back_kernel(count, upstream, middle, inverse, gain, *refs):
    chunks, (wide, low, gain_grad) = refs[:count], refs[-3:]
    grad, gain_grad[...] = norm_gradient(
        sum_chunks(chunks), middle[...], inverse[:, :1], gain[...]
    )
    total = upstream[...].astype(F32) + grad
    wide[...] = total
    low[...] = total.astype(BF)


def norm_back(upstream, middle, inverse, gain, chunks, deps=()):
    rows, depth = middle.shape
    args = (middle, inverse, gain, *chunks)
    outs = (
        jax.ShapeDtypeStruct((rows, depth), F32),
        jax.ShapeDtypeStruct((rows, depth), BF),
        jax.ShapeDtypeStruct((1, depth), F32),
    )
    return pl.pallas_call(
        functools.partial(norm_back_kernel, len(chunks)),
        out_shape=outs,
        grid=(1,),
        in_specs=[pl.BlockSpec((rows, depth), lambda i: (0, 0))]
        + [whole_spec(a) for a in args]
        + unread(deps),
        out_specs=tuple(whole_spec(a) for a in outs),
        compiler_params=kernel_params(1),
        cost_estimate=spent(3),
        name="norm_back",
    )(upstream, *args, *deps)


def finish_kernel(count, me, x, inverse, gain, grad_middle, block, *refs):
    grad, _ = norm_gradient(
        sum_chunks(refs[:count]), x[...].astype(F32), inverse[:, :1], gain[...]
    )
    refs[-1][...] = jnp.concatenate([grad_middle[...] + grad, block[...]], axis=0).astype(BF)


def finish(me, x, inverse, gain, grad_middle, block, chunks, deps=()):
    rows, depth = grad_middle.shape
    args = (gain, grad_middle, block, *chunks)
    outs = jax.ShapeDtypeStruct((2 * rows, depth), BF)
    return pl.pallas_call(
        functools.partial(finish_kernel, len(chunks)),
        out_shape=outs,
        grid_spec=pltpu.PrefetchScalarGridSpec(
            num_scalar_prefetch=1,
            grid=(1,),
            in_specs=[
                chunk_spec(x, len(chunks), 0),
                pl.BlockSpec((rows, 128), lambda i, c: (0, 0)),
            ]
            + [whole_spec(a) for a in args]
            + unread(deps),
            out_specs=whole_spec(outs),
        ),
        compiler_params=kernel_params(1),
        cost_estimate=spent(3),
        name="finish",
    )(me, x, inverse, *args, *deps)


def add_kernel(count, *refs):
    refs[-1][...] = sum_chunks(refs[:count]).astype(refs[-1].dtype)


def add_up(arrays, dtype, deps=()):
    out = jax.ShapeDtypeStruct(arrays[0].shape, dtype)
    return pl.pallas_call(
        functools.partial(add_kernel, len(arrays)),
        out_shape=out,
        grid=(1,),
        in_specs=[whole_spec(a) for a in arrays] + unread(deps),
        out_specs=whole_spec(out),
        compiler_params=kernel_params(1),
        cost_estimate=spent(2),
        name="add_up",
    )(*arrays, *deps)


def restore_kernel(count, me, *refs):
    step = pl.program_id(0)
    for k in range(count):

        @pl.when(step == k)
        def _():
            rows = refs[k].shape[0] // 2
            refs[-2][...] = refs[k][:rows]
            refs[-1][...] = refs[k][rows:]


def restore(me, pieces, deps=()):
    count = len(pieces)
    rows, depth = pieces[0].shape[0] // 2, pieces[0].shape[1]
    if rows % 16:
        halves = [[p[:rows] for p in pieces], [p[rows:] for p in pieces]]
        return [reorder(jnp.concatenate(h, axis=0), "tensor") for h in halves]
    out = jax.ShapeDtypeStruct((count * rows, depth), BF)
    place = pl.BlockSpec((rows, depth), lambda i, c: (c[0] ^ i, 0))
    return pl.pallas_call(
        functools.partial(restore_kernel, count),
        out_shape=(out, out),
        grid_spec=pltpu.PrefetchScalarGridSpec(
            num_scalar_prefetch=1,
            grid=(count,),
            in_specs=[whole_spec(p) for p in pieces] + unread(deps),
            out_specs=(place, place),
        ),
        compiler_params=kernel_params(1),
        cost_estimate=spent(87),
        name="restore",
    )(me, *pieces, *deps)


def widen(wo, wq, wkv, width, deps=()):
    steps = 4
    depth = wq.shape[0]
    shapes = [wo.shape, wq.shape, (depth, width), (depth, width)]

    def spec(shape):
        return pl.BlockSpec((shape[0] // steps, shape[1]), lambda i: (i, 0))

    def kernel(wo, wq, wkv, *refs):
        wo_out, wq_out, wk_out, wv_out = refs[-4:]
        wo_out[...] = wo[...].astype(F32)
        wq_out[...] = wq[...].astype(F32)
        turned = jnp.transpose(wkv[: 2 * width, :].astype(F32))
        wk_out[...] = turned[:, :width]
        wv_out[...] = turned[:, width:]

    return pl.pallas_call(
        kernel,
        out_shape=tuple(jax.ShapeDtypeStruct(v, F32) for v in shapes),
        grid=(steps,),
        in_specs=[
            spec(wo.shape),
            spec(wq.shape),
            pl.BlockSpec((wkv.shape[0], depth // steps), lambda i: (0, i)),
        ]
        + unread(deps),
        out_specs=tuple(spec(v) for v in shapes),
        compiler_params=kernel_params(1),
        cost_estimate=spent(8),
        name="widen",
    )(wo, wq, wkv, *deps)


def attend_back_kernel(blocks, count, shift, query, attended, stats, place, place_row, begin_row,
                       cosine, sine, w_output, *refs):
    packed = refs[:blocks]
    chunks = refs[blocks : blocks + count]
    grad_query = refs[-1 - blocks]
    terms = refs[-blocks:]
    span, width = query.shape
    heads_kv = packed[0].shape[1] // (2 * HEAD_SIZE)
    group = width // HEAD_SIZE // heads_kv
    grad_middle = join(chunks)
    grad_attended = contract(grad_middle, w_output[...], 1, 1).astype(BF)
    last = jnp.concatenate([place_row[...]] * group, axis=1)
    first = jnp.concatenate([begin_row[...]] * group, axis=1)
    key_terms = [[] for _ in range(blocks)]
    value_terms = [[] for _ in range(blocks)]
    for g in range(heads_kv):
        mine = range(g * group, (g + 1) * group)
        q = stack_heads(query, mine)
        grad = stack_heads(grad_attended, mine)
        norm = stats[g : g + 1, :]
        inner = lax.dot_general(
            jnp.ones((8, HEAD_SIZE), F32),
            grad.astype(F32) * stack_heads(attended, mine).astype(F32),
            (((1,), (1,)), ((), ())),
            preferred_element_type=F32,
            precision=lax.Precision.HIGHEST,
        )[:1]
        total = None
        for j in range(blocks):
            keys = head_columns(packed[j], g)
            values = head_columns(packed[j], heads_kv + g)
            key_place = place[...] + shift[j]
            allowed = (key_place >= first) & (key_place <= last)
            scores = contract(keys, q, 1, 1)
            probs = jnp.exp(jnp.where(allowed, scores - norm, -1e30))
            grad_scores = (probs * (contract(values, grad, 1, 1) - inner)).astype(BF)
            value_terms[j].append(contract(probs.astype(BF), grad, 1, 0))
            key_terms[j].append(contract(grad_scores, q, 1, 0))
            term = contract(keys, grad_scores, 0, 0)
            total = term if total is None else total + term
        store_heads(
            grad_query,
            total,
            g * group,
            span,
            lambda v: rotate_block(v * HEAD_SIZE**-0.5, cosine[...], -sine[...]),
        )
    for j in range(blocks):
        terms[j][...] = jnp.concatenate(key_terms[j] + value_terms[j], axis=1).astype(BF)


def attend_back(shift, query, attended, stats, packed, places, cosine, sine, w_output, chunks,
                deps=()):
    span, width = query.shape
    blocks = len(packed)
    args = (
        query,
        attended,
        stats,
        *places,
        cosine,
        sine,
        w_output,
        *packed,
        *chunks,
    )
    outs = (jax.ShapeDtypeStruct((span, width), BF),)
    outs += (jax.ShapeDtypeStruct(packed[0].shape, BF),) * blocks
    out = pl.pallas_call(
        functools.partial(attend_back_kernel, blocks, len(chunks)),
        out_shape=outs,
        grid_spec=pltpu.PrefetchScalarGridSpec(
            num_scalar_prefetch=1,
            grid=(1,),
            in_specs=[whole_spec(a) for a in args] + unread(deps),
            out_specs=tuple(whole_spec(a) for a in outs),
        ),
        compiler_params=kernel_params(1),
        cost_estimate=spent(16),
        name="attend_back",
    )(shift, *args, *deps)
    return out[0], list(out[1:])


def input_back_kernel(
    count, chunks, me, grad_query, w_query, key_w, value_w, cosine, sine, inverse, *refs
):
    terms, rows = refs[:count], refs[count : count + chunks]
    lin, gain_grad, *parts = refs[-2 - chunks :]
    normed = join(rows).astype(F32) * inverse[:, :1]
    width = key_w.shape[1]
    total = sum_chunks(terms)
    low = pack_rotated(total[:, :width], total[:, width:], cosine[...], -sine[...]).astype(BF)
    lin[...] = low
    part = contract(grad_query[...], w_query[...], 1, 1)
    part = part + contract(low[:, :width], key_w[...], 1, 1)
    part = part + contract(low[:, width:], value_w[...], 1, 1)
    rows = part.shape[0] // chunks
    for k, out in enumerate(parts):
        out[...] = part[k * rows : (k + 1) * rows].astype(BF)
    gain_grad[...] = jnp.sum(part * normed, axis=0, keepdims=True)


def input_back(
    me, grad_query, w_query, key_matrix, value_matrix, cosine, sine, inverse, x, terms, chunks, deps=()
):
    span = grad_query.shape[0]
    depth = w_query.shape[0]
    args = (grad_query, w_query, key_matrix, value_matrix, cosine, sine, inverse, *terms)
    outs = (
        jax.ShapeDtypeStruct(terms[0].shape, BF),
        jax.ShapeDtypeStruct((1, depth), F32),
    )
    outs += (jax.ShapeDtypeStruct((span // chunks, depth), BF),) * chunks
    out = pl.pallas_call(
        functools.partial(input_back_kernel, len(terms), chunks),
        out_shape=outs,
        grid_spec=pltpu.PrefetchScalarGridSpec(
            num_scalar_prefetch=1,
            grid=(1,),
            in_specs=[whole_spec(a) for a in args]
            + [chunk_spec(x, chunks, k) for k in range(chunks)]
            + unread(deps),
            out_specs=tuple(whole_spec(a) for a in outs),
        ),
        compiler_params=kernel_params(1),
        cost_estimate=spent(6),
        name="input_back",
    )(me, *args, *[x] * chunks, *deps)
    return out[0], out[1], list(out[2:])


def rope_tables(positions):
    expo = np.arange(HEAD_SIZE // 2, dtype=np.float64) * 2.0 / HEAD_SIZE
    inverse = 1.0 / 500000.0**expo
    wavelength = 2.0 * np.pi / inverse
    smooth = (8192.0 / wavelength - 1.0) / 3.0
    middle = (1.0 - smooth) * inverse / 32.0 + smooth * inverse
    scaled = np.where(
        wavelength < 2048.0, inverse, np.where(wavelength > 8192.0, inverse / 32.0, middle)
    )
    scaled = jnp.asarray(np.tile(scaled, 4)[None, :].astype(np.float32))
    sign = jnp.asarray(np.tile(np.repeat([-1.0, 1.0], HEAD_SIZE // 2), 2)[None, :].astype(np.float32))
    angles = positions.astype(F32)[:, None] * scaled
    return jnp.cos(angles), jnp.sin(angles) * sign


def flip(value, axis, mask):
    return lax.ppermute(value, axis, [(i, i ^ mask) for i in range(lax.axis_size(axis))])


def reorder(value, axis):
    n = lax.axis_size(axis)
    me = lax.axis_index(axis)
    chunk = value.shape[0] // n
    return jnp.concatenate(
        [lax.dynamic_slice_in_dim(value, (me ^ k) * chunk, chunk, 0) for k in range(n)], axis=0
    )


def exchange(chunks, axis):
    return chunks[:1] + [flip(chunks[k], axis, k) for k in reversed(range(1, len(chunks)))]


def spread(chunk, axis):
    return [chunk] + [flip(chunk, axis, k) for k in range(1, lax.axis_size(axis))]


def gather_halves(first, second):
    return [
        lax.all_gather(first, ("rows", "seq"), axis=0, tiled=True),
        lax.all_gather(second, ("seq", "rows"), axis=0, tiled=True),
    ]


def per_device(
    activations,
    doc_lengths,
    w_query,
    key_matrix,
    value_matrix,
    w_output,
    w_gate,
    w_up,
    w_down,
    gain_attn,
    gain_ffn,
    cotangent,
):
    span = activations.shape[1]
    blocks = lax.axis_size("seq")
    chunks = lax.axis_size("tensor")
    chunk = span // chunks
    core = lax.axis_index("rows").astype(jnp.int32).reshape(1)
    block_here = lax.axis_index("seq")
    gain_attn = gain_attn.reshape(1, -1)
    gain_ffn = gain_ffn.reshape(1, -1)
    stream, cotangent = activations[0], cotangent[0]
    me = lax.axis_index("tensor").astype(jnp.int32)
    token = jnp.arange(span, dtype=jnp.int32)
    place = block_here * span + (me ^ (token // chunk)) * chunk + token % chunk
    if chunk % 16:
        stream, cotangent = reorder(stream, "tensor"), reorder(cotangent, "tensor")
        me = jnp.zeros_like(me)
    ends = [doc_lengths[0, 0]]
    for d in range(1, DOCS):
        ends.append(ends[-1] + doc_lengths[0, d])
    begin = jnp.zeros_like(place)
    for end in ends:
        begin = jnp.where(place >= end, end, begin)
    cosine, sine = rope_tables(place - begin)
    shift = jnp.stack([((block_here ^ j) - block_here) * span for j in range(blocks)])
    shift = shift.astype(jnp.int32)
    scalars = jnp.stack([me, ends[-1].astype(jnp.int32)])
    places = (place.reshape(span, 1), place.reshape(1, span), begin.reshape(1, span))

    upstream, *upstream_halves = mask_padding(scalars, cotangent, places[0], chunks, ())
    upstream_all = gather_halves(*upstream_halves)
    normed_one, inverse_one, packed = project_kv(
        scalars, stream, gain_attn, key_matrix, value_matrix, cosine, sine, chunks, (shift, *places, upstream)
    )
    packed = spread(packed, "seq")
    query = project_query(normed_one, w_query, cosine, sine)
    attended, stats, parts = attend(
        shift, query, packed, places, w_output, chunks
    )

    sent = exchange(parts, "tensor")
    grad_hidden = grad_hidden_of(core, upstream, w_down, 1, (parts[0],))
    middle, inverse_two, normed = middle_norm(scalars, stream, gain_ffn, sent, (grad_hidden,))

    grad_hidden_first = grad_hidden_of(core, upstream_all[0], w_down, 2, (middle,))
    normed = join_halves(spread(normed, "tensor"), (grad_hidden_first,))
    normed_all = gather_halves(*normed)
    hidden, parts = feed_own(normed, w_gate, w_up, grad_hidden, chunks)

    sent = exchange(parts, "tensor")
    grad_hidden_second = grad_hidden_of(core, upstream_all[1], w_down, 2, (parts[0],))
    grad_middle, grad_middle_low, gain_two = norm_back(
        upstream, middle, inverse_two, gain_ffn, sent, (grad_hidden_second,)
    )
    grad_middle_all = spread(grad_middle_low, "tensor")
    feed_first = feed_half(
        core, normed_all[0], w_gate, w_up, grad_hidden_first, (grad_middle,)
    )
    down_parts = down_projection(hidden, w_down, (feed_first[0],))
    grad_query, kv_terms = attend_back(
        shift,
        query,
        attended,
        stats,
        packed,
        places,
        cosine,
        sine,
        w_output,
        grad_middle_all,
        (down_parts[0],),
    )
    mask = chunks // 2
    down_came = flip(down_parts[1], "tensor", mask)

    kv_sent = exchange(kv_terms, "seq")
    wo_part = left_product(attended, grad_middle_all, (grad_query,))
    wq_part = left_product(normed_one, [grad_query], (wo_part,))
    grad_kv, gain_one, parts = input_back(
        scalars,
        grad_query,
        w_query,
        key_matrix,
        value_matrix,
        cosine,
        sine,
        inverse_one,
        stream,
        kv_sent,
        chunks,
        (wq_part, normed_all[1]),
    )

    sent = exchange(parts, "tensor")
    wkv_part = kv_product(normed_one, grad_kv, gain_one, gain_two, (parts[0],))
    grad_wo, grad_wq, grad_wkv = lax.psum((wo_part, wq_part, wkv_part), ("rows", "seq"))
    feed_second = feed_half(
        core, normed_all[1], w_gate, w_up, grad_hidden_second, (corner(wkv_part),)
    )
    keep, send = add_half(down_parts[0], down_came, (feed_second[0],))
    while mask > 2:
        mask //= 2
        keep, send = add_half(keep, flip(send, "tensor", mask))
    mask //= 2
    hidden_all, grad_gate_all, grad_up_all = zip(feed_first, feed_second)
    grad_down, low = weight_grad(core, hidden_all, upstream_all, 0, 2, (keep,))
    down_other = [flip(v[None], "rows", 1) for v in low]
    block_chunk = add_up([middle, keep, flip(send, "tensor", mask)], F32, (grad_down,))
    both = finish(
        scalars, stream, inverse_one, gain_attn, grad_middle, block_chunk, sent
    )
    both_all = spread(both, "tensor")
    grad_gate_w, grad_up_w, low = pair_grad(
        core, normed_all, grad_gate_all, grad_up_all, (both,)
    )
    pair_other = flip(low, "rows", 1)
    grad_down = fill_other(core, down_other, 0, grad_down, 0, (grad_up_w,))
    grad_wo, grad_wq, grad_wk, grad_wv = widen(
        grad_wo, grad_wq, grad_wkv, key_matrix.shape[1], (grad_down,)
    )
    grad_input, block_output = restore(scalars, both_all, (grad_wo,))
    grad_gate_w = fill_other(core, [pair_other], 0, grad_gate_w, 1, (grad_input,))
    gains = gain_rows(grad_wkv, (grad_gate_w,))
    grad_up_w = fill_other(core, [pair_other], 1, grad_up_w, 1, (gains,))
    gains = add_up(spread(gains, "tensor"), F32, (grad_up_w,))
    return (
        block_output[None],
        grad_input[None],
        grad_wq,
        grad_wk,
        grad_wv,
        grad_wo,
        grad_gate_w,
        grad_up_w,
        grad_down,
        gains[0],
        gains[1],
    )


def solution(mesh):
    placed = (
        P("rows", "seq", None),
        P("rows", None),
        P(None, "tensor"),
        P(None, "tensor"),
        P(None, "tensor"),
        P("tensor", None),
        P(None, "tensor"),
        P(None, "tensor"),
        P("tensor", None),
        P(),
        P(),
        P("rows", "seq", None),
    )
    return jax.shard_map(
        per_device,
        mesh=mesh,
        in_specs=placed,
        out_specs=(
            P("rows", "seq", None),
            P("rows", "seq", None),
            P(None, "tensor"),
            P(None, "tensor"),
            P(None, "tensor"),
            P("tensor", None),
            P(None, "tensor"),
            P(None, "tensor"),
            P("tensor", None),
            P(),
            P(),
        ),
        check_vma=False,
    )
```

```python
import functools

import jax
import jax.numpy as jnp
from jax import lax
from jax.experimental import pallas as pl
from jax.experimental.pallas import tpu as pltpu
import numpy as np
from jax.sharding import PartitionSpec as P

HEAD_SIZE = 64
DOCS = 4
EPSILON = 1e-05
BF = jnp.bfloat16
F32 = jnp.float32


MIB = 1 << 20


def kernel_params(dims, mib=63):
    return pltpu.CompilerParams(
        vmem_limit_bytes=mib * MIB, dimension_semantics=("arbitrary",) * dims
    )


def contract(a, b, dim_a, dim_b):
    return lax.dot_general(
        a, b, (((dim_a,), (dim_b,)), ((), ())), preferred_element_type=F32
    )


def tile(limit, size):
    while size > limit and size % 2 == 0:
        size //= 2
    return size


SMALL = pl.CostEstimate(flops=1, bytes_accessed=1, transcendentals=0)


def spent(us):
    return pl.CostEstimate(flops=us * 10**9, bytes_accessed=1, transcendentals=0)


def whole_spec(array):
    shape = array.shape
    return pl.BlockSpec(shape, lambda *_: (0,) * len(shape))


def join(refs):
    if refs[0].shape[0] % 16 == 0:
        return jnp.concatenate([r[...] for r in refs], axis=0)
    return jnp.concatenate([r[...].astype(F32) for r in refs], axis=0).astype(refs[0].dtype)


def unread(deps):
    return [pl.BlockSpec(memory_space=pl.ANY)] * len(deps)


def times_transposed_kernel(count, core, weight, *refs):
    refs[-1][...] = contract(join(refs[:count]), weight[...], 1, 1).astype(BF)


def grad_hidden_of(core, pieces, w_down, shares, deps=()):
    count = len(pieces)
    tokens, depth = pieces[0].shape
    units = w_down.shape[0] // shares
    rows, cols = tile(640, tokens), tile(1024 // (3 - shares), units)
    steps = units // cols
    offset = steps * (shares - 1)
    return pl.pallas_call(
        functools.partial(times_transposed_kernel, count),
        out_shape=jax.ShapeDtypeStruct((count * tokens, units), BF),
        grid_spec=pltpu.PrefetchScalarGridSpec(
            num_scalar_prefetch=1,
            grid=(steps, tokens // rows),
            in_specs=[pl.BlockSpec((cols, depth), lambda j, i, c: (c[0] * offset + j, 0))]
            + [pl.BlockSpec((rows, depth), lambda j, i, c: (i, 0))] * count
            + unread(deps),
            out_specs=pl.BlockSpec((count * rows, cols), lambda j, i, c: (i, j)),
        ),
        compiler_params=kernel_params(2),
        cost_estimate=spent(10),
        name="grad_hidden_of",
    )(core, w_down, *pieces, *deps)


def swish_grads(gate, up_proj, grad_hidden):
    sigmoid = 1.0 / (1.0 + jnp.exp(-gate))
    activated = gate * sigmoid
    hidden = (activated * up_proj).astype(BF)
    grad_gate = (grad_hidden * up_proj * (sigmoid * (1.0 + gate * (1.0 - sigmoid)))).astype(BF)
    grad_up = (grad_hidden * activated).astype(BF)
    return hidden, grad_gate, grad_up


def feed_half_kernel(core, normed, gate_w, up_w, grad_hidden, *refs):
    hidden, grad_gate, grad_up = refs[-3:]
    rows = normed[...]
    hidden[...], grad_gate[...], grad_up[...] = swish_grads(
        contract(rows, gate_w[...], 1, 0),
        contract(rows, up_w[...], 1, 0),
        grad_hidden[...].astype(F32),
    )


def feed_half(core, normed, w_gate, w_up, grad_hidden, deps=()):
    tokens, depth = normed.shape
    half = w_gate.shape[1] // 2
    rows, cols = tile(640, tokens), tile(512, half)
    steps = half // cols
    out = jax.ShapeDtypeStruct((tokens, half), BF)
    weight = pl.BlockSpec((depth, cols), lambda j, i, c: (0, c[0] * steps + j))
    block = pl.BlockSpec((rows, cols), lambda j, i, c: (i, j))
    return pl.pallas_call(
        feed_half_kernel,
        out_shape=(out, out, out),
        grid_spec=pltpu.PrefetchScalarGridSpec(
            num_scalar_prefetch=1,
            grid=(steps, tokens // rows),
            in_specs=[
                pl.BlockSpec((rows, depth), lambda j, i, c: (i, 0)),
                weight,
                weight,
                block,
            ]
            + unread(deps),
            out_specs=(block, block, block),
        ),
        compiler_params=kernel_params(2),
        cost_estimate=spent(18),
        name="feed_half",
    )(core, normed, w_gate, w_up, grad_hidden, *deps)


def feed_own_kernel(pieces, chunks, gate_w, up_w, grad_hidden, *refs):
    normed = refs[:pieces]
    hidden, parts = refs[-chunks - 3], refs[-chunks - 2 : -2]
    rows, total = refs[-2:]
    step = pl.program_id(0)
    size = total.shape[0] // chunks

    @pl.when(step == 0)
    def _():
        rows[...] = join(normed)

    gate_now = gate_w[...]
    up_now = up_w[...]
    hidden[...], grad_gate, grad_up = swish_grads(
        contract(rows[...], gate_now, 1, 0),
        contract(rows[...], up_now, 1, 0),
        grad_hidden[...].astype(F32),
    )
    term = contract(grad_gate, gate_now, 1, 1) + contract(grad_up, up_now, 1, 1)

    @pl.when(step == 0)
    def _():
        total[...] = term

    @pl.when(step > 0)
    def _():
        total[...] += term

    @pl.when(step == pl.num_programs(0) - 1)
    def _():
        for k, part in enumerate(parts):
            part[...] = total[k * size : (k + 1) * size].astype(BF)


def feed_own(normed, w_gate, w_up, grad_hidden, chunks, deps=()):
    tokens, units = grad_hidden.shape
    depth = w_gate.shape[0]
    size = tokens // chunks
    cols = tile(512, units)
    weight = pl.BlockSpec((depth, cols), lambda j: (0, j))
    block = pl.BlockSpec((tokens, cols), lambda j: (0, j))
    rows = pl.BlockSpec((size, depth), lambda j: (0, 0))
    out = pl.pallas_call(
        functools.partial(feed_own_kernel, len(normed), chunks),
        out_shape=(jax.ShapeDtypeStruct((tokens, units), BF),)
        + (jax.ShapeDtypeStruct((size, depth), BF),) * chunks,
        grid=(units // cols,),
        in_specs=[weight, weight, block] + [whole_spec(n) for n in normed] + unread(deps),
        out_specs=(block,) + (rows,) * chunks,
        scratch_shapes=[pltpu.VMEM((tokens, depth), BF), pltpu.VMEM((tokens, depth), F32)],
        compiler_params=kernel_params(1),
        cost_estimate=spent(18),
        name="feed_own",
    )(w_gate, w_up, grad_hidden, *normed, *deps)
    return out[0], list(out[1:])


def down_kernel(hidden, weight, *refs):
    keep, send = refs[-2:]
    part = contract(hidden[...], weight[...], 1, 0).astype(BF)
    rows = keep.shape[0]
    keep[...] = part[:rows]
    send[...] = part[rows:]


def down_projection(hidden, w_down, deps=()):
    tokens, units = hidden.shape
    depth = w_down.shape[1]
    cols = tile(512, depth)
    half = jax.ShapeDtypeStruct((tokens // 2, depth), BF)
    block = pl.BlockSpec((tokens // 2, cols), lambda j: (0, j))
    return pl.pallas_call(
        down_kernel,
        out_shape=(half, half),
        grid=(depth // cols,),
        in_specs=[whole_spec(hidden), pl.BlockSpec((units, cols), lambda j: (0, j))]
        + unread(deps),
        out_specs=(block, block),
        compiler_params=kernel_params(1),
        cost_estimate=spent(7),
        name="down_projection",
    )(hidden, w_down, *deps)


def add_half_kernel(keep, came, *refs):
    total = keep[...].astype(F32) + came[...].astype(F32)
    first, second = refs[-2:]
    rows = first.shape[0]
    first[...] = total[:rows].astype(BF)
    second[...] = total[rows:].astype(BF)


def add_half(keep, came, deps=()):
    rows, depth = keep.shape
    half = jax.ShapeDtypeStruct((rows // 2, depth), BF)
    return pl.pallas_call(
        add_half_kernel,
        out_shape=(half, half),
        grid=(1,),
        in_specs=[whole_spec(keep), whole_spec(came)] + unread(deps),
        out_specs=(whole_spec(half), whole_spec(half)),
        compiler_params=kernel_params(1),
        cost_estimate=spent(2),
        name="add_half",
    )(keep, came, *deps)


STEPS = 4


def weight_grad_kernel(count, pieces, core, *refs):
    lefts, rights = refs[:count], refs[count : 2 * count]
    wide, lows = refs[-1 - pieces], refs[-pieces:]
    total = contract(lefts[0][...], rights[0][...], 0, 0)
    for left, right in zip(lefts[1:], rights[1:]):
        total = total + contract(left[...], right[...], 0, 0)
    wide[...] = total
    for k, low in enumerate(lows):

        @pl.when(pl.program_id(1) == k)
        def _():
            low[...] = total.astype(BF)


def weight_grad(core, lefts, rights, dim, pieces, deps=()):
    tokens, m = lefts[0].shape
    n = rights[0].shape[1]
    count = len(lefts)
    rows, cols = m // pieces, tile(1024, n)
    across = n // cols
    if dim == 0:
        full = (2 * m, n)
        place = lambda j, i, c: (c[0] * pieces + i, j)
    else:
        full = (m, 2 * n)
        place = lambda j, i, c: (i, c[0] * across + j)
    share = 1

    def piece(k):
        last = share - 1
        return pl.BlockSpec(
            (rows, cols), lambda j, i, c: (jnp.clip(i - k * share, 0, last), j)
        )

    out = pl.pallas_call(
        functools.partial(weight_grad_kernel, count, pieces),
        out_shape=(jax.ShapeDtypeStruct(full, F32),)
        + (jax.ShapeDtypeStruct((rows * share, n), BF),) * pieces,
        grid_spec=pltpu.PrefetchScalarGridSpec(
            num_scalar_prefetch=1,
            grid=(across, pieces),
            in_specs=[pl.BlockSpec((tokens, rows), lambda j, i, c: (0, i))] * count
            + [pl.BlockSpec((tokens, cols), lambda j, i, c: (0, j))] * count
            + unread(deps),
            out_specs=(pl.BlockSpec((rows, cols), place),)
            + tuple(piece(k) for k in range(pieces)),
        ),
        compiler_params=kernel_params(2),
        cost_estimate=spent(19),
        name="weight_grad",
    )(core, *lefts, *rights, *deps)
    return out[0], list(out[1:])


def pair_grad_kernel(count, core, *refs):
    lefts = [r[...] for r in refs[:count]]
    wides, lows = refs[-4:-2], refs[-2:]
    for k in range(2):
        rights = refs[count * (k + 1) : count * (k + 2)]
        total = contract(lefts[0], rights[0][...], 0, 0)
        for left, right in zip(lefts[1:], rights[1:]):
            total = total + contract(left, right[...], 0, 0)
        wides[k][...] = total
        lows[k][0] = total.astype(BF)


def pair_grad(core, lefts, first, second, deps=()):
    tokens, m = lefts[0].shape
    n = first[0].shape[1]
    count = len(lefts)
    rows = m // STEPS
    wide = jax.ShapeDtypeStruct((m, 2 * n), F32)
    low = jax.ShapeDtypeStruct((1, m, n), BF)
    place = pl.BlockSpec((rows, n), lambda i, c: (i, c[0]))
    here = pl.BlockSpec((1, rows, n), lambda i, c: (0, i, 0))
    out = pl.pallas_call(
        functools.partial(pair_grad_kernel, count),
        out_shape=(wide, wide, low, low),
        grid_spec=pltpu.PrefetchScalarGridSpec(
            num_scalar_prefetch=1,
            grid=(STEPS,),
            in_specs=[pl.BlockSpec((tokens, rows), lambda i, c: (0, i))] * count
            + [whole_spec(v) for v in (*first, *second)]
            + unread(deps),
            out_specs=(place, place, here, here),
        ),
        compiler_params=kernel_params(1),
        cost_estimate=spent(34),
        name="pair_grad",
    )(core, *lefts, *first, *second, *deps)
    return out


def left_product_kernel(count, left, *refs):
    right = join(refs[:count])
    refs[-1][...] = contract(left[...], right, 0, 0).astype(BF)


def left_product(left, pieces, deps=()):
    tokens, m = left.shape
    n = pieces[0].shape[1]
    rows, cols = tile(1024, m), tile(512, n)
    return pl.pallas_call(
        functools.partial(left_product_kernel, len(pieces)),
        out_shape=jax.ShapeDtypeStruct((m, n), BF),
        grid=(m // rows, n // cols),
        in_specs=[pl.BlockSpec((tokens, rows), lambda i, j: (0, i))]
        + [pl.BlockSpec((p.shape[0], cols), lambda i, j: (0, j)) for p in pieces]
        + unread(deps),
        out_specs=pl.BlockSpec((rows, cols), lambda i, j: (i, j)),
        compiler_params=kernel_params(2),
        cost_estimate=spent(4),
        name="left_product",
    )(left, *pieces, *deps)


def kv_product_kernel(left, right, *refs):
    gains, out = refs[:-1], refs[-1]
    width = right.shape[1]
    out[:width, :] = contract(right[...], left[...], 0, 0).astype(BF)
    total = sum_chunks(gains)
    out[width:, :] = jnp.concatenate([total, jnp.zeros(total.shape, F32)], axis=0).astype(BF)


def kv_product(left, right, gains, deps=()):
    tokens, m = left.shape
    width = right.shape[1]
    cols = tile(1024, m)

    def kernel(*refs):
        kv_product_kernel(*refs[: 2 + len(gains)], refs[-1])

    return pl.pallas_call(
        kernel,
        out_shape=jax.ShapeDtypeStruct((width + 16, m), BF),
        grid=(m // cols,),
        in_specs=[pl.BlockSpec((tokens, cols), lambda i: (0, i)), whole_spec(right)]
        + [pl.BlockSpec((8, cols), lambda i: (0, i))] * len(gains)
        + unread(deps),
        out_specs=pl.BlockSpec((width + 16, cols), lambda i: (0, i)),
        compiler_params=kernel_params(1),
        cost_estimate=spent(3),
        name="kv_product",
    )(left, right, *gains, *deps)


def mask_kernel(chunks, scalars, place, *refs):
    value = join(refs[:chunks]).astype(F32)
    refs[-1][...] = jnp.where(place[...] < scalars[1], value, 0.0).astype(BF)


def mask_padding(scalars, value, place, chunks, half, deps=()):
    span, depth = value.shape
    rows = span // 2
    first = half * chunks // 2
    out = jax.ShapeDtypeStruct((rows, depth), BF)
    return pl.pallas_call(
        functools.partial(mask_kernel, chunks // 2),
        out_shape=out,
        grid_spec=pltpu.PrefetchScalarGridSpec(
            num_scalar_prefetch=1,
            grid=(1,),
            in_specs=[pl.BlockSpec((rows, 1), lambda i, c: (half, 0))]
            + [chunk_spec(value, chunks, k) for k in range(first, first + chunks // 2)]
            + unread(deps),
            out_specs=whole_spec(out),
        ),
        compiler_params=kernel_params(1),
        cost_estimate=spent(4),
        name="mask_padding",
    )(scalars, place, *[value] * (chunks // 2), *deps)


def corner_kernel(value, out):
    out[...] = value[...]


def corner(value):
    return pl.pallas_call(
        corner_kernel,
        out_shape=jax.ShapeDtypeStruct((16, 128), value.dtype),
        grid=(1,),
        in_specs=[pl.BlockSpec((16, 128), lambda i: (0, 0))],
        out_specs=pl.BlockSpec((16, 128), lambda i: (0, 0)),
        compiler_params=kernel_params(1),
        cost_estimate=spent(5),
        name="corner",
    )(value)


def fill_other_kernel(pieces, core, *refs):
    step = pl.program_id(0)
    for k in range(pieces):

        @pl.when(step // (STEPS // pieces) == k)
        def _():
            refs[-1][...] = refs[k][...].astype(F32).reshape(refs[-1].shape)


def fill_other(core, others, index, held, dim, deps=()):
    pieces = len(others)
    share = STEPS // pieces
    rows, n = others[0].shape[1] // share, others[0].shape[2]
    if dim == 0:
        place = lambda i, c: ((1 - c[0]) * STEPS + i, 0)
    else:
        place = lambda i, c: (i, 1 - c[0])

    def piece(k):
        last = share - 1
        return pl.BlockSpec(
            (1, rows, n), lambda i, c: (index, jnp.clip(i - k * share, 0, last), 0)
        )

    return pl.pallas_call(
        functools.partial(fill_other_kernel, pieces),
        out_shape=jax.ShapeDtypeStruct(held.shape, F32),
        grid_spec=pltpu.PrefetchScalarGridSpec(
            num_scalar_prefetch=1,
            grid=(STEPS,),
            in_specs=[piece(k) for k in range(pieces)]
            + [pl.BlockSpec(memory_space=pl.ANY)]
            + unread(deps),
            out_specs=pl.BlockSpec((rows, n), place),
        ),
        input_output_aliases={1 + pieces: 0},
        compiler_params=kernel_params(1),
        cost_estimate=spent(87),
        name="fill_other",
    )(core, *others, held, *deps)


def rotate_block(values, cosine, sine):
    width = values.shape[1]
    column = lax.broadcasted_iota(jnp.int32, values.shape, 1)
    other = jnp.where(
        column % HEAD_SIZE < HEAD_SIZE // 2,
        pltpu.roll(values, width - HEAD_SIZE // 2, 1),
        pltpu.roll(values, HEAD_SIZE // 2, 1),
    )
    return values * cosine + other * sine


def pack_rotated(keys, values, cosine, sine):
    width = keys.shape[1]
    if width % 128 == 0:
        turned = [
            rotate_block(keys[:, i : i + 128], cosine, sine) for i in range(0, width, 128)
        ]
        return jnp.concatenate(turned + [values], axis=1)
    both = jnp.concatenate([keys, values], axis=1)
    column = lax.broadcasted_iota(jnp.int32, both.shape, 1)
    return jnp.where(column < width, rotate_block(both, cosine, sine), both)


def chunk_spec(array, chunks, k):
    block = (array.shape[0] // chunks, array.shape[1])
    return pl.BlockSpec(block, lambda *a: (a[-1][0] ^ k, 0))


def project_kv_kernel(chunks, waits, me, *refs):
    gain, key_w, value_w, cosine, sine = refs[chunks : chunks + 5]
    normed, inverse, packed = refs[-3:]
    stream = join(refs[:chunks]).astype(F32)
    scale = lax.rsqrt(jnp.mean(stream * stream, axis=1, keepdims=True) + EPSILON)
    low = (stream * scale * gain[...]).astype(BF)
    normed[...] = low
    inverse[...] = jnp.broadcast_to(scale, inverse.shape)
    packed[...] = pack_rotated(
        contract(low, key_w[...], 1, 0), contract(low, value_w[...], 1, 0), cosine[...], sine[...]
    ).astype(BF)


def project_kv(me, x, gain, key_matrix, value_matrix, cosine, sine, chunks, deps=()):
    span, depth = x.shape
    args = (gain, key_matrix, value_matrix, cosine, sine)
    outs = (
        jax.ShapeDtypeStruct((span, depth), BF),
        jax.ShapeDtypeStruct((span, 128), F32),
        jax.ShapeDtypeStruct((span, 2 * key_matrix.shape[1]), BF),
    )
    return pl.pallas_call(
        functools.partial(project_kv_kernel, chunks, len(deps)),
        out_shape=outs,
        grid_spec=pltpu.PrefetchScalarGridSpec(
            num_scalar_prefetch=1,
            grid=(1,),
            in_specs=[chunk_spec(x, chunks, k) for k in range(chunks)]
            + [whole_spec(a) for a in args]
            + unread(deps),
            out_specs=tuple(whole_spec(a) for a in outs),
        ),
        compiler_params=kernel_params(1),
        cost_estimate=spent(4),
        name="project_kv",
    )(me, *[x] * chunks, *args, *deps)


def project_query_kernel(normed, weight, cosine, sine, *refs):
    out = refs[-1]
    lin = contract(normed[...], weight[...], 1, 0)
    for i in range(0, lin.shape[1], 128):
        turned = rotate_block(lin[:, i : i + 128], cosine[...], sine[...])
        out[:, i : i + 128] = (turned * HEAD_SIZE**-0.5).astype(BF)


def project_query(normed, w_query, cosine, sine, deps=()):
    span, depth = normed.shape
    width = w_query.shape[1]
    cols = 256
    return pl.pallas_call(
        project_query_kernel,
        out_shape=jax.ShapeDtypeStruct((span, width), BF),
        grid=(width // cols,),
        in_specs=[
            whole_spec(normed),
            pl.BlockSpec((depth, cols), lambda j: (0, j)),
            whole_spec(cosine),
            whole_spec(sine),
        ]
        + unread(deps),
        out_specs=pl.BlockSpec((span, cols), lambda j: (0, j)),
        compiler_params=kernel_params(1),
        cost_estimate=spent(4),
        name="project_query",
    )(normed, w_query, cosine, sine, *deps)


def head_columns(array, index):
    return array[:, index * HEAD_SIZE : (index + 1) * HEAD_SIZE]


def stack_heads(array, heads):
    return jnp.concatenate([head_columns(array, h) for h in heads], axis=0)


def store_heads(out, turned, first, span, finish):
    for i in range(0, turned.shape[1] // span, 2):
        pair = jnp.concatenate(
            [turned[:, (i + e) * span : (i + e + 1) * span] for e in range(2)], axis=0
        )
        at = (first + i) * HEAD_SIZE
        out[:, at : at + 128] = finish(jnp.transpose(pair)).astype(BF)


def attend_kernel(blocks, chunks, shift, query, place, place_row, begin_row, w_output, *refs):
    packed = refs[:blocks]
    attended, stats, *parts = refs[-2 - chunks :]
    span, width = query.shape
    heads_kv = packed[0].shape[1] // (2 * HEAD_SIZE)
    group = width // HEAD_SIZE // heads_kv
    last = jnp.concatenate([place_row[...]] * group, axis=1)
    first = jnp.concatenate([begin_row[...]] * group, axis=1)
    for g in range(heads_kv):
        q = stack_heads(query, range(g * group, (g + 1) * group))
        top = total = mixed = None
        for j in range(blocks):
            keys = head_columns(packed[j], g)
            values = head_columns(packed[j], heads_kv + g)
            key_place = place[...] + shift[j]
            allowed = (key_place >= first) & (key_place <= last)
            masked = jnp.where(allowed, contract(keys, q, 1, 1), -1e30)
            peak = jnp.max(masked, axis=0, keepdims=True)
            peak = peak if j == 0 else jnp.maximum(top, peak)
            terms = jnp.exp(masked - peak)
            amount = jnp.sum(terms, axis=0, keepdims=True)
            term = contract(values, terms.astype(BF), 0, 0)
            if j == 0:
                total, mixed = amount, term
            else:
                fade = jnp.exp(top - peak)
                total, mixed = total * fade + amount, mixed * fade + term
            top = peak
        stats[g : g + 1, :] = top + jnp.log(total)
        store_heads(attended, mixed * (1.0 / total), g * group, span, lambda v: v)
    part = contract(attended[...], w_output[...], 1, 0)
    chunk = span // len(parts)
    for k, out in enumerate(parts):
        out[...] = part[k * chunk : (k + 1) * chunk].astype(BF)


def attend(shift, query, packed, places, w_output, chunks, deps=()):
    span, width = query.shape
    depth = w_output.shape[1]
    blocks = len(packed)
    heads_kv = packed[0].shape[1] // (2 * HEAD_SIZE)
    args = (
        query,
        *places,
        w_output,
        *packed,
    )
    outs = (
        jax.ShapeDtypeStruct((span, width), BF),
        jax.ShapeDtypeStruct((heads_kv, width // HEAD_SIZE // heads_kv * span), F32),
    )
    outs += (jax.ShapeDtypeStruct((span // chunks, depth), BF),) * chunks
    out = pl.pallas_call(
        functools.partial(attend_kernel, blocks, chunks),
        out_shape=outs,
        grid_spec=pltpu.PrefetchScalarGridSpec(
            num_scalar_prefetch=1,
            grid=(1,),
            in_specs=[whole_spec(a) for a in args] + unread(deps),
            out_specs=tuple(whole_spec(a) for a in outs),
        ),
        compiler_params=kernel_params(1),
        cost_estimate=spent(11),
        name="attend",
    )(shift, *args, *deps)
    return out[0], out[1], list(out[2:])


def sum_chunks(refs):
    total = refs[0][...].astype(F32)
    for ref in refs[1:]:
        total = total + ref[...].astype(F32)
    return total


def middle_kernel(count, me, x, gain, *refs):
    chunks, (middle, inverse, normed) = refs[:count], refs[-3:]
    stream = x[...].astype(F32) + sum_chunks(chunks)
    scale = lax.rsqrt(jnp.mean(stream * stream, axis=1, keepdims=True) + EPSILON)
    middle[...] = stream
    inverse[...] = jnp.broadcast_to(scale, inverse.shape)
    normed[...] = (stream * scale * gain[...]).astype(BF)


def middle_norm(me, x, gain, chunks, deps=()):
    rows, depth = chunks[0].shape
    outs = (
        jax.ShapeDtypeStruct((rows, depth), F32),
        jax.ShapeDtypeStruct((rows, 128), F32),
        jax.ShapeDtypeStruct((rows, depth), BF),
    )
    return pl.pallas_call(
        functools.partial(middle_kernel, len(chunks)),
        out_shape=outs,
        grid_spec=pltpu.PrefetchScalarGridSpec(
            num_scalar_prefetch=1,
            grid=(1,),
            in_specs=[chunk_spec(x, len(chunks), 0)]
            + [whole_spec(a) for a in (gain, *chunks)]
            + unread(deps),
            out_specs=tuple(whole_spec(a) for a in outs),
        ),
        compiler_params=kernel_params(1),
        cost_estimate=spent(120),
        name="middle_norm",
    )(me, x, gain, *chunks, *deps)


def halves_kernel(count, *refs):
    half = count // 2
    refs[-2][...] = join(refs[:half])
    refs[-1][...] = join(refs[half:count])


def join_halves(chunks, deps=()):
    rows, depth = chunks[0].shape
    outs = (jax.ShapeDtypeStruct((rows * len(chunks) // 2, depth), BF),) * 2
    return pl.pallas_call(
        functools.partial(halves_kernel, len(chunks)),
        out_shape=outs,
        grid=(1,),
        in_specs=[whole_spec(a) for a in chunks] + unread(deps),
        out_specs=tuple(whole_spec(a) for a in outs),
        compiler_params=kernel_params(1),
        cost_estimate=spent(2),
        name="join_halves",
    )(*chunks, *deps)


def norm_gradient(grad, rows, scale, gain):
    scaled = grad * gain
    product = jnp.mean(scaled * rows, axis=1, keepdims=True)
    gain_grad = jnp.sum(grad * rows * scale, axis=0, keepdims=True)
    return scale * scaled - rows * (scale * scale * scale * product), gain_grad


def norm_back_kernel(count, upstream, middle, inverse, gain, *refs):
    chunks, (wide, low, gain_grad) = refs[:count], refs[-3:]
    grad, gain_grad[...] = norm_gradient(
        sum_chunks(chunks), middle[...], inverse[:, :1], gain[...]
    )
    total = upstream[...].astype(F32) + grad
    wide[...] = total
    low[...] = total.astype(BF)


def norm_back(upstream, middle, inverse, gain, chunks, deps=()):
    rows, depth = middle.shape
    args = (middle, inverse, gain, *chunks)
    outs = (
        jax.ShapeDtypeStruct((rows, depth), F32),
        jax.ShapeDtypeStruct((rows, depth), BF),
        jax.ShapeDtypeStruct((1, depth), F32),
    )
    return pl.pallas_call(
        functools.partial(norm_back_kernel, len(chunks)),
        out_shape=outs,
        grid=(1,),
        in_specs=[pl.BlockSpec((rows, depth), lambda i: (0, 0))]
        + [whole_spec(a) for a in args]
        + unread(deps),
        out_specs=tuple(whole_spec(a) for a in outs),
        compiler_params=kernel_params(1),
        cost_estimate=spent(3),
        name="norm_back",
    )(upstream, *args, *deps)


def finish_kernel(count, me, x, inverse, gain, grad_middle, block, *refs):
    grad, _ = norm_gradient(
        sum_chunks(refs[:count]), x[...].astype(F32), inverse[:, :1], gain[...]
    )
    refs[-1][...] = jnp.concatenate([grad_middle[...] + grad, block[...]], axis=0).astype(BF)


def finish(me, x, inverse, gain, grad_middle, block, chunks, deps=()):
    rows, depth = grad_middle.shape
    args = (gain, grad_middle, block, *chunks)
    outs = jax.ShapeDtypeStruct((2 * rows, depth), BF)
    return pl.pallas_call(
        functools.partial(finish_kernel, len(chunks)),
        out_shape=outs,
        grid_spec=pltpu.PrefetchScalarGridSpec(
            num_scalar_prefetch=1,
            grid=(1,),
            in_specs=[
                chunk_spec(x, len(chunks), 0),
                pl.BlockSpec((rows, 128), lambda i, c: (0, 0)),
            ]
            + [whole_spec(a) for a in args]
            + unread(deps),
            out_specs=whole_spec(outs),
        ),
        compiler_params=kernel_params(1),
        cost_estimate=spent(3),
        name="finish",
    )(me, x, inverse, *args, *deps)


def add_kernel(count, *refs):
    refs[-1][...] = sum_chunks(refs[:count]).astype(refs[-1].dtype)


def add_up(arrays, dtype, deps=()):
    out = jax.ShapeDtypeStruct(arrays[0].shape, dtype)
    return pl.pallas_call(
        functools.partial(add_kernel, len(arrays)),
        out_shape=out,
        grid=(1,),
        in_specs=[whole_spec(a) for a in arrays] + unread(deps),
        out_specs=whole_spec(out),
        compiler_params=kernel_params(1),
        cost_estimate=spent(2),
        name="add_up",
    )(*arrays, *deps)


def restore_kernel(count, me, *refs):
    step = pl.program_id(0)
    for k in range(count):

        @pl.when(step == k)
        def _():
            rows = refs[k].shape[0] // 2
            refs[-2][...] = refs[k][:rows]
            refs[-1][...] = refs[k][rows:]


def restore(me, pieces, deps=()):
    count = len(pieces)
    rows, depth = pieces[0].shape[0] // 2, pieces[0].shape[1]
    if rows % 16:
        halves = [[p[:rows] for p in pieces], [p[rows:] for p in pieces]]
        return [reorder(jnp.concatenate(h, axis=0), "tensor") for h in halves]
    out = jax.ShapeDtypeStruct((count * rows, depth), BF)
    place = pl.BlockSpec((rows, depth), lambda i, c: (c[0] ^ i, 0))
    return pl.pallas_call(
        functools.partial(restore_kernel, count),
        out_shape=(out, out),
        grid_spec=pltpu.PrefetchScalarGridSpec(
            num_scalar_prefetch=1,
            grid=(count,),
            in_specs=[whole_spec(p) for p in pieces] + unread(deps),
            out_specs=(place, place),
        ),
        compiler_params=kernel_params(1),
        cost_estimate=spent(87),
        name="restore",
    )(me, *pieces, *deps)


def widen(wo, wq, wkv, width, deps=()):
    steps = 4
    depth = wq.shape[0]
    shapes = [wo.shape, wq.shape, (depth, width), (depth, width)]

    def spec(shape):
        return pl.BlockSpec((shape[0] // steps, shape[1]), lambda i: (i, 0))

    def kernel(wo, wq, wkv, *refs):
        wo_out, wq_out, wk_out, wv_out, gains = refs[-5:]
        wo_out[...] = wo[...].astype(F32)
        wq_out[...] = wq[...].astype(F32)
        turned = jnp.transpose(wkv[: 2 * width, :].astype(F32))
        wk_out[...] = turned[:, :width]
        wv_out[...] = turned[:, width:]
        gains[...] = wkv[2 * width :, :].astype(F32)

    return pl.pallas_call(
        kernel,
        out_shape=tuple(jax.ShapeDtypeStruct(v, F32) for v in [*shapes, (16, depth)]),
        grid=(steps,),
        in_specs=[
            spec(wo.shape),
            spec(wq.shape),
            pl.BlockSpec((wkv.shape[0], depth // steps), lambda i: (0, i)),
        ]
        + unread(deps),
        out_specs=tuple(spec(v) for v in shapes)
        + (pl.BlockSpec((16, depth // steps), lambda i: (0, i)),),
        compiler_params=kernel_params(1),
        cost_estimate=spent(8),
        name="widen",
    )(wo, wq, wkv, *deps)


def attend_back_kernel(blocks, count, shift, query, attended, stats, place, place_row, begin_row,
                       cosine, sine, w_output, *refs):
    packed = refs[:blocks]
    chunks = refs[blocks : blocks + count]
    grad_query = refs[-1 - blocks]
    terms = refs[-blocks:]
    span, width = query.shape
    heads_kv = packed[0].shape[1] // (2 * HEAD_SIZE)
    group = width // HEAD_SIZE // heads_kv
    grad_middle = join(chunks)
    grad_attended = contract(grad_middle, w_output[...], 1, 1).astype(BF)
    last = jnp.concatenate([place_row[...]] * group, axis=1)
    first = jnp.concatenate([begin_row[...]] * group, axis=1)
    key_terms = [[] for _ in range(blocks)]
    value_terms = [[] for _ in range(blocks)]
    for g in range(heads_kv):
        mine = range(g * group, (g + 1) * group)
        q = stack_heads(query, mine)
        grad = stack_heads(grad_attended, mine)
        norm = stats[g : g + 1, :]
        inner = lax.dot_general(
            jnp.ones((8, HEAD_SIZE), F32),
            grad.astype(F32) * stack_heads(attended, mine).astype(F32),
            (((1,), (1,)), ((), ())),
            preferred_element_type=F32,
            precision=lax.Precision.HIGHEST,
        )[:1]
        total = None
        for j in range(blocks):
            keys = head_columns(packed[j], g)
            values = head_columns(packed[j], heads_kv + g)
            key_place = place[...] + shift[j]
            allowed = (key_place >= first) & (key_place <= last)
            scores = contract(keys, q, 1, 1)
            probs = jnp.exp(jnp.where(allowed, scores - norm, -1e30))
            grad_scores = (probs * (contract(values, grad, 1, 1) - inner)).astype(BF)
            value_terms[j].append(contract(probs.astype(BF), grad, 1, 0))
            key_terms[j].append(contract(grad_scores, q, 1, 0))
            term = contract(keys, grad_scores, 0, 0)
            total = term if total is None else total + term
        store_heads(
            grad_query,
            total,
            g * group,
            span,
            lambda v: rotate_block(v * HEAD_SIZE**-0.5, cosine[...], -sine[...]),
        )
    for j in range(blocks):
        terms[j][...] = jnp.concatenate(key_terms[j] + value_terms[j], axis=1).astype(BF)


def attend_back(shift, query, attended, stats, packed, places, cosine, sine, w_output, chunks,
                deps=()):
    span, width = query.shape
    blocks = len(packed)
    args = (
        query,
        attended,
        stats,
        *places,
        cosine,
        sine,
        w_output,
        *packed,
        *chunks,
    )
    outs = (jax.ShapeDtypeStruct((span, width), BF),)
    outs += (jax.ShapeDtypeStruct(packed[0].shape, BF),) * blocks
    out = pl.pallas_call(
        functools.partial(attend_back_kernel, blocks, len(chunks)),
        out_shape=outs,
        grid_spec=pltpu.PrefetchScalarGridSpec(
            num_scalar_prefetch=1,
            grid=(1,),
            in_specs=[whole_spec(a) for a in args] + unread(deps),
            out_specs=tuple(whole_spec(a) for a in outs),
        ),
        compiler_params=kernel_params(1),
        cost_estimate=spent(16),
        name="attend_back",
    )(shift, *args, *deps)
    return out[0], list(out[1:])


def input_back_kernel(
    count, chunks, me, grad_query, w_query, key_w, value_w, cosine, sine, inverse, gain_two, *refs
):
    terms, rows = refs[:count], refs[count : count + chunks]
    lin, gains, *parts = refs[-2 - chunks :]
    normed = join(rows).astype(F32) * inverse[:, :1]
    width = key_w.shape[1]
    total = sum_chunks(terms)
    low = pack_rotated(total[:, :width], total[:, width:], cosine[...], -sine[...]).astype(BF)
    lin[...] = low
    part = contract(grad_query[...], w_query[...], 1, 1)
    part = part + contract(low[:, :width], key_w[...], 1, 1)
    part = part + contract(low[:, width:], value_w[...], 1, 1)
    rows = part.shape[0] // chunks
    for k, out in enumerate(parts):
        out[...] = part[k * rows : (k + 1) * rows].astype(BF)
    gain_one = jnp.sum(part * normed, axis=0, keepdims=True)
    empty = jnp.zeros((6, part.shape[1]), F32)
    gains[...] = jnp.concatenate([gain_one, gain_two[...], empty], axis=0)


def input_back(
    me,
    grad_query,
    w_query,
    key_matrix,
    value_matrix,
    cosine,
    sine,
    inverse,
    x,
    gain_two,
    terms,
    chunks,
    deps=(),
):
    span = grad_query.shape[0]
    depth = w_query.shape[0]
    args = (grad_query, w_query, key_matrix, value_matrix, cosine, sine, inverse, gain_two)
    args += tuple(terms)
    outs = (
        jax.ShapeDtypeStruct(terms[0].shape, BF),
        jax.ShapeDtypeStruct((8, depth), F32),
    )
    outs += (jax.ShapeDtypeStruct((span // chunks, depth), BF),) * chunks
    out = pl.pallas_call(
        functools.partial(input_back_kernel, len(terms), chunks),
        out_shape=outs,
        grid_spec=pltpu.PrefetchScalarGridSpec(
            num_scalar_prefetch=1,
            grid=(1,),
            in_specs=[whole_spec(a) for a in args]
            + [chunk_spec(x, chunks, k) for k in range(chunks)]
            + unread(deps),
            out_specs=tuple(whole_spec(a) for a in outs),
        ),
        compiler_params=kernel_params(1),
        cost_estimate=spent(6),
        name="input_back",
    )(me, *args, *[x] * chunks, *deps)
    return out[0], out[1], list(out[2:])


def rope_tables(positions):
    expo = np.arange(HEAD_SIZE // 2, dtype=np.float64) * 2.0 / HEAD_SIZE
    inverse = 1.0 / 500000.0**expo
    wavelength = 2.0 * np.pi / inverse
    smooth = (8192.0 / wavelength - 1.0) / 3.0
    middle = (1.0 - smooth) * inverse / 32.0 + smooth * inverse
    scaled = np.where(
        wavelength < 2048.0, inverse, np.where(wavelength > 8192.0, inverse / 32.0, middle)
    )
    scaled = jnp.asarray(np.tile(scaled, 4)[None, :].astype(np.float32))
    sign = jnp.asarray(np.tile(np.repeat([-1.0, 1.0], HEAD_SIZE // 2), 2)[None, :].astype(np.float32))
    angles = positions.astype(F32)[:, None] * scaled
    return jnp.cos(angles), jnp.sin(angles) * sign


def flip(value, axis, mask):
    return lax.ppermute(value, axis, [(i, i ^ mask) for i in range(lax.axis_size(axis))])


def reorder(value, axis):
    n = lax.axis_size(axis)
    me = lax.axis_index(axis)
    chunk = value.shape[0] // n
    return jnp.concatenate(
        [lax.dynamic_slice_in_dim(value, (me ^ k) * chunk, chunk, 0) for k in range(n)], axis=0
    )


def exchange(chunks, axis):
    return chunks[:1] + [flip(chunks[k], axis, k) for k in reversed(range(1, len(chunks)))]


def spread(chunk, axis):
    return [chunk] + [flip(chunk, axis, k) for k in range(1, lax.axis_size(axis))]


def gather_halves(first, second):
    return [
        lax.all_gather(first, ("rows", "seq"), axis=0, tiled=True),
        lax.all_gather(second, ("seq", "rows"), axis=0, tiled=True),
    ]


def per_device(
    activations,
    doc_lengths,
    w_query,
    key_matrix,
    value_matrix,
    w_output,
    w_gate,
    w_up,
    w_down,
    gain_attn,
    gain_ffn,
    cotangent,
):
    span = activations.shape[1]
    blocks = lax.axis_size("seq")
    chunks = lax.axis_size("tensor")
    chunk = span // chunks
    core = lax.axis_index("rows").astype(jnp.int32).reshape(1)
    block_here = lax.axis_index("seq")
    gain_attn = gain_attn.reshape(1, -1)
    gain_ffn = gain_ffn.reshape(1, -1)
    stream, cotangent = activations[0], cotangent[0]
    me = lax.axis_index("tensor").astype(jnp.int32)
    token = jnp.arange(span, dtype=jnp.int32)
    place = block_here * span + (me ^ (token // chunk)) * chunk + token % chunk
    if chunk % 16:
        stream, cotangent = reorder(stream, "tensor"), reorder(cotangent, "tensor")
        me = jnp.zeros_like(me)
    ends = [doc_lengths[0, 0]]
    for d in range(1, DOCS):
        ends.append(ends[-1] + doc_lengths[0, d])
    begin = jnp.zeros_like(place)
    for end in ends:
        begin = jnp.where(place >= end, end, begin)
    cosine, sine = rope_tables(place - begin)
    shift = jnp.stack([((block_here ^ j) - block_here) * span for j in range(blocks)])
    shift = shift.astype(jnp.int32)
    scalars = jnp.stack([me, ends[-1].astype(jnp.int32)])
    places = (place.reshape(span, 1), place.reshape(1, span), begin.reshape(1, span))

    normed_one, inverse_one, packed = project_kv(
        scalars, stream, gain_attn, key_matrix, value_matrix, cosine, sine, chunks, (shift, *places)
    )
    packed = spread(packed, "seq")
    query = project_query(normed_one, w_query, cosine, sine)
    upstream = [mask_padding(scalars, cotangent, places[0], chunks, 0, (query, *packed))]
    upstream_all = [lax.all_gather(upstream[0], ("rows", "seq"), axis=0, tiled=True)]
    attended, stats, parts = attend(
        shift, query, packed, places, w_output, chunks, (upstream[0],)
    )
    upstream.append(mask_padding(scalars, cotangent, places[0], chunks, 1, (parts[0],)))
    upstream_all.append(lax.all_gather(upstream[1], ("seq", "rows"), axis=0, tiled=True))

    sent = exchange(parts, "tensor")
    grad_hidden = grad_hidden_of(core, upstream, w_down, 1, (parts[0],))
    middle, inverse_two, normed = middle_norm(scalars, stream, gain_ffn, sent, (grad_hidden,))

    grad_hidden_first = grad_hidden_of(core, upstream_all[:1], w_down, 2, (middle,))
    normed = join_halves(spread(normed, "tensor"), (grad_hidden_first,))
    normed_all = gather_halves(*normed)
    hidden, parts = feed_own(normed, w_gate, w_up, grad_hidden, chunks)

    sent = exchange(parts, "tensor")
    grad_hidden_second = grad_hidden_of(core, upstream_all[1:], w_down, 2, (parts[0],))
    grad_middle, grad_middle_low, gain_two = norm_back(
        upstream[0], middle, inverse_two, gain_ffn, sent, (grad_hidden_second,)
    )
    grad_middle_all = spread(grad_middle_low, "tensor")
    feed_first = feed_half(
        core, normed_all[0], w_gate, w_up, grad_hidden_first, (grad_middle,)
    )
    down_parts = down_projection(hidden, w_down, (feed_first[0],))
    grad_query, kv_terms = attend_back(
        shift,
        query,
        attended,
        stats,
        packed,
        places,
        cosine,
        sine,
        w_output,
        grad_middle_all,
        (corner(down_parts[0]),),
    )
    mask = chunks // 2
    down_came = flip(down_parts[1], "tensor", mask)

    kv_sent = exchange(kv_terms, "seq")
    wq_part = left_product(normed_one, [grad_query])
    keep, send = add_half(down_parts[0], down_came, (wq_part,))
    while mask > 2:
        mask //= 2
        keep, send = add_half(keep, flip(send, "tensor", mask))
    block_sent = [middle, keep, flip(send, "tensor", mask // 2)]
    grad_kv, gains, parts = input_back(
        scalars,
        grad_query,
        w_query,
        key_matrix,
        value_matrix,
        cosine,
        sine,
        inverse_one,
        stream,
        gain_two,
        kv_sent,
        chunks,
        (keep, normed_all[1]),
    )

    gains = spread(gains, "tensor")
    wo_part = left_product(attended, grad_middle_all, (parts[0],))
    wkv_part = kv_product(normed_one, grad_kv, gains, (wo_part,))
    sent = exchange(parts, "tensor")
    grad_wo, grad_wq, grad_wkv = lax.psum((wo_part, wq_part, wkv_part), ("rows", "seq"))
    block_chunk = add_up(block_sent, F32, (wkv_part,))
    feed_second = feed_half(
        core, normed_all[1], w_gate, w_up, grad_hidden_second, (block_chunk,)
    )
    hidden_all, grad_gate_all, grad_up_all = zip(feed_first, feed_second)
    grad_down, low = weight_grad(core, hidden_all, upstream_all, 0, 2)
    down_other = [flip(v[None], "rows", 1) for v in low]
    both = finish(
        scalars, stream, inverse_one, gain_attn, grad_middle, block_chunk, sent, (grad_down,)
    )
    both_all = spread(both, "tensor")
    grad_gate_w, grad_up_w, *low = pair_grad(
        core, normed_all, grad_gate_all, grad_up_all, (both,)
    )
    gate_other, up_other = [flip(v, "rows", 1) for v in low]
    grad_down = fill_other(core, down_other, 0, grad_down, 0, (grad_up_w,))
    grad_gate_w = fill_other(core, [gate_other], 0, grad_gate_w, 1, (grad_down,))
    grad_wo, grad_wq, grad_wk, grad_wv, gains = widen(
        grad_wo, grad_wq, grad_wkv, key_matrix.shape[1], (grad_gate_w,)
    )
    grad_input, block_output = restore(scalars, both_all, (grad_wo,))
    grad_up_w = fill_other(core, [up_other], 0, grad_up_w, 1, (grad_input,))
    return (
        block_output[None],
        grad_input[None],
        grad_wq,
        grad_wk,
        grad_wv,
        grad_wo,
        grad_gate_w,
        grad_up_w,
        grad_down,
        gains[0],
        gains[1],
    )


def solution(mesh):
    placed = (
        P("rows", "seq", None),
        P("rows", None),
        P(None, "tensor"),
        P(None, "tensor"),
        P(None, "tensor"),
        P("tensor", None),
        P(None, "tensor"),
        P(None, "tensor"),
        P("tensor", None),
        P(),
        P(),
        P("rows", "seq", None),
    )
    return jax.shard_map(
        per_device,
        mesh=mesh,
        in_specs=placed,
        out_specs=(
            P("rows", "seq", None),
            P("rows", "seq", None),
            P(None, "tensor"),
            P(None, "tensor"),
            P(None, "tensor"),
            P("tensor", None),
            P(None, "tensor"),
            P(None, "tensor"),
            P("tensor", None),
            P(),
            P(),
        ),
        check_vma=False,
    )
```

```python
import functools

import jax
import jax.numpy as jnp
from jax import lax
from jax.experimental import pallas as pl
from jax.experimental.pallas import tpu as pltpu
import numpy as np
from jax.sharding import PartitionSpec as P

HEAD_SIZE = 64
DOCS = 4
EPSILON = 1e-05
BF = jnp.bfloat16
F32 = jnp.float32


MIB = 1 << 20


def kernel_params(dims, mib=63):
    return pltpu.CompilerParams(
        vmem_limit_bytes=mib * MIB, dimension_semantics=("arbitrary",) * dims
    )


def contract(a, b, dim_a, dim_b):
    return lax.dot_general(
        a, b, (((dim_a,), (dim_b,)), ((), ())), preferred_element_type=F32
    )


def tile(limit, size):
    while size > limit and size % 2 == 0:
        size //= 2
    return size


SMALL = pl.CostEstimate(flops=1, bytes_accessed=1, transcendentals=0)


def spent(us):
    return pl.CostEstimate(flops=us * 10**9, bytes_accessed=1, transcendentals=0)


def whole_spec(array):
    shape = array.shape
    return pl.BlockSpec(shape, lambda *_: (0,) * len(shape))


def join(refs):
    if refs[0].shape[0] % 16 == 0:
        return jnp.concatenate([r[...] for r in refs], axis=0)
    return jnp.concatenate([r[...].astype(F32) for r in refs], axis=0).astype(refs[0].dtype)


def unread(deps):
    return [pl.BlockSpec(memory_space=pl.ANY)] * len(deps)


def times_transposed_kernel(count, core, weight, *refs):
    refs[-1][...] = contract(join(refs[:count]), weight[...], 1, 1).astype(BF)


def grad_hidden_of(core, pieces, w_down, shares, deps=()):
    count = len(pieces)
    tokens, depth = pieces[0].shape
    units = w_down.shape[0] // shares
    rows, cols = tile(640, tokens), tile(1024 // (3 - shares), units)
    steps = units // cols
    offset = steps * (shares - 1)
    return pl.pallas_call(
        functools.partial(times_transposed_kernel, count),
        out_shape=jax.ShapeDtypeStruct((count * tokens, units), BF),
        grid_spec=pltpu.PrefetchScalarGridSpec(
            num_scalar_prefetch=1,
            grid=(steps, tokens // rows),
            in_specs=[pl.BlockSpec((cols, depth), lambda j, i, c: (c[0] * offset + j, 0))]
            + [pl.BlockSpec((rows, depth), lambda j, i, c: (i, 0))] * count
            + unread(deps),
            out_specs=pl.BlockSpec((count * rows, cols), lambda j, i, c: (i, j)),
        ),
        compiler_params=kernel_params(2),
        cost_estimate=spent(10),
        name="grad_hidden_of",
    )(core, w_down, *pieces, *deps)


def swish_grads(gate, up_proj, grad_hidden):
    sigmoid = 1.0 / (1.0 + jnp.exp(-gate))
    activated = gate * sigmoid
    hidden = (activated * up_proj).astype(BF)
    grad_gate = (grad_hidden * up_proj * (sigmoid * (1.0 + gate * (1.0 - sigmoid)))).astype(BF)
    grad_up = (grad_hidden * activated).astype(BF)
    return hidden, grad_gate, grad_up


def feed_half_kernel(core, normed, gate_w, up_w, grad_hidden, *refs):
    hidden, grad_gate, grad_up = refs[-3:]
    rows = normed[...]
    hidden[...], grad_gate[...], grad_up[...] = swish_grads(
        contract(rows, gate_w[...], 1, 0),
        contract(rows, up_w[...], 1, 0),
        grad_hidden[...].astype(F32),
    )


def feed_half(core, normed, w_gate, w_up, grad_hidden, deps=()):
    tokens, depth = normed.shape
    half = w_gate.shape[1] // 2
    rows, cols = tile(640, tokens), tile(512, half)
    steps = half // cols
    out = jax.ShapeDtypeStruct((tokens, half), BF)
    weight = pl.BlockSpec((depth, cols), lambda j, i, c: (0, c[0] * steps + j))
    block = pl.BlockSpec((rows, cols), lambda j, i, c: (i, j))
    return pl.pallas_call(
        feed_half_kernel,
        out_shape=(out, out, out),
        grid_spec=pltpu.PrefetchScalarGridSpec(
            num_scalar_prefetch=1,
            grid=(steps, tokens // rows),
            in_specs=[
                pl.BlockSpec((rows, depth), lambda j, i, c: (i, 0)),
                weight,
                weight,
                block,
            ]
            + unread(deps),
            out_specs=(block, block, block),
        ),
        compiler_params=kernel_params(2),
        cost_estimate=spent(18),
        name="feed_half",
    )(core, normed, w_gate, w_up, grad_hidden, *deps)


def feed_own_kernel(pieces, chunks, gate_w, up_w, grad_hidden, *refs):
    normed = refs[:pieces]
    hidden, parts = refs[-chunks - 3], refs[-chunks - 2 : -2]
    rows, total = refs[-2:]
    step = pl.program_id(0)
    size = total.shape[0] // chunks

    @pl.when(step == 0)
    def _():
        rows[...] = join(normed)

    gate_now = gate_w[...]
    up_now = up_w[...]
    hidden[...], grad_gate, grad_up = swish_grads(
        contract(rows[...], gate_now, 1, 0),
        contract(rows[...], up_now, 1, 0),
        grad_hidden[...].astype(F32),
    )
    term = contract(grad_gate, gate_now, 1, 1) + contract(grad_up, up_now, 1, 1)

    @pl.when(step == 0)
    def _():
        total[...] = term

    @pl.when(step > 0)
    def _():
        total[...] += term

    @pl.when(step == pl.num_programs(0) - 1)
    def _():
        for k, part in enumerate(parts):
            part[...] = total[k * size : (k + 1) * size].astype(BF)


def feed_own(normed, w_gate, w_up, grad_hidden, chunks, deps=()):
    tokens, units = grad_hidden.shape
    depth = w_gate.shape[0]
    size = tokens // chunks
    cols = tile(512, units)
    weight = pl.BlockSpec((depth, cols), lambda j: (0, j))
    block = pl.BlockSpec((tokens, cols), lambda j: (0, j))
    rows = pl.BlockSpec((size, depth), lambda j: (0, 0))
    out = pl.pallas_call(
        functools.partial(feed_own_kernel, len(normed), chunks),
        out_shape=(jax.ShapeDtypeStruct((tokens, units), BF),)
        + (jax.ShapeDtypeStruct((size, depth), BF),) * chunks,
        grid=(units // cols,),
        in_specs=[weight, weight, block] + [whole_spec(n) for n in normed] + unread(deps),
        out_specs=(block,) + (rows,) * chunks,
        scratch_shapes=[pltpu.VMEM((tokens, depth), BF), pltpu.VMEM((tokens, depth), F32)],
        compiler_params=kernel_params(1),
        cost_estimate=spent(18),
        name="feed_own",
    )(w_gate, w_up, grad_hidden, *normed, *deps)
    return out[0], list(out[1:])


def down_kernel(hidden, weight, *refs):
    keep, send = refs[-2:]
    part = contract(hidden[...], weight[...], 1, 0).astype(BF)
    rows = keep.shape[0]
    keep[...] = part[:rows]
    send[...] = part[rows:]


def down_projection(hidden, w_down, deps=()):
    tokens, units = hidden.shape
    depth = w_down.shape[1]
    cols = tile(512, depth)
    half = jax.ShapeDtypeStruct((tokens // 2, depth), BF)
    block = pl.BlockSpec((tokens // 2, cols), lambda j: (0, j))
    return pl.pallas_call(
        down_kernel,
        out_shape=(half, half),
        grid=(depth // cols,),
        in_specs=[whole_spec(hidden), pl.BlockSpec((units, cols), lambda j: (0, j))]
        + unread(deps),
        out_specs=(block, block),
        compiler_params=kernel_params(1),
        cost_estimate=spent(7),
        name="down_projection",
    )(hidden, w_down, *deps)


def add_half_kernel(keep, came, *refs):
    total = keep[...].astype(F32) + came[...].astype(F32)
    first, second = refs[-2:]
    rows = first.shape[0]
    first[...] = total[:rows].astype(BF)
    second[...] = total[rows:].astype(BF)


def add_half(keep, came, deps=()):
    rows, depth = keep.shape
    half = jax.ShapeDtypeStruct((rows // 2, depth), BF)
    return pl.pallas_call(
        add_half_kernel,
        out_shape=(half, half),
        grid=(1,),
        in_specs=[whole_spec(keep), whole_spec(came)] + unread(deps),
        out_specs=(whole_spec(half), whole_spec(half)),
        compiler_params=kernel_params(1),
        cost_estimate=spent(1),
        name="add_half",
    )(keep, came, *deps)


STEPS = 4


def weight_grad_kernel(count, pieces, core, *refs):
    lefts, rights = refs[:count], refs[count : 2 * count]
    wide, lows = refs[-1 - pieces], refs[-pieces:]
    total = contract(lefts[0][...], rights[0][...], 0, 0)
    for left, right in zip(lefts[1:], rights[1:]):
        total = total + contract(left[...], right[...], 0, 0)
    wide[...] = total
    for k, low in enumerate(lows):

        @pl.when(pl.program_id(1) == k)
        def _():
            low[...] = total.astype(BF)


def weight_grad(core, lefts, rights, dim, pieces, deps=()):
    tokens, m = lefts[0].shape
    n = rights[0].shape[1]
    count = len(lefts)
    rows, cols = m // pieces, tile(1024, n)
    across = n // cols
    if dim == 0:
        full = (2 * m, n)
        place = lambda j, i, c: (c[0] * pieces + i, j)
    else:
        full = (m, 2 * n)
        place = lambda j, i, c: (i, c[0] * across + j)
    share = 1

    def piece(k):
        last = share - 1
        return pl.BlockSpec(
            (rows, cols), lambda j, i, c: (jnp.clip(i - k * share, 0, last), j)
        )

    out = pl.pallas_call(
        functools.partial(weight_grad_kernel, count, pieces),
        out_shape=(jax.ShapeDtypeStruct(full, F32),)
        + (jax.ShapeDtypeStruct((rows * share, n), BF),) * pieces,
        grid_spec=pltpu.PrefetchScalarGridSpec(
            num_scalar_prefetch=1,
            grid=(across, pieces),
            in_specs=[pl.BlockSpec((tokens, rows), lambda j, i, c: (0, i))] * count
            + [pl.BlockSpec((tokens, cols), lambda j, i, c: (0, j))] * count
            + unread(deps),
            out_specs=(pl.BlockSpec((rows, cols), place),)
            + tuple(piece(k) for k in range(pieces)),
        ),
        compiler_params=kernel_params(2),
        cost_estimate=spent(19),
        name="weight_grad",
    )(core, *lefts, *rights, *deps)
    return out[0], list(out[1:])


def pair_grad_kernel(count, core, *refs):
    lefts = [r[...] for r in refs[:count]]
    wides, lows = refs[-4:-2], refs[-2:]
    for k in range(2):
        rights = refs[count * (k + 1) : count * (k + 2)]
        total = contract(lefts[0], rights[0][...], 0, 0)
        for left, right in zip(lefts[1:], rights[1:]):
            total = total + contract(left, right[...], 0, 0)
        wides[k][...] = total
        lows[k][0] = total.astype(BF)


def pair_grad(core, lefts, first, second, deps=()):
    tokens, m = lefts[0].shape
    n = first[0].shape[1]
    count = len(lefts)
    rows = m // STEPS
    wide = jax.ShapeDtypeStruct((m, 2 * n), F32)
    low = jax.ShapeDtypeStruct((1, m, n), BF)
    place = pl.BlockSpec((rows, n), lambda i, c: (i, c[0]))
    here = pl.BlockSpec((1, rows, n), lambda i, c: (0, i, 0))
    out = pl.pallas_call(
        functools.partial(pair_grad_kernel, count),
        out_shape=(wide, wide, low, low),
        grid_spec=pltpu.PrefetchScalarGridSpec(
            num_scalar_prefetch=1,
            grid=(STEPS,),
            in_specs=[pl.BlockSpec((tokens, rows), lambda i, c: (0, i))] * count
            + [whole_spec(v) for v in (*first, *second)]
            + unread(deps),
            out_specs=(place, place, here, here),
        ),
        compiler_params=kernel_params(1),
        cost_estimate=spent(34),
        name="pair_grad",
    )(core, *lefts, *first, *second, *deps)
    return out


def left_product_kernel(count, left, *refs):
    right = join(refs[:count])
    refs[-1][...] = contract(left[...], right, 0, 0).astype(BF)


def left_product(left, pieces, deps=()):
    tokens, m = left.shape
    n = pieces[0].shape[1]
    rows, cols = tile(1024, m), tile(512, n)
    return pl.pallas_call(
        functools.partial(left_product_kernel, len(pieces)),
        out_shape=jax.ShapeDtypeStruct((m, n), BF),
        grid=(m // rows, n // cols),
        in_specs=[pl.BlockSpec((tokens, rows), lambda i, j: (0, i))]
        + [pl.BlockSpec((p.shape[0], cols), lambda i, j: (0, j)) for p in pieces]
        + unread(deps),
        out_specs=pl.BlockSpec((rows, cols), lambda i, j: (i, j)),
        compiler_params=kernel_params(2),
        cost_estimate=spent(1),
        name="left_product",
    )(left, *pieces, *deps)


def kv_product_kernel(left, right, *refs):
    gains, out = refs[:-1], refs[-1]
    width = right.shape[1]
    out[:width, :] = contract(right[...], left[...], 0, 0).astype(BF)
    total = sum_chunks(gains)
    out[width:, :] = jnp.concatenate([total, jnp.zeros(total.shape, F32)], axis=0).astype(BF)


def kv_product(left, right, gains, deps=()):
    tokens, m = left.shape
    width = right.shape[1]
    cols = tile(1024, m)

    def kernel(*refs):
        kv_product_kernel(*refs[: 2 + len(gains)], refs[-1])

    return pl.pallas_call(
        kernel,
        out_shape=jax.ShapeDtypeStruct((width + 16, m), BF),
        grid=(m // cols,),
        in_specs=[pl.BlockSpec((tokens, cols), lambda i: (0, i)), whole_spec(right)]
        + [pl.BlockSpec((8, cols), lambda i: (0, i))] * len(gains)
        + unread(deps),
        out_specs=pl.BlockSpec((width + 16, cols), lambda i: (0, i)),
        compiler_params=kernel_params(1),
        cost_estimate=spent(1),
        name="kv_product",
    )(left, right, *gains, *deps)


def mask_kernel(chunks, scalars, place, *refs):
    value = join(refs[:chunks]).astype(F32)
    refs[-1][...] = jnp.where(place[...] < scalars[1], value, 0.0).astype(BF)


def mask_padding(scalars, value, place, chunks, half, deps=()):
    span, depth = value.shape
    rows = span // 2
    first = half * chunks // 2
    out = jax.ShapeDtypeStruct((rows, depth), BF)
    return pl.pallas_call(
        functools.partial(mask_kernel, chunks // 2),
        out_shape=out,
        grid_spec=pltpu.PrefetchScalarGridSpec(
            num_scalar_prefetch=1,
            grid=(1,),
            in_specs=[pl.BlockSpec((rows, 1), lambda i, c: (half, 0))]
            + [chunk_spec(value, chunks, k) for k in range(first, first + chunks // 2)]
            + unread(deps),
            out_specs=whole_spec(out),
        ),
        compiler_params=kernel_params(1),
        cost_estimate=spent(4),
        name="mask_padding",
    )(scalars, place, *[value] * (chunks // 2), *deps)


def corner_kernel(value, out):
    out[...] = value[...]


def corner(value):
    return pl.pallas_call(
        corner_kernel,
        out_shape=jax.ShapeDtypeStruct((16, 128), value.dtype),
        grid=(1,),
        in_specs=[pl.BlockSpec((16, 128), lambda i: (0, 0))],
        out_specs=pl.BlockSpec((16, 128), lambda i: (0, 0)),
        compiler_params=kernel_params(1),
        cost_estimate=spent(5),
        name="corner",
    )(value)


def fill_other_kernel(pieces, core, *refs):
    step = pl.program_id(0)
    for k in range(pieces):

        @pl.when(step // (STEPS // pieces) == k)
        def _():
            refs[-1][...] = refs[k][...].astype(F32).reshape(refs[-1].shape)


def fill_other(core, others, index, held, dim, deps=()):
    pieces = len(others)
    share = STEPS // pieces
    rows, n = others[0].shape[1] // share, others[0].shape[2]
    if dim == 0:
        place = lambda i, c: ((1 - c[0]) * STEPS + i, 0)
    else:
        place = lambda i, c: (i, 1 - c[0])

    def piece(k):
        last = share - 1
        return pl.BlockSpec(
            (1, rows, n), lambda i, c: (index, jnp.clip(i - k * share, 0, last), 0)
        )

    return pl.pallas_call(
        functools.partial(fill_other_kernel, pieces),
        out_shape=jax.ShapeDtypeStruct(held.shape, F32),
        grid_spec=pltpu.PrefetchScalarGridSpec(
            num_scalar_prefetch=1,
            grid=(STEPS,),
            in_specs=[piece(k) for k in range(pieces)]
            + [pl.BlockSpec(memory_space=pl.ANY)]
            + unread(deps),
            out_specs=pl.BlockSpec((rows, n), place),
        ),
        input_output_aliases={1 + pieces: 0},
        compiler_params=kernel_params(1),
        cost_estimate=spent(87),
        name="fill_other",
    )(core, *others, held, *deps)


def rotate_block(values, cosine, sine):
    width = values.shape[1]
    column = lax.broadcasted_iota(jnp.int32, values.shape, 1)
    other = jnp.where(
        column % HEAD_SIZE < HEAD_SIZE // 2,
        pltpu.roll(values, width - HEAD_SIZE // 2, 1),
        pltpu.roll(values, HEAD_SIZE // 2, 1),
    )
    return values * cosine + other * sine


def pack_rotated(keys, values, cosine, sine):
    width = keys.shape[1]
    if width % 128 == 0:
        turned = [
            rotate_block(keys[:, i : i + 128], cosine, sine) for i in range(0, width, 128)
        ]
        return jnp.concatenate(turned + [values], axis=1)
    both = jnp.concatenate([keys, values], axis=1)
    column = lax.broadcasted_iota(jnp.int32, both.shape, 1)
    return jnp.where(column < width, rotate_block(both, cosine, sine), both)


def chunk_spec(array, chunks, k):
    block = (array.shape[0] // chunks, array.shape[1])
    return pl.BlockSpec(block, lambda *a: (a[-1][0] ^ k, 0))


def project_kv_kernel(chunks, waits, me, *refs):
    gain, key_w, value_w, cosine, sine = refs[chunks : chunks + 5]
    normed, inverse, packed = refs[-3:]
    stream = join(refs[:chunks]).astype(F32)
    scale = lax.rsqrt(jnp.mean(stream * stream, axis=1, keepdims=True) + EPSILON)
    low = (stream * scale * gain[...]).astype(BF)
    normed[...] = low
    inverse[...] = jnp.broadcast_to(scale, inverse.shape)
    packed[...] = pack_rotated(
        contract(low, key_w[...], 1, 0), contract(low, value_w[...], 1, 0), cosine[...], sine[...]
    ).astype(BF)


def project_kv(me, x, gain, key_matrix, value_matrix, cosine, sine, chunks, deps=()):
    span, depth = x.shape
    args = (gain, key_matrix, value_matrix, cosine, sine)
    outs = (
        jax.ShapeDtypeStruct((span, depth), BF),
        jax.ShapeDtypeStruct((span, 128), F32),
        jax.ShapeDtypeStruct((span, 2 * key_matrix.shape[1]), BF),
    )
    return pl.pallas_call(
        functools.partial(project_kv_kernel, chunks, len(deps)),
        out_shape=outs,
        grid_spec=pltpu.PrefetchScalarGridSpec(
            num_scalar_prefetch=1,
            grid=(1,),
            in_specs=[chunk_spec(x, chunks, k) for k in range(chunks)]
            + [whole_spec(a) for a in args]
            + unread(deps),
            out_specs=tuple(whole_spec(a) for a in outs),
        ),
        compiler_params=kernel_params(1),
        cost_estimate=spent(4),
        name="project_kv",
    )(me, *[x] * chunks, *args, *deps)


def project_query_kernel(normed, weight, cosine, sine, *refs):
    out = refs[-1]
    lin = contract(normed[...], weight[...], 1, 0)
    for i in range(0, lin.shape[1], 128):
        turned = rotate_block(lin[:, i : i + 128], cosine[...], sine[...])
        out[:, i : i + 128] = (turned * HEAD_SIZE**-0.5).astype(BF)


def project_query(normed, w_query, cosine, sine, deps=()):
    span, depth = normed.shape
    width = w_query.shape[1]
    cols = 256
    return pl.pallas_call(
        project_query_kernel,
        out_shape=jax.ShapeDtypeStruct((span, width), BF),
        grid=(width // cols,),
        in_specs=[
            whole_spec(normed),
            pl.BlockSpec((depth, cols), lambda j: (0, j)),
            whole_spec(cosine),
            whole_spec(sine),
        ]
        + unread(deps),
        out_specs=pl.BlockSpec((span, cols), lambda j: (0, j)),
        compiler_params=kernel_params(1),
        cost_estimate=spent(4),
        name="project_query",
    )(normed, w_query, cosine, sine, *deps)


def head_columns(array, index):
    return array[:, index * HEAD_SIZE : (index + 1) * HEAD_SIZE]


def stack_heads(array, heads):
    return jnp.concatenate([head_columns(array, h) for h in heads], axis=0)


def store_heads(out, turned, first, span, finish):
    for i in range(0, turned.shape[1] // span, 2):
        pair = jnp.concatenate(
            [turned[:, (i + e) * span : (i + e + 1) * span] for e in range(2)], axis=0
        )
        at = (first + i) * HEAD_SIZE
        out[:, at : at + 128] = finish(jnp.transpose(pair)).astype(BF)


def attend_kernel(blocks, chunks, shift, query, place, place_row, begin_row, w_output, *refs):
    packed = refs[:blocks]
    attended, stats, *parts = refs[-2 - chunks :]
    span, width = query.shape
    heads_kv = packed[0].shape[1] // (2 * HEAD_SIZE)
    group = width // HEAD_SIZE // heads_kv
    last = jnp.concatenate([place_row[...]] * group, axis=1)
    first = jnp.concatenate([begin_row[...]] * group, axis=1)
    for g in range(heads_kv):
        q = stack_heads(query, range(g * group, (g + 1) * group))
        top = total = mixed = None
        for j in range(blocks):
            keys = head_columns(packed[j], g)
            values = head_columns(packed[j], heads_kv + g)
            key_place = place[...] + shift[j]
            allowed = (key_place >= first) & (key_place <= last)
            masked = jnp.where(allowed, contract(keys, q, 1, 1), -1e30)
            peak = jnp.max(masked, axis=0, keepdims=True)
            peak = peak if j == 0 else jnp.maximum(top, peak)
            terms = jnp.exp(masked - peak)
            amount = jnp.sum(terms, axis=0, keepdims=True)
            term = contract(values, terms.astype(BF), 0, 0)
            if j == 0:
                total, mixed = amount, term
            else:
                fade = jnp.exp(top - peak)
                total, mixed = total * fade + amount, mixed * fade + term
            top = peak
        stats[g : g + 1, :] = top + jnp.log(total)
        store_heads(attended, mixed * (1.0 / total), g * group, span, lambda v: v)
    part = contract(attended[...], w_output[...], 1, 0)
    chunk = span // len(parts)
    for k, out in enumerate(parts):
        out[...] = part[k * chunk : (k + 1) * chunk].astype(BF)


def attend(shift, query, packed, places, w_output, chunks, deps=()):
    span, width = query.shape
    depth = w_output.shape[1]
    blocks = len(packed)
    heads_kv = packed[0].shape[1] // (2 * HEAD_SIZE)
    args = (
        query,
        *places,
        w_output,
        *packed,
    )
    outs = (
        jax.ShapeDtypeStruct((span, width), BF),
        jax.ShapeDtypeStruct((heads_kv, width // HEAD_SIZE // heads_kv * span), F32),
    )
    outs += (jax.ShapeDtypeStruct((span // chunks, depth), BF),) * chunks
    out = pl.pallas_call(
        functools.partial(attend_kernel, blocks, chunks),
        out_shape=outs,
        grid_spec=pltpu.PrefetchScalarGridSpec(
            num_scalar_prefetch=1,
            grid=(1,),
            in_specs=[whole_spec(a) for a in args] + unread(deps),
            out_specs=tuple(whole_spec(a) for a in outs),
        ),
        compiler_params=kernel_params(1),
        cost_estimate=spent(11),
        name="attend",
    )(shift, *args, *deps)
    return out[0], out[1], list(out[2:])


def sum_chunks(refs):
    total = refs[0][...].astype(F32)
    for ref in refs[1:]:
        total = total + ref[...].astype(F32)
    return total


def middle_kernel(count, me, x, gain, *refs):
    chunks, (middle, inverse, normed) = refs[:count], refs[-3:]
    stream = x[...].astype(F32) + sum_chunks(chunks)
    scale = lax.rsqrt(jnp.mean(stream * stream, axis=1, keepdims=True) + EPSILON)
    middle[...] = stream
    inverse[...] = jnp.broadcast_to(scale, inverse.shape)
    normed[...] = (stream * scale * gain[...]).astype(BF)


def middle_norm(me, x, gain, chunks, deps=()):
    rows, depth = chunks[0].shape
    outs = (
        jax.ShapeDtypeStruct((rows, depth), F32),
        jax.ShapeDtypeStruct((rows, 128), F32),
        jax.ShapeDtypeStruct((rows, depth), BF),
    )
    return pl.pallas_call(
        functools.partial(middle_kernel, len(chunks)),
        out_shape=outs,
        grid_spec=pltpu.PrefetchScalarGridSpec(
            num_scalar_prefetch=1,
            grid=(1,),
            in_specs=[chunk_spec(x, len(chunks), 0)]
            + [whole_spec(a) for a in (gain, *chunks)]
            + unread(deps),
            out_specs=tuple(whole_spec(a) for a in outs),
        ),
        compiler_params=kernel_params(1),
        cost_estimate=spent(120),
        name="middle_norm",
    )(me, x, gain, *chunks, *deps)


def halves_kernel(count, *refs):
    half = count // 2
    refs[-2][...] = join(refs[:half])
    refs[-1][...] = join(refs[half:count])


def join_halves(chunks, deps=()):
    rows, depth = chunks[0].shape
    outs = (jax.ShapeDtypeStruct((rows * len(chunks) // 2, depth), BF),) * 2
    return pl.pallas_call(
        functools.partial(halves_kernel, len(chunks)),
        out_shape=outs,
        grid=(1,),
        in_specs=[whole_spec(a) for a in chunks] + unread(deps),
        out_specs=tuple(whole_spec(a) for a in outs),
        compiler_params=kernel_params(1),
        cost_estimate=spent(2),
        name="join_halves",
    )(*chunks, *deps)


def norm_gradient(grad, rows, scale, gain):
    scaled = grad * gain
    product = jnp.mean(scaled * rows, axis=1, keepdims=True)
    gain_grad = jnp.sum(grad * rows * scale, axis=0, keepdims=True)
    return scale * scaled - rows * (scale * scale * scale * product), gain_grad


def norm_back_kernel(count, upstream, middle, inverse, gain, *refs):
    chunks, (wide, low, gain_grad) = refs[:count], refs[-3:]
    grad, gain_grad[...] = norm_gradient(
        sum_chunks(chunks), middle[...], inverse[:, :1], gain[...]
    )
    total = upstream[...].astype(F32) + grad
    wide[...] = total
    low[...] = total.astype(BF)


def norm_back(upstream, middle, inverse, gain, chunks, deps=()):
    rows, depth = middle.shape
    args = (middle, inverse, gain, *chunks)
    outs = (
        jax.ShapeDtypeStruct((rows, depth), F32),
        jax.ShapeDtypeStruct((rows, depth), BF),
        jax.ShapeDtypeStruct((1, depth), F32),
    )
    return pl.pallas_call(
        functools.partial(norm_back_kernel, len(chunks)),
        out_shape=outs,
        grid=(1,),
        in_specs=[pl.BlockSpec((rows, depth), lambda i: (0, 0))]
        + [whole_spec(a) for a in args]
        + unread(deps),
        out_specs=tuple(whole_spec(a) for a in outs),
        compiler_params=kernel_params(1),
        cost_estimate=spent(3),
        name="norm_back",
    )(upstream, *args, *deps)


def finish_kernel(count, me, x, inverse, gain, grad_middle, block, *refs):
    grad, _ = norm_gradient(
        sum_chunks(refs[:count]), x[...].astype(F32), inverse[:, :1], gain[...]
    )
    refs[-1][...] = jnp.concatenate([grad_middle[...] + grad, block[...]], axis=0).astype(BF)


def finish(me, x, inverse, gain, grad_middle, block, chunks, deps=()):
    rows, depth = grad_middle.shape
    args = (gain, grad_middle, block, *chunks)
    outs = jax.ShapeDtypeStruct((2 * rows, depth), BF)
    return pl.pallas_call(
        functools.partial(finish_kernel, len(chunks)),
        out_shape=outs,
        grid_spec=pltpu.PrefetchScalarGridSpec(
            num_scalar_prefetch=1,
            grid=(1,),
            in_specs=[
                chunk_spec(x, len(chunks), 0),
                pl.BlockSpec((rows, 128), lambda i, c: (0, 0)),
            ]
            + [whole_spec(a) for a in args]
            + unread(deps),
            out_specs=whole_spec(outs),
        ),
        compiler_params=kernel_params(1),
        cost_estimate=spent(3),
        name="finish",
    )(me, x, inverse, *args, *deps)


def add_kernel(count, *refs):
    refs[-1][...] = sum_chunks(refs[:count]).astype(refs[-1].dtype)


def add_up(arrays, dtype, deps=()):
    out = jax.ShapeDtypeStruct(arrays[0].shape, dtype)
    return pl.pallas_call(
        functools.partial(add_kernel, len(arrays)),
        out_shape=out,
        grid=(1,),
        in_specs=[whole_spec(a) for a in arrays] + unread(deps),
        out_specs=whole_spec(out),
        compiler_params=kernel_params(1),
        cost_estimate=spent(2),
        name="add_up",
    )(*arrays, *deps)


def restore_kernel(count, me, *refs):
    step = pl.program_id(0)
    for k in range(count):

        @pl.when(step == k)
        def _():
            rows = refs[k].shape[0] // 2
            refs[-2][...] = refs[k][:rows]
            refs[-1][...] = refs[k][rows:]


def restore(me, pieces, deps=()):
    count = len(pieces)
    rows, depth = pieces[0].shape[0] // 2, pieces[0].shape[1]
    if rows % 16:
        halves = [[p[:rows] for p in pieces], [p[rows:] for p in pieces]]
        return [reorder(jnp.concatenate(h, axis=0), "tensor") for h in halves]
    out = jax.ShapeDtypeStruct((count * rows, depth), BF)
    place = pl.BlockSpec((rows, depth), lambda i, c: (c[0] ^ i, 0))
    return pl.pallas_call(
        functools.partial(restore_kernel, count),
        out_shape=(out, out),
        grid_spec=pltpu.PrefetchScalarGridSpec(
            num_scalar_prefetch=1,
            grid=(count,),
            in_specs=[whole_spec(p) for p in pieces] + unread(deps),
            out_specs=(place, place),
        ),
        compiler_params=kernel_params(1),
        cost_estimate=spent(87),
        name="restore",
    )(me, *pieces, *deps)


def widen(wo, wq, wkv, width, deps=()):
    steps = 4
    depth = wq.shape[0]
    shapes = [wo.shape, wq.shape, (depth, width), (depth, width)]

    def spec(shape):
        return pl.BlockSpec((shape[0] // steps, shape[1]), lambda i: (i, 0))

    def kernel(wo, wq, wkv, *refs):
        wo_out, wq_out, wk_out, wv_out, gains = refs[-5:]
        wo_out[...] = wo[...].astype(F32)
        wq_out[...] = wq[...].astype(F32)
        turned = jnp.transpose(wkv[: 2 * width, :].astype(F32))
        wk_out[...] = turned[:, :width]
        wv_out[...] = turned[:, width:]
        gains[...] = wkv[2 * width :, :].astype(F32)

    return pl.pallas_call(
        kernel,
        out_shape=tuple(jax.ShapeDtypeStruct(v, F32) for v in [*shapes, (16, depth)]),
        grid=(steps,),
        in_specs=[
            spec(wo.shape),
            spec(wq.shape),
            pl.BlockSpec((wkv.shape[0], depth // steps), lambda i: (0, i)),
        ]
        + unread(deps),
        out_specs=tuple(spec(v) for v in shapes)
        + (pl.BlockSpec((16, depth // steps), lambda i: (0, i)),),
        compiler_params=kernel_params(1),
        cost_estimate=spent(8),
        name="widen",
    )(wo, wq, wkv, *deps)


def attend_back_kernel(blocks, count, shift, query, attended, stats, place, place_row, begin_row,
                       cosine, sine, w_output, *refs):
    packed = refs[:blocks]
    chunks = refs[blocks : blocks + count]
    grad_query = refs[-1 - blocks]
    terms = refs[-blocks:]
    span, width = query.shape
    heads_kv = packed[0].shape[1] // (2 * HEAD_SIZE)
    group = width // HEAD_SIZE // heads_kv
    grad_middle = join(chunks)
    grad_attended = contract(grad_middle, w_output[...], 1, 1).astype(BF)
    last = jnp.concatenate([place_row[...]] * group, axis=1)
    first = jnp.concatenate([begin_row[...]] * group, axis=1)
    key_terms = [[] for _ in range(blocks)]
    value_terms = [[] for _ in range(blocks)]
    for g in range(heads_kv):
        mine = range(g * group, (g + 1) * group)
        q = stack_heads(query, mine)
        grad = stack_heads(grad_attended, mine)
        norm = stats[g : g + 1, :]
        inner = lax.dot_general(
            jnp.ones((8, HEAD_SIZE), F32),
            grad.astype(F32) * stack_heads(attended, mine).astype(F32),
            (((1,), (1,)), ((), ())),
            preferred_element_type=F32,
            precision=lax.Precision.HIGHEST,
        )[:1]
        total = None
        for j in range(blocks):
            keys = head_columns(packed[j], g)
            values = head_columns(packed[j], heads_kv + g)
            key_place = place[...] + shift[j]
            allowed = (key_place >= first) & (key_place <= last)
            scores = contract(keys, q, 1, 1)
            probs = jnp.exp(jnp.where(allowed, scores - norm, -1e30))
            grad_scores = (probs * (contract(values, grad, 1, 1) - inner)).astype(BF)
            value_terms[j].append(contract(probs.astype(BF), grad, 1, 0))
            key_terms[j].append(contract(grad_scores, q, 1, 0))
            term = contract(keys, grad_scores, 0, 0)
            total = term if total is None else total + term
        store_heads(
            grad_query,
            total,
            g * group,
            span,
            lambda v: rotate_block(v * HEAD_SIZE**-0.5, cosine[...], -sine[...]),
        )
    for j in range(blocks):
        terms[j][...] = jnp.concatenate(key_terms[j] + value_terms[j], axis=1).astype(BF)


def attend_back(shift, query, attended, stats, packed, places, cosine, sine, w_output, chunks,
                deps=()):
    span, width = query.shape
    blocks = len(packed)
    args = (
        query,
        attended,
        stats,
        *places,
        cosine,
        sine,
        w_output,
        *packed,
        *chunks,
    )
    outs = (jax.ShapeDtypeStruct((span, width), BF),)
    outs += (jax.ShapeDtypeStruct(packed[0].shape, BF),) * blocks
    out = pl.pallas_call(
        functools.partial(attend_back_kernel, blocks, len(chunks)),
        out_shape=outs,
        grid_spec=pltpu.PrefetchScalarGridSpec(
            num_scalar_prefetch=1,
            grid=(1,),
            in_specs=[whole_spec(a) for a in args] + unread(deps),
            out_specs=tuple(whole_spec(a) for a in outs),
        ),
        compiler_params=kernel_params(1),
        cost_estimate=spent(16),
        name="attend_back",
    )(shift, *args, *deps)
    return out[0], list(out[1:])


def input_back_kernel(
    count, chunks, me, grad_query, w_query, key_w, value_w, cosine, sine, inverse, gain_two, *refs
):
    terms, rows = refs[:count], refs[count : count + chunks]
    lin, gains, *parts = refs[-2 - chunks :]
    normed = join(rows).astype(F32) * inverse[:, :1]
    width = key_w.shape[1]
    total = sum_chunks(terms)
    low = pack_rotated(total[:, :width], total[:, width:], cosine[...], -sine[...]).astype(BF)
    lin[...] = low
    part = contract(grad_query[...], w_query[...], 1, 1)
    part = part + contract(low[:, :width], key_w[...], 1, 1)
    part = part + contract(low[:, width:], value_w[...], 1, 1)
    rows = part.shape[0] // chunks
    for k, out in enumerate(parts):
        out[...] = part[k * rows : (k + 1) * rows].astype(BF)
    gain_one = jnp.sum(part * normed, axis=0, keepdims=True)
    empty = jnp.zeros((6, part.shape[1]), F32)
    gains[...] = jnp.concatenate([gain_one, gain_two[...], empty], axis=0)


def input_back(
    me,
    grad_query,
    w_query,
    key_matrix,
    value_matrix,
    cosine,
    sine,
    inverse,
    x,
    gain_two,
    terms,
    chunks,
    deps=(),
):
    span = grad_query.shape[0]
    depth = w_query.shape[0]
    args = (grad_query, w_query, key_matrix, value_matrix, cosine, sine, inverse, gain_two)
    args += tuple(terms)
    outs = (
        jax.ShapeDtypeStruct(terms[0].shape, BF),
        jax.ShapeDtypeStruct((8, depth), F32),
    )
    outs += (jax.ShapeDtypeStruct((span // chunks, depth), BF),) * chunks
    out = pl.pallas_call(
        functools.partial(input_back_kernel, len(terms), chunks),
        out_shape=outs,
        grid_spec=pltpu.PrefetchScalarGridSpec(
            num_scalar_prefetch=1,
            grid=(1,),
            in_specs=[whole_spec(a) for a in args]
            + [chunk_spec(x, chunks, k) for k in range(chunks)]
            + unread(deps),
            out_specs=tuple(whole_spec(a) for a in outs),
        ),
        compiler_params=kernel_params(1),
        cost_estimate=spent(1),
        name="input_back",
    )(me, *args, *[x] * chunks, *deps)
    return out[0], out[1], list(out[2:])


def rope_tables(positions):
    expo = np.arange(HEAD_SIZE // 2, dtype=np.float64) * 2.0 / HEAD_SIZE
    inverse = 1.0 / 500000.0**expo
    wavelength = 2.0 * np.pi / inverse
    smooth = (8192.0 / wavelength - 1.0) / 3.0
    middle = (1.0 - smooth) * inverse / 32.0 + smooth * inverse
    scaled = np.where(
        wavelength < 2048.0, inverse, np.where(wavelength > 8192.0, inverse / 32.0, middle)
    )
    scaled = jnp.asarray(np.tile(scaled, 4)[None, :].astype(np.float32))
    sign = jnp.asarray(np.tile(np.repeat([-1.0, 1.0], HEAD_SIZE // 2), 2)[None, :].astype(np.float32))
    angles = positions.astype(F32)[:, None] * scaled
    return jnp.cos(angles), jnp.sin(angles) * sign


def flip(value, axis, mask):
    return lax.ppermute(value, axis, [(i, i ^ mask) for i in range(lax.axis_size(axis))])


def reorder(value, axis):
    n = lax.axis_size(axis)
    me = lax.axis_index(axis)
    chunk = value.shape[0] // n
    return jnp.concatenate(
        [lax.dynamic_slice_in_dim(value, (me ^ k) * chunk, chunk, 0) for k in range(n)], axis=0
    )


def exchange(chunks, axis):
    return chunks[:1] + [flip(chunks[k], axis, k) for k in reversed(range(1, len(chunks)))]


def spread(chunk, axis):
    return [chunk] + [flip(chunk, axis, k) for k in range(1, lax.axis_size(axis))]


def gather_halves(first, second):
    return [
        lax.all_gather(first, ("rows", "seq"), axis=0, tiled=True),
        lax.all_gather(second, ("seq", "rows"), axis=0, tiled=True),
    ]


def per_device(
    activations,
    doc_lengths,
    w_query,
    key_matrix,
    value_matrix,
    w_output,
    w_gate,
    w_up,
    w_down,
    gain_attn,
    gain_ffn,
    cotangent,
):
    span = activations.shape[1]
    blocks = lax.axis_size("seq")
    chunks = lax.axis_size("tensor")
    chunk = span // chunks
    core = lax.axis_index("rows").astype(jnp.int32).reshape(1)
    block_here = lax.axis_index("seq")
    gain_attn = gain_attn.reshape(1, -1)
    gain_ffn = gain_ffn.reshape(1, -1)
    stream, cotangent = activations[0], cotangent[0]
    me = lax.axis_index("tensor").astype(jnp.int32)
    token = jnp.arange(span, dtype=jnp.int32)
    place = block_here * span + (me ^ (token // chunk)) * chunk + token % chunk
    if chunk % 16:
        stream, cotangent = reorder(stream, "tensor"), reorder(cotangent, "tensor")
        me = jnp.zeros_like(me)
    ends = [doc_lengths[0, 0]]
    for d in range(1, DOCS):
        ends.append(ends[-1] + doc_lengths[0, d])
    begin = jnp.zeros_like(place)
    for end in ends:
        begin = jnp.where(place >= end, end, begin)
    cosine, sine = rope_tables(place - begin)
    shift = jnp.stack([((block_here ^ j) - block_here) * span for j in range(blocks)])
    shift = shift.astype(jnp.int32)
    scalars = jnp.stack([me, ends[-1].astype(jnp.int32)])
    places = (place.reshape(span, 1), place.reshape(1, span), begin.reshape(1, span))

    normed_one, inverse_one, packed = project_kv(
        scalars, stream, gain_attn, key_matrix, value_matrix, cosine, sine, chunks, (shift, *places)
    )
    packed = spread(packed, "seq")
    query = project_query(normed_one, w_query, cosine, sine)
    upstream = [mask_padding(scalars, cotangent, places[0], chunks, 0, (query, *packed))]
    upstream_all = [lax.all_gather(upstream[0], ("rows", "seq"), axis=0, tiled=True)]
    attended, stats, parts = attend(
        shift, query, packed, places, w_output, chunks, (upstream[0],)
    )
    upstream.append(mask_padding(scalars, cotangent, places[0], chunks, 1, (parts[0],)))
    upstream_all.append(lax.all_gather(upstream[1], ("seq", "rows"), axis=0, tiled=True))

    sent = exchange(parts, "tensor")
    grad_hidden = grad_hidden_of(core, upstream, w_down, 1, (parts[0],))
    middle, inverse_two, normed = middle_norm(scalars, stream, gain_ffn, sent, (grad_hidden,))

    grad_hidden_first = grad_hidden_of(core, upstream_all[:1], w_down, 2, (middle,))
    normed = join_halves(spread(normed, "tensor"), (grad_hidden_first,))
    normed_all = gather_halves(*normed)
    hidden, parts = feed_own(normed, w_gate, w_up, grad_hidden, chunks)

    sent = exchange(parts, "tensor")
    grad_hidden_second = grad_hidden_of(core, upstream_all[1:], w_down, 2, (parts[0],))
    grad_middle, grad_middle_low, gain_two = norm_back(
        upstream[0], middle, inverse_two, gain_ffn, sent, (grad_hidden_second,)
    )
    grad_middle_all = spread(grad_middle_low, "tensor")
    feed_first = feed_half(
        core, normed_all[0], w_gate, w_up, grad_hidden_first, (grad_middle,)
    )
    down_parts = down_projection(hidden, w_down, (feed_first[0],))
    grad_query, kv_terms = attend_back(
        shift,
        query,
        attended,
        stats,
        packed,
        places,
        cosine,
        sine,
        w_output,
        grad_middle_all,
        (corner(down_parts[0]),),
    )
    mask = chunks // 2
    down_came = flip(down_parts[1], "tensor", mask)

    kv_sent = exchange(kv_terms, "seq")
    wq_part = left_product(normed_one, [grad_query])
    grad_kv, gains, parts = input_back(
        scalars,
        grad_query,
        w_query,
        key_matrix,
        value_matrix,
        cosine,
        sine,
        inverse_one,
        stream,
        gain_two,
        kv_sent,
        chunks,
        (wq_part, normed_all[1]),
    )

    gains = spread(gains, "tensor")
    wo_part = left_product(attended, grad_middle_all, (parts[0],))
    wkv_part = kv_product(normed_one, grad_kv, gains, (wo_part,))
    sent = exchange(parts, "tensor")
    grad_wo, grad_wq, grad_wkv = lax.psum((wo_part, wq_part, wkv_part), ("rows", "seq"))
    keep, send = add_half(down_parts[0], down_came, (wkv_part,))
    while mask > 2:
        mask //= 2
        keep, send = add_half(keep, flip(send, "tensor", mask))
    feed_second = feed_half(
        core, normed_all[1], w_gate, w_up, grad_hidden_second, (keep,)
    )
    hidden_all, grad_gate_all, grad_up_all = zip(feed_first, feed_second)
    grad_down, low = weight_grad(core, hidden_all, upstream_all, 0, 2)
    down_other = [flip(v[None], "rows", 1) for v in low]
    block_chunk = add_up(
        [middle, keep, flip(send, "tensor", mask // 2)], F32, (grad_down,)
    )
    both = finish(
        scalars, stream, inverse_one, gain_attn, grad_middle, block_chunk, sent
    )
    both_all = spread(both, "tensor")
    grad_gate_w, grad_up_w, *low = pair_grad(
        core, normed_all, grad_gate_all, grad_up_all, (both,)
    )
    gate_other, up_other = [flip(v, "rows", 1) for v in low]
    grad_down = fill_other(core, down_other, 0, grad_down, 0, (grad_up_w,))
    grad_gate_w = fill_other(core, [gate_other], 0, grad_gate_w, 1, (grad_down,))
    grad_wo, grad_wq, grad_wk, grad_wv, gains = widen(
        grad_wo, grad_wq, grad_wkv, key_matrix.shape[1], (grad_gate_w,)
    )
    grad_input, block_output = restore(scalars, both_all, (grad_wo,))
    grad_up_w = fill_other(core, [up_other], 0, grad_up_w, 1, (grad_input,))
    return (
        block_output[None],
        grad_input[None],
        grad_wq,
        grad_wk,
        grad_wv,
        grad_wo,
        grad_gate_w,
        grad_up_w,
        grad_down,
        gains[0],
        gains[1],
    )


def solution(mesh):
    placed = (
        P("rows", "seq", None),
        P("rows", None),
        P(None, "tensor"),
        P(None, "tensor"),
        P(None, "tensor"),
        P("tensor", None),
        P(None, "tensor"),
        P(None, "tensor"),
        P("tensor", None),
        P(),
        P(),
        P("rows", "seq", None),
    )
    return jax.shard_map(
        per_device,
        mesh=mesh,
        in_specs=placed,
        out_specs=(
            P("rows", "seq", None),
            P("rows", "seq", None),
            P(None, "tensor"),
            P(None, "tensor"),
            P(None, "tensor"),
            P("tensor", None),
            P(None, "tensor"),
            P(None, "tensor"),
            P("tensor", None),
            P(),
            P(),
        ),
        check_vma=False,
    )
```

```python
import functools

import jax
import jax.numpy as jnp
from jax import lax
from jax.experimental import pallas as pl
from jax.experimental.pallas import tpu as pltpu
import numpy as np
from jax.sharding import PartitionSpec as P

HEAD_SIZE = 64
DOCS = 4
EPSILON = 1e-05
BF = jnp.bfloat16
F32 = jnp.float32


MIB = 1 << 20


def kernel_params(dims, mib=63):
    return pltpu.CompilerParams(
        vmem_limit_bytes=mib * MIB, dimension_semantics=("arbitrary",) * dims
    )


def contract(a, b, dim_a, dim_b):
    return lax.dot_general(
        a, b, (((dim_a,), (dim_b,)), ((), ())), preferred_element_type=F32
    )


def tile(limit, size):
    while size > limit and size % 2 == 0:
        size //= 2
    return size


SMALL = pl.CostEstimate(flops=1, bytes_accessed=1, transcendentals=0)


def spent(us):
    return pl.CostEstimate(flops=us * 10**9, bytes_accessed=1, transcendentals=0)


def whole_spec(array):
    shape = array.shape
    return pl.BlockSpec(shape, lambda *_: (0,) * len(shape))


def join(refs):
    if refs[0].shape[0] % 16 == 0:
        return jnp.concatenate([r[...] for r in refs], axis=0)
    return jnp.concatenate([r[...].astype(F32) for r in refs], axis=0).astype(refs[0].dtype)


def unread(deps):
    return [pl.BlockSpec(memory_space=pl.ANY)] * len(deps)


def times_transposed_kernel(count, core, weight, *refs):
    refs[-1][...] = contract(join(refs[:count]), weight[...], 1, 1).astype(BF)


def grad_hidden_of(core, pieces, w_down, shares, deps=()):
    count = len(pieces)
    tokens, depth = pieces[0].shape
    units = w_down.shape[0] // shares
    rows, cols = tile(640, tokens), tile(1024 // (3 - shares), units)
    steps = units // cols
    offset = steps * (shares - 1)
    return pl.pallas_call(
        functools.partial(times_transposed_kernel, count),
        out_shape=jax.ShapeDtypeStruct((count * tokens, units), BF),
        grid_spec=pltpu.PrefetchScalarGridSpec(
            num_scalar_prefetch=1,
            grid=(steps, tokens // rows),
            in_specs=[pl.BlockSpec((cols, depth), lambda j, i, c: (c[0] * offset + j, 0))]
            + [pl.BlockSpec((rows, depth), lambda j, i, c: (i, 0))] * count
            + unread(deps),
            out_specs=pl.BlockSpec((count * rows, cols), lambda j, i, c: (i, j)),
        ),
        compiler_params=kernel_params(2),
        cost_estimate=spent(10),
        name="grad_hidden_of",
    )(core, w_down, *pieces, *deps)


def swish_grads(gate, up_proj, grad_hidden):
    sigmoid = 1.0 / (1.0 + jnp.exp(-gate))
    activated = gate * sigmoid
    hidden = (activated * up_proj).astype(BF)
    grad_gate = (grad_hidden * up_proj * (sigmoid * (1.0 + gate * (1.0 - sigmoid)))).astype(BF)
    grad_up = (grad_hidden * activated).astype(BF)
    return hidden, grad_gate, grad_up


def feed_half_kernel(core, normed, gate_w, up_w, grad_hidden, *refs):
    hidden, grad_gate, grad_up = refs[-3:]
    rows = normed[...]
    hidden[...], grad_gate[...], grad_up[...] = swish_grads(
        contract(rows, gate_w[...], 1, 0),
        contract(rows, up_w[...], 1, 0),
        grad_hidden[...].astype(F32),
    )


def feed_half(core, normed, w_gate, w_up, grad_hidden, deps=()):
    tokens, depth = normed.shape
    half = w_gate.shape[1] // 2
    rows, cols = tile(640, tokens), tile(512, half)
    steps = half // cols
    out = jax.ShapeDtypeStruct((tokens, half), BF)
    weight = pl.BlockSpec((depth, cols), lambda j, i, c: (0, c[0] * steps + j))
    block = pl.BlockSpec((rows, cols), lambda j, i, c: (i, j))
    return pl.pallas_call(
        feed_half_kernel,
        out_shape=(out, out, out),
        grid_spec=pltpu.PrefetchScalarGridSpec(
            num_scalar_prefetch=1,
            grid=(steps, tokens // rows),
            in_specs=[
                pl.BlockSpec((rows, depth), lambda j, i, c: (i, 0)),
                weight,
                weight,
                block,
            ]
            + unread(deps),
            out_specs=(block, block, block),
        ),
        compiler_params=kernel_params(2),
        cost_estimate=spent(18),
        name="feed_half",
    )(core, normed, w_gate, w_up, grad_hidden, *deps)


def feed_own_kernel(pieces, chunks, gate_w, up_w, grad_hidden, *refs):
    normed = refs[:pieces]
    hidden, parts = refs[-chunks - 3], refs[-chunks - 2 : -2]
    rows, total = refs[-2:]
    step = pl.program_id(0)
    size = total.shape[0] // chunks

    @pl.when(step == 0)
    def _():
        rows[...] = join(normed)

    gate_now = gate_w[...]
    up_now = up_w[...]
    hidden[...], grad_gate, grad_up = swish_grads(
        contract(rows[...], gate_now, 1, 0),
        contract(rows[...], up_now, 1, 0),
        grad_hidden[...].astype(F32),
    )
    term = contract(grad_gate, gate_now, 1, 1) + contract(grad_up, up_now, 1, 1)

    @pl.when(step == 0)
    def _():
        total[...] = term

    @pl.when(step > 0)
    def _():
        total[...] += term

    @pl.when(step == pl.num_programs(0) - 1)
    def _():
        for k, part in enumerate(parts):
            part[...] = total[k * size : (k + 1) * size].astype(BF)


def feed_own(normed, w_gate, w_up, grad_hidden, chunks, deps=()):
    tokens, units = grad_hidden.shape
    depth = w_gate.shape[0]
    size = tokens // chunks
    cols = tile(512, units)
    weight = pl.BlockSpec((depth, cols), lambda j: (0, j))
    block = pl.BlockSpec((tokens, cols), lambda j: (0, j))
    rows = pl.BlockSpec((size, depth), lambda j: (0, 0))
    out = pl.pallas_call(
        functools.partial(feed_own_kernel, len(normed), chunks),
        out_shape=(jax.ShapeDtypeStruct((tokens, units), BF),)
        + (jax.ShapeDtypeStruct((size, depth), BF),) * chunks,
        grid=(units // cols,),
        in_specs=[weight, weight, block] + [whole_spec(n) for n in normed] + unread(deps),
        out_specs=(block,) + (rows,) * chunks,
        scratch_shapes=[pltpu.VMEM((tokens, depth), BF), pltpu.VMEM((tokens, depth), F32)],
        compiler_params=kernel_params(1),
        cost_estimate=spent(18),
        name="feed_own",
    )(w_gate, w_up, grad_hidden, *normed, *deps)
    return out[0], list(out[1:])


def down_kernel(hidden, weight, *refs):
    keep, send = refs[-2:]
    part = contract(hidden[...], weight[...], 1, 0).astype(BF)
    rows = keep.shape[0]
    keep[...] = part[:rows]
    send[...] = part[rows:]


def down_projection(hidden, w_down, deps=()):
    tokens, units = hidden.shape
    depth = w_down.shape[1]
    cols = tile(512, depth)
    half = jax.ShapeDtypeStruct((tokens // 2, depth), BF)
    block = pl.BlockSpec((tokens // 2, cols), lambda j: (0, j))
    return pl.pallas_call(
        down_kernel,
        out_shape=(half, half),
        grid=(depth // cols,),
        in_specs=[whole_spec(hidden), pl.BlockSpec((units, cols), lambda j: (0, j))]
        + unread(deps),
        out_specs=(block, block),
        compiler_params=kernel_params(1),
        cost_estimate=spent(7),
        name="down_projection",
    )(hidden, w_down, *deps)


def add_half_kernel(keep, came, *refs):
    total = keep[...].astype(F32) + came[...].astype(F32)
    first, second = refs[-2:]
    rows = first.shape[0]
    first[...] = total[:rows].astype(BF)
    second[...] = total[rows:].astype(BF)


def add_half(keep, came, deps=()):
    rows, depth = keep.shape
    half = jax.ShapeDtypeStruct((rows // 2, depth), BF)
    return pl.pallas_call(
        add_half_kernel,
        out_shape=(half, half),
        grid=(1,),
        in_specs=[whole_spec(keep), whole_spec(came)] + unread(deps),
        out_specs=(whole_spec(half), whole_spec(half)),
        compiler_params=kernel_params(1),
        cost_estimate=spent(1),
        name="add_half",
    )(keep, came, *deps)


STEPS = 4


def weight_grad_kernel(count, pieces, core, *refs):
    lefts, rights = refs[:count], refs[count : 2 * count]
    wide, lows = refs[-1 - pieces], refs[-pieces:]
    total = contract(lefts[0][...], rights[0][...], 0, 0)
    for left, right in zip(lefts[1:], rights[1:]):
        total = total + contract(left[...], right[...], 0, 0)
    wide[...] = total
    for k, low in enumerate(lows):

        @pl.when(pl.program_id(1) == k)
        def _():
            low[...] = total.astype(BF)


def weight_grad(core, lefts, rights, dim, pieces, deps=()):
    tokens, m = lefts[0].shape
    n = rights[0].shape[1]
    count = len(lefts)
    rows, cols = m // pieces, tile(1024, n)
    across = n // cols
    if dim == 0:
        full = (2 * m, n)
        place = lambda j, i, c: (c[0] * pieces + i, j)
    else:
        full = (m, 2 * n)
        place = lambda j, i, c: (i, c[0] * across + j)
    share = 1

    def piece(k):
        last = share - 1
        return pl.BlockSpec(
            (rows, cols), lambda j, i, c: (jnp.clip(i - k * share, 0, last), j)
        )

    out = pl.pallas_call(
        functools.partial(weight_grad_kernel, count, pieces),
        out_shape=(jax.ShapeDtypeStruct(full, F32),)
        + (jax.ShapeDtypeStruct((rows * share, n), BF),) * pieces,
        grid_spec=pltpu.PrefetchScalarGridSpec(
            num_scalar_prefetch=1,
            grid=(across, pieces),
            in_specs=[pl.BlockSpec((tokens, rows), lambda j, i, c: (0, i))] * count
            + [pl.BlockSpec((tokens, cols), lambda j, i, c: (0, j))] * count
            + unread(deps),
            out_specs=(pl.BlockSpec((rows, cols), place),)
            + tuple(piece(k) for k in range(pieces)),
        ),
        compiler_params=kernel_params(2),
        cost_estimate=spent(19),
        name="weight_grad",
    )(core, *lefts, *rights, *deps)
    return out[0], list(out[1:])


def pair_grad_kernel(count, core, *refs):
    lefts = [r[...] for r in refs[:count]]
    wides, lows = refs[-4:-2], refs[-2:]
    for k in range(2):
        rights = refs[count * (k + 1) : count * (k + 2)]
        total = contract(lefts[0], rights[0][...], 0, 0)
        for left, right in zip(lefts[1:], rights[1:]):
            total = total + contract(left, right[...], 0, 0)
        wides[k][...] = total
        lows[k][0] = total.astype(BF)


def pair_grad(core, lefts, first, second, deps=()):
    tokens, m = lefts[0].shape
    n = first[0].shape[1]
    count = len(lefts)
    rows = m // STEPS
    wide = jax.ShapeDtypeStruct((m, 2 * n), F32)
    low = jax.ShapeDtypeStruct((1, m, n), BF)
    place = pl.BlockSpec((rows, n), lambda i, c: (i, c[0]))
    here = pl.BlockSpec((1, rows, n), lambda i, c: (0, i, 0))
    out = pl.pallas_call(
        functools.partial(pair_grad_kernel, count),
        out_shape=(wide, wide, low, low),
        grid_spec=pltpu.PrefetchScalarGridSpec(
            num_scalar_prefetch=1,
            grid=(STEPS,),
            in_specs=[pl.BlockSpec((tokens, rows), lambda i, c: (0, i))] * count
            + [whole_spec(v) for v in (*first, *second)]
            + unread(deps),
            out_specs=(place, place, here, here),
        ),
        compiler_params=kernel_params(1),
        cost_estimate=spent(34),
        name="pair_grad",
    )(core, *lefts, *first, *second, *deps)
    return out


def left_product_kernel(count, left, *refs):
    right = join(refs[:count])
    refs[-1][...] = contract(left[...], right, 0, 0).astype(BF)


def left_product(left, pieces, deps=()):
    tokens, m = left.shape
    n = pieces[0].shape[1]
    rows, cols = tile(1024, m), tile(512, n)
    return pl.pallas_call(
        functools.partial(left_product_kernel, len(pieces)),
        out_shape=jax.ShapeDtypeStruct((m, n), BF),
        grid=(m // rows, n // cols),
        in_specs=[pl.BlockSpec((tokens, rows), lambda i, j: (0, i))]
        + [pl.BlockSpec((p.shape[0], cols), lambda i, j: (0, j)) for p in pieces]
        + unread(deps),
        out_specs=pl.BlockSpec((rows, cols), lambda i, j: (i, j)),
        compiler_params=kernel_params(2),
        cost_estimate=spent(1),
        name="left_product",
    )(left, *pieces, *deps)


def kv_product_kernel(left, right, *refs):
    gains, out = refs[:-1], refs[-1]
    width = right.shape[1]
    out[:width, :] = contract(right[...], left[...], 0, 0).astype(BF)
    total = sum_chunks(gains)
    out[width:, :] = jnp.concatenate([total, jnp.zeros(total.shape, F32)], axis=0).astype(BF)


def kv_product(left, right, gains, deps=()):
    tokens, m = left.shape
    width = right.shape[1]
    cols = tile(1024, m)

    def kernel(*refs):
        kv_product_kernel(*refs[: 2 + len(gains)], refs[-1])

    return pl.pallas_call(
        kernel,
        out_shape=jax.ShapeDtypeStruct((width + 16, m), BF),
        grid=(m // cols,),
        in_specs=[pl.BlockSpec((tokens, cols), lambda i: (0, i)), whole_spec(right)]
        + [pl.BlockSpec((8, cols), lambda i: (0, i))] * len(gains)
        + unread(deps),
        out_specs=pl.BlockSpec((width + 16, cols), lambda i: (0, i)),
        compiler_params=kernel_params(1),
        cost_estimate=spent(1),
        name="kv_product",
    )(left, right, *gains, *deps)


def mask_kernel(chunks, scalars, place, *refs):
    value = join(refs[:chunks]).astype(F32)
    refs[-1][...] = jnp.where(place[...] < scalars[1], value, 0.0).astype(BF)


def mask_padding(scalars, value, place, chunks, half, deps=()):
    span, depth = value.shape
    rows = span // 2
    first = half * chunks // 2
    out = jax.ShapeDtypeStruct((rows, depth), BF)
    return pl.pallas_call(
        functools.partial(mask_kernel, chunks // 2),
        out_shape=out,
        grid_spec=pltpu.PrefetchScalarGridSpec(
            num_scalar_prefetch=1,
            grid=(1,),
            in_specs=[pl.BlockSpec((rows, 1), lambda i, c: (half, 0))]
            + [chunk_spec(value, chunks, k) for k in range(first, first + chunks // 2)]
            + unread(deps),
            out_specs=whole_spec(out),
        ),
        compiler_params=kernel_params(1),
        cost_estimate=spent(4),
        name="mask_padding",
    )(scalars, place, *[value] * (chunks // 2), *deps)


def pass_on_kernel(value, *refs):
    refs[-1][...] = value[...]


def pass_on(value, deps):
    return pl.pallas_call(
        pass_on_kernel,
        out_shape=jax.ShapeDtypeStruct(value.shape, value.dtype),
        grid=(1,),
        in_specs=[whole_spec(value)] + unread(deps),
        out_specs=whole_spec(value),
        compiler_params=kernel_params(1),
        cost_estimate=spent(2),
        name="pass_on",
    )(value, *deps)


def corner_kernel(value, out):
    out[...] = value[...]


def corner(value):
    return pl.pallas_call(
        corner_kernel,
        out_shape=jax.ShapeDtypeStruct((16, 128), value.dtype),
        grid=(1,),
        in_specs=[pl.BlockSpec((16, 128), lambda i: (0, 0))],
        out_specs=pl.BlockSpec((16, 128), lambda i: (0, 0)),
        compiler_params=kernel_params(1),
        cost_estimate=spent(5),
        name="corner",
    )(value)


def fill_other_kernel(pieces, core, *refs):
    step = pl.program_id(0)
    for k in range(pieces):

        @pl.when(step // (STEPS // pieces) == k)
        def _():
            refs[-1][...] = refs[k][...].astype(F32).reshape(refs[-1].shape)


def fill_other(core, others, index, held, dim, deps=()):
    pieces = len(others)
    share = STEPS // pieces
    rows, n = others[0].shape[1] // share, others[0].shape[2]
    if dim == 0:
        place = lambda i, c: ((1 - c[0]) * STEPS + i, 0)
    else:
        place = lambda i, c: (i, 1 - c[0])

    def piece(k):
        last = share - 1
        return pl.BlockSpec(
            (1, rows, n), lambda i, c: (index, jnp.clip(i - k * share, 0, last), 0)
        )

    return pl.pallas_call(
        functools.partial(fill_other_kernel, pieces),
        out_shape=jax.ShapeDtypeStruct(held.shape, F32),
        grid_spec=pltpu.PrefetchScalarGridSpec(
            num_scalar_prefetch=1,
            grid=(STEPS,),
            in_specs=[piece(k) for k in range(pieces)]
            + [pl.BlockSpec(memory_space=pl.ANY)]
            + unread(deps),
            out_specs=pl.BlockSpec((rows, n), place),
        ),
        input_output_aliases={1 + pieces: 0},
        compiler_params=kernel_params(1),
        cost_estimate=spent(87),
        name="fill_other",
    )(core, *others, held, *deps)


def rotate_block(values, cosine, sine):
    width = values.shape[1]
    column = lax.broadcasted_iota(jnp.int32, values.shape, 1)
    other = jnp.where(
        column % HEAD_SIZE < HEAD_SIZE // 2,
        pltpu.roll(values, width - HEAD_SIZE // 2, 1),
        pltpu.roll(values, HEAD_SIZE // 2, 1),
    )
    return values * cosine + other * sine


def pack_rotated(keys, values, cosine, sine):
    width = keys.shape[1]
    if width % 128 == 0:
        turned = [
            rotate_block(keys[:, i : i + 128], cosine, sine) for i in range(0, width, 128)
        ]
        return jnp.concatenate(turned + [values], axis=1)
    both = jnp.concatenate([keys, values], axis=1)
    column = lax.broadcasted_iota(jnp.int32, both.shape, 1)
    return jnp.where(column < width, rotate_block(both, cosine, sine), both)


def chunk_spec(array, chunks, k):
    block = (array.shape[0] // chunks, array.shape[1])
    return pl.BlockSpec(block, lambda *a: (a[-1][0] ^ k, 0))


def project_kv_kernel(chunks, waits, me, *refs):
    gain, key_w, value_w, cosine, sine = refs[chunks : chunks + 5]
    normed, inverse, packed = refs[-3:]
    stream = join(refs[:chunks]).astype(F32)
    scale = lax.rsqrt(jnp.mean(stream * stream, axis=1, keepdims=True) + EPSILON)
    low = (stream * scale * gain[...]).astype(BF)
    normed[...] = low
    inverse[...] = jnp.broadcast_to(scale, inverse.shape)
    packed[...] = pack_rotated(
        contract(low, key_w[...], 1, 0), contract(low, value_w[...], 1, 0), cosine[...], sine[...]
    ).astype(BF)


def project_kv(me, x, gain, key_matrix, value_matrix, cosine, sine, chunks, deps=()):
    span, depth = x.shape
    args = (gain, key_matrix, value_matrix, cosine, sine)
    outs = (
        jax.ShapeDtypeStruct((span, depth), BF),
        jax.ShapeDtypeStruct((span, 128), F32),
        jax.ShapeDtypeStruct((span, 2 * key_matrix.shape[1]), BF),
    )
    return pl.pallas_call(
        functools.partial(project_kv_kernel, chunks, len(deps)),
        out_shape=outs,
        grid_spec=pltpu.PrefetchScalarGridSpec(
            num_scalar_prefetch=1,
            grid=(1,),
            in_specs=[chunk_spec(x, chunks, k) for k in range(chunks)]
            + [whole_spec(a) for a in args]
            + unread(deps),
            out_specs=tuple(whole_spec(a) for a in outs),
        ),
        compiler_params=kernel_params(1),
        cost_estimate=spent(4),
        name="project_kv",
    )(me, *[x] * chunks, *args, *deps)


def project_query_kernel(normed, weight, cosine, sine, *refs):
    out = refs[-1]
    lin = contract(normed[...], weight[...], 1, 0)
    for i in range(0, lin.shape[1], 128):
        turned = rotate_block(lin[:, i : i + 128], cosine[...], sine[...])
        out[:, i : i + 128] = (turned * HEAD_SIZE**-0.5).astype(BF)


def project_query(normed, w_query, cosine, sine, deps=()):
    span, depth = normed.shape
    width = w_query.shape[1]
    cols = 256
    return pl.pallas_call(
        project_query_kernel,
        out_shape=jax.ShapeDtypeStruct((span, width), BF),
        grid=(width // cols,),
        in_specs=[
            whole_spec(normed),
            pl.BlockSpec((depth, cols), lambda j: (0, j)),
            whole_spec(cosine),
            whole_spec(sine),
        ]
        + unread(deps),
        out_specs=pl.BlockSpec((span, cols), lambda j: (0, j)),
        compiler_params=kernel_params(1),
        cost_estimate=spent(4),
        name="project_query",
    )(normed, w_query, cosine, sine, *deps)


def head_columns(array, index):
    return array[:, index * HEAD_SIZE : (index + 1) * HEAD_SIZE]


def stack_heads(array, heads):
    return jnp.concatenate([head_columns(array, h) for h in heads], axis=0)


def store_heads(out, turned, first, span, finish):
    for i in range(0, turned.shape[1] // span, 2):
        pair = jnp.concatenate(
            [turned[:, (i + e) * span : (i + e + 1) * span] for e in range(2)], axis=0
        )
        at = (first + i) * HEAD_SIZE
        out[:, at : at + 128] = finish(jnp.transpose(pair)).astype(BF)


def attend_kernel(blocks, chunks, shift, query, place, place_row, begin_row, w_output, *refs):
    packed = refs[:blocks]
    attended, stats, *parts = refs[-2 - chunks :]
    span, width = query.shape
    heads_kv = packed[0].shape[1] // (2 * HEAD_SIZE)
    group = width // HEAD_SIZE // heads_kv
    last = jnp.concatenate([place_row[...]] * group, axis=1)
    first = jnp.concatenate([begin_row[...]] * group, axis=1)
    for g in range(heads_kv):
        q = stack_heads(query, range(g * group, (g + 1) * group))
        top = total = mixed = None
        for j in range(blocks):
            keys = head_columns(packed[j], g)
            values = head_columns(packed[j], heads_kv + g)
            key_place = place[...] + shift[j]
            allowed = (key_place >= first) & (key_place <= last)
            masked = jnp.where(allowed, contract(keys, q, 1, 1), -1e30)
            peak = jnp.max(masked, axis=0, keepdims=True)
            peak = peak if j == 0 else jnp.maximum(top, peak)
            terms = jnp.exp(masked - peak)
            amount = jnp.sum(terms, axis=0, keepdims=True)
            term = contract(values, terms.astype(BF), 0, 0)
            if j == 0:
                total, mixed = amount, term
            else:
                fade = jnp.exp(top - peak)
                total, mixed = total * fade + amount, mixed * fade + term
            top = peak
        stats[g : g + 1, :] = top + jnp.log(total)
        store_heads(attended, mixed * (1.0 / total), g * group, span, lambda v: v)
    part = contract(attended[...], w_output[...], 1, 0)
    chunk = span // len(parts)
    for k, out in enumerate(parts):
        out[...] = part[k * chunk : (k + 1) * chunk].astype(BF)


def attend(shift, query, packed, places, w_output, chunks, deps=()):
    span, width = query.shape
    depth = w_output.shape[1]
    blocks = len(packed)
    heads_kv = packed[0].shape[1] // (2 * HEAD_SIZE)
    args = (
        query,
        *places,
        w_output,
        *packed,
    )
    outs = (
        jax.ShapeDtypeStruct((span, width), BF),
        jax.ShapeDtypeStruct((heads_kv, width // HEAD_SIZE // heads_kv * span), F32),
    )
    outs += (jax.ShapeDtypeStruct((span // chunks, depth), BF),) * chunks
    out = pl.pallas_call(
        functools.partial(attend_kernel, blocks, chunks),
        out_shape=outs,
        grid_spec=pltpu.PrefetchScalarGridSpec(
            num_scalar_prefetch=1,
            grid=(1,),
            in_specs=[whole_spec(a) for a in args] + unread(deps),
            out_specs=tuple(whole_spec(a) for a in outs),
        ),
        compiler_params=kernel_params(1),
        cost_estimate=spent(11),
        name="attend",
    )(shift, *args, *deps)
    return out[0], out[1], list(out[2:])


def sum_chunks(refs):
    total = refs[0][...].astype(F32)
    for ref in refs[1:]:
        total = total + ref[...].astype(F32)
    return total


def middle_kernel(count, me, x, gain, *refs):
    chunks, (middle, inverse, normed) = refs[:count], refs[-3:]
    stream = x[...].astype(F32) + sum_chunks(chunks)
    scale = lax.rsqrt(jnp.mean(stream * stream, axis=1, keepdims=True) + EPSILON)
    middle[...] = stream
    inverse[...] = jnp.broadcast_to(scale, inverse.shape)
    normed[...] = (stream * scale * gain[...]).astype(BF)


def middle_norm(me, x, gain, chunks, deps=()):
    rows, depth = chunks[0].shape
    outs = (
        jax.ShapeDtypeStruct((rows, depth), F32),
        jax.ShapeDtypeStruct((rows, 128), F32),
        jax.ShapeDtypeStruct((rows, depth), BF),
    )
    return pl.pallas_call(
        functools.partial(middle_kernel, len(chunks)),
        out_shape=outs,
        grid_spec=pltpu.PrefetchScalarGridSpec(
            num_scalar_prefetch=1,
            grid=(1,),
            in_specs=[chunk_spec(x, len(chunks), 0)]
            + [whole_spec(a) for a in (gain, *chunks)]
            + unread(deps),
            out_specs=tuple(whole_spec(a) for a in outs),
        ),
        compiler_params=kernel_params(1),
        cost_estimate=spent(120),
        name="middle_norm",
    )(me, x, gain, *chunks, *deps)


def halves_kernel(count, *refs):
    half = count // 2
    refs[-2][...] = join(refs[:half])
    refs[-1][...] = join(refs[half:count])


def join_halves(chunks, deps=()):
    rows, depth = chunks[0].shape
    outs = (jax.ShapeDtypeStruct((rows * len(chunks) // 2, depth), BF),) * 2
    return pl.pallas_call(
        functools.partial(halves_kernel, len(chunks)),
        out_shape=outs,
        grid=(1,),
        in_specs=[whole_spec(a) for a in chunks] + unread(deps),
        out_specs=tuple(whole_spec(a) for a in outs),
        compiler_params=kernel_params(1),
        cost_estimate=spent(2),
        name="join_halves",
    )(*chunks, *deps)


def norm_gradient(grad, rows, scale, gain):
    scaled = grad * gain
    product = jnp.mean(scaled * rows, axis=1, keepdims=True)
    gain_grad = jnp.sum(grad * rows * scale, axis=0, keepdims=True)
    return scale * scaled - rows * (scale * scale * scale * product), gain_grad


def norm_back_kernel(count, upstream, middle, inverse, gain, *refs):
    chunks, (wide, low, gain_grad) = refs[:count], refs[-3:]
    grad, gain_grad[...] = norm_gradient(
        sum_chunks(chunks), middle[...], inverse[:, :1], gain[...]
    )
    total = upstream[...].astype(F32) + grad
    wide[...] = total
    low[...] = total.astype(BF)


def norm_back(upstream, middle, inverse, gain, chunks, deps=()):
    rows, depth = middle.shape
    args = (middle, inverse, gain, *chunks)
    outs = (
        jax.ShapeDtypeStruct((rows, depth), F32),
        jax.ShapeDtypeStruct((rows, depth), BF),
        jax.ShapeDtypeStruct((1, depth), F32),
    )
    return pl.pallas_call(
        functools.partial(norm_back_kernel, len(chunks)),
        out_shape=outs,
        grid=(1,),
        in_specs=[pl.BlockSpec((rows, depth), lambda i: (0, 0))]
        + [whole_spec(a) for a in args]
        + unread(deps),
        out_specs=tuple(whole_spec(a) for a in outs),
        compiler_params=kernel_params(1),
        cost_estimate=spent(3),
        name="norm_back",
    )(upstream, *args, *deps)


def finish_kernel(count, me, x, inverse, gain, grad_middle, block, *refs):
    grad, _ = norm_gradient(
        sum_chunks(refs[:count]), x[...].astype(F32), inverse[:, :1], gain[...]
    )
    refs[-1][...] = jnp.concatenate([grad_middle[...] + grad, block[...]], axis=0).astype(BF)


def finish(me, x, inverse, gain, grad_middle, block, chunks, deps=()):
    rows, depth = grad_middle.shape
    args = (gain, grad_middle, block, *chunks)
    outs = jax.ShapeDtypeStruct((2 * rows, depth), BF)
    return pl.pallas_call(
        functools.partial(finish_kernel, len(chunks)),
        out_shape=outs,
        grid_spec=pltpu.PrefetchScalarGridSpec(
            num_scalar_prefetch=1,
            grid=(1,),
            in_specs=[
                chunk_spec(x, len(chunks), 0),
                pl.BlockSpec((rows, 128), lambda i, c: (0, 0)),
            ]
            + [whole_spec(a) for a in args]
            + unread(deps),
            out_specs=whole_spec(outs),
        ),
        compiler_params=kernel_params(1),
        cost_estimate=spent(3),
        name="finish",
    )(me, x, inverse, *args, *deps)


def add_kernel(count, *refs):
    refs[-1][...] = sum_chunks(refs[:count]).astype(refs[-1].dtype)


def add_up(arrays, dtype, deps=()):
    out = jax.ShapeDtypeStruct(arrays[0].shape, dtype)
    return pl.pallas_call(
        functools.partial(add_kernel, len(arrays)),
        out_shape=out,
        grid=(1,),
        in_specs=[whole_spec(a) for a in arrays] + unread(deps),
        out_specs=whole_spec(out),
        compiler_params=kernel_params(1),
        cost_estimate=spent(2),
        name="add_up",
    )(*arrays, *deps)


def restore_kernel(count, me, *refs):
    step = pl.program_id(0)
    for k in range(count):

        @pl.when(step == k)
        def _():
            rows = refs[k].shape[0] // 2
            refs[-2][...] = refs[k][:rows]
            refs[-1][...] = refs[k][rows:]


def restore(me, pieces, deps=()):
    count = len(pieces)
    rows, depth = pieces[0].shape[0] // 2, pieces[0].shape[1]
    if rows % 16:
        halves = [[p[:rows] for p in pieces], [p[rows:] for p in pieces]]
        return [reorder(jnp.concatenate(h, axis=0), "tensor") for h in halves]
    out = jax.ShapeDtypeStruct((count * rows, depth), BF)
    place = pl.BlockSpec((rows, depth), lambda i, c: (c[0] ^ i, 0))
    return pl.pallas_call(
        functools.partial(restore_kernel, count),
        out_shape=(out, out),
        grid_spec=pltpu.PrefetchScalarGridSpec(
            num_scalar_prefetch=1,
            grid=(count,),
            in_specs=[whole_spec(p) for p in pieces] + unread(deps),
            out_specs=(place, place),
        ),
        compiler_params=kernel_params(1),
        cost_estimate=spent(87),
        name="restore",
    )(me, *pieces, *deps)


def widen(wo, wq, wkv, width, deps=()):
    steps = 4
    depth = wq.shape[0]
    shapes = [wo.shape, wq.shape, (depth, width), (depth, width)]

    def spec(shape):
        return pl.BlockSpec((shape[0] // steps, shape[1]), lambda i: (i, 0))

    def kernel(wo, wq, wkv, *refs):
        wo_out, wq_out, wk_out, wv_out, gains = refs[-5:]
        wo_out[...] = wo[...].astype(F32)
        wq_out[...] = wq[...].astype(F32)
        turned = jnp.transpose(wkv[: 2 * width, :].astype(F32))
        wk_out[...] = turned[:, :width]
        wv_out[...] = turned[:, width:]
        gains[...] = wkv[2 * width :, :].astype(F32)[:8]

    return pl.pallas_call(
        kernel,
        out_shape=tuple(jax.ShapeDtypeStruct(v, F32) for v in [*shapes, (8, depth)]),
        grid=(steps,),
        in_specs=[
            spec(wo.shape),
            spec(wq.shape),
            pl.BlockSpec((wkv.shape[0], depth // steps), lambda i: (0, i)),
        ]
        + unread(deps),
        out_specs=tuple(spec(v) for v in shapes)
        + (pl.BlockSpec((8, depth // steps), lambda i: (0, i)),),
        compiler_params=kernel_params(1),
        cost_estimate=spent(8),
        name="widen",
    )(wo, wq, wkv, *deps)


def gain_sum_kernel(count, *refs):
    total = sum_chunks(refs[:count])
    refs[-2][...] = total[:1]
    refs[-1][...] = total[1:2]


def gain_sum(pieces, deps=()):
    out = jax.ShapeDtypeStruct((1, pieces[0].shape[1]), F32)
    return pl.pallas_call(
        functools.partial(gain_sum_kernel, len(pieces)),
        out_shape=(out, out),
        grid=(1,),
        in_specs=[whole_spec(p) for p in pieces] + unread(deps),
        out_specs=(whole_spec(out), whole_spec(out)),
        compiler_params=kernel_params(1),
        cost_estimate=spent(2),
        name="gain_sum",
    )(*pieces, *deps)


def attend_back_kernel(blocks, count, shift, query, attended, stats, place, place_row, begin_row,
                       cosine, sine, w_output, *refs):
    packed = refs[:blocks]
    chunks = refs[blocks : blocks + count]
    grad_query = refs[-1 - blocks]
    terms = refs[-blocks:]
    span, width = query.shape
    heads_kv = packed[0].shape[1] // (2 * HEAD_SIZE)
    group = width // HEAD_SIZE // heads_kv
    grad_middle = join(chunks)
    grad_attended = contract(grad_middle, w_output[...], 1, 1).astype(BF)
    last = jnp.concatenate([place_row[...]] * group, axis=1)
    first = jnp.concatenate([begin_row[...]] * group, axis=1)
    key_terms = [[] for _ in range(blocks)]
    value_terms = [[] for _ in range(blocks)]
    for g in range(heads_kv):
        mine = range(g * group, (g + 1) * group)
        q = stack_heads(query, mine)
        grad = stack_heads(grad_attended, mine)
        norm = stats[g : g + 1, :]
        inner = lax.dot_general(
            jnp.ones((8, HEAD_SIZE), F32),
            grad.astype(F32) * stack_heads(attended, mine).astype(F32),
            (((1,), (1,)), ((), ())),
            preferred_element_type=F32,
            precision=lax.Precision.HIGHEST,
        )[:1]
        total = None
        for j in range(blocks):
            keys = head_columns(packed[j], g)
            values = head_columns(packed[j], heads_kv + g)
            key_place = place[...] + shift[j]
            allowed = (key_place >= first) & (key_place <= last)
            scores = contract(keys, q, 1, 1)
            probs = jnp.exp(jnp.where(allowed, scores - norm, -1e30))
            grad_scores = (probs * (contract(values, grad, 1, 1) - inner)).astype(BF)
            value_terms[j].append(contract(probs.astype(BF), grad, 1, 0))
            key_terms[j].append(contract(grad_scores, q, 1, 0))
            term = contract(keys, grad_scores, 0, 0)
            total = term if total is None else total + term
        store_heads(
            grad_query,
            total,
            g * group,
            span,
            lambda v: rotate_block(v * HEAD_SIZE**-0.5, cosine[...], -sine[...]),
        )
    for j in range(blocks):
        terms[j][...] = jnp.concatenate(key_terms[j] + value_terms[j], axis=1).astype(BF)


def attend_back(shift, query, attended, stats, packed, places, cosine, sine, w_output, chunks,
                deps=()):
    span, width = query.shape
    blocks = len(packed)
    args = (
        query,
        attended,
        stats,
        *places,
        cosine,
        sine,
        w_output,
        *packed,
        *chunks,
    )
    outs = (jax.ShapeDtypeStruct((span, width), BF),)
    outs += (jax.ShapeDtypeStruct(packed[0].shape, BF),) * blocks
    out = pl.pallas_call(
        functools.partial(attend_back_kernel, blocks, len(chunks)),
        out_shape=outs,
        grid_spec=pltpu.PrefetchScalarGridSpec(
            num_scalar_prefetch=1,
            grid=(1,),
            in_specs=[whole_spec(a) for a in args] + unread(deps),
            out_specs=tuple(whole_spec(a) for a in outs),
        ),
        compiler_params=kernel_params(1),
        cost_estimate=spent(16),
        name="attend_back",
    )(shift, *args, *deps)
    return out[0], list(out[1:])


def input_back_kernel(
    count, chunks, me, grad_query, w_query, key_w, value_w, cosine, sine, inverse, gain_two, *refs
):
    terms, rows = refs[:count], refs[count : count + chunks]
    lin, gains, *parts = refs[-2 - chunks :]
    normed = join(rows).astype(F32) * inverse[:, :1]
    width = key_w.shape[1]
    total = sum_chunks(terms)
    low = pack_rotated(total[:, :width], total[:, width:], cosine[...], -sine[...]).astype(BF)
    lin[...] = low
    part = contract(grad_query[...], w_query[...], 1, 1)
    part = part + contract(low[:, :width], key_w[...], 1, 1)
    part = part + contract(low[:, width:], value_w[...], 1, 1)
    rows = part.shape[0] // chunks
    for k, out in enumerate(parts):
        out[...] = part[k * rows : (k + 1) * rows].astype(BF)
    gain_one = jnp.sum(part * normed, axis=0, keepdims=True)
    empty = jnp.zeros((6, part.shape[1]), F32)
    gains[...] = jnp.concatenate([gain_one, gain_two[...], empty], axis=0)


def input_back(
    me,
    grad_query,
    w_query,
    key_matrix,
    value_matrix,
    cosine,
    sine,
    inverse,
    x,
    gain_two,
    terms,
    chunks,
    deps=(),
):
    span = grad_query.shape[0]
    depth = w_query.shape[0]
    args = (grad_query, w_query, key_matrix, value_matrix, cosine, sine, inverse, gain_two)
    args += tuple(terms)
    outs = (
        jax.ShapeDtypeStruct(terms[0].shape, BF),
        jax.ShapeDtypeStruct((8, depth), F32),
    )
    outs += (jax.ShapeDtypeStruct((span // chunks, depth), BF),) * chunks
    out = pl.pallas_call(
        functools.partial(input_back_kernel, len(terms), chunks),
        out_shape=outs,
        grid_spec=pltpu.PrefetchScalarGridSpec(
            num_scalar_prefetch=1,
            grid=(1,),
            in_specs=[whole_spec(a) for a in args]
            + [chunk_spec(x, chunks, k) for k in range(chunks)]
            + unread(deps),
            out_specs=tuple(whole_spec(a) for a in outs),
        ),
        compiler_params=kernel_params(1),
        cost_estimate=spent(1),
        name="input_back",
    )(me, *args, *[x] * chunks, *deps)
    return out[0], out[1], list(out[2:])


def rope_tables(positions):
    expo = np.arange(HEAD_SIZE // 2, dtype=np.float64) * 2.0 / HEAD_SIZE
    inverse = 1.0 / 500000.0**expo
    wavelength = 2.0 * np.pi / inverse
    smooth = (8192.0 / wavelength - 1.0) / 3.0
    middle = (1.0 - smooth) * inverse / 32.0 + smooth * inverse
    scaled = np.where(
        wavelength < 2048.0, inverse, np.where(wavelength > 8192.0, inverse / 32.0, middle)
    )
    scaled = jnp.asarray(np.tile(scaled, 4)[None, :].astype(np.float32))
    sign = jnp.asarray(np.tile(np.repeat([-1.0, 1.0], HEAD_SIZE // 2), 2)[None, :].astype(np.float32))
    angles = positions.astype(F32)[:, None] * scaled
    return jnp.cos(angles), jnp.sin(angles) * sign


def flip(value, axis, mask):
    return lax.ppermute(value, axis, [(i, i ^ mask) for i in range(lax.axis_size(axis))])


def reorder(value, axis):
    n = lax.axis_size(axis)
    me = lax.axis_index(axis)
    chunk = value.shape[0] // n
    return jnp.concatenate(
        [lax.dynamic_slice_in_dim(value, (me ^ k) * chunk, chunk, 0) for k in range(n)], axis=0
    )


def exchange(chunks, axis):
    return chunks[:1] + [flip(chunks[k], axis, k) for k in reversed(range(1, len(chunks)))]


def spread(chunk, axis):
    return [chunk] + [flip(chunk, axis, k) for k in range(1, lax.axis_size(axis))]


def gather_halves(first, second):
    return [
        lax.all_gather(first, ("rows", "seq"), axis=0, tiled=True),
        lax.all_gather(second, ("seq", "rows"), axis=0, tiled=True),
    ]


def per_device(
    activations,
    doc_lengths,
    w_query,
    key_matrix,
    value_matrix,
    w_output,
    w_gate,
    w_up,
    w_down,
    gain_attn,
    gain_ffn,
    cotangent,
):
    span = activations.shape[1]
    blocks = lax.axis_size("seq")
    chunks = lax.axis_size("tensor")
    chunk = span // chunks
    core = lax.axis_index("rows").astype(jnp.int32).reshape(1)
    block_here = lax.axis_index("seq")
    gain_attn = gain_attn.reshape(1, -1)
    gain_ffn = gain_ffn.reshape(1, -1)
    stream, cotangent = activations[0], cotangent[0]
    me = lax.axis_index("tensor").astype(jnp.int32)
    token = jnp.arange(span, dtype=jnp.int32)
    place = block_here * span + (me ^ (token // chunk)) * chunk + token % chunk
    if chunk % 16:
        stream, cotangent = reorder(stream, "tensor"), reorder(cotangent, "tensor")
        me = jnp.zeros_like(me)
    order = jnp.arange(DOCS, dtype=jnp.int32)
    ends = jnp.sum(jnp.where(order[None, :] <= order[:, None], doc_lengths[0][None, :], 0), axis=1)
    begin = jnp.max(jnp.where(place[:, None] >= ends[None, :], ends[None, :], 0), axis=1)
    cosine, sine = rope_tables(place - begin)
    shift = jnp.stack([((block_here ^ j) - block_here) * span for j in range(blocks)])
    shift = shift.astype(jnp.int32)
    scalars = jnp.stack([me, ends[-1].astype(jnp.int32)])
    places = (place.reshape(span, 1), place.reshape(1, span), begin.reshape(1, span))

    normed_one, inverse_one, packed = project_kv(
        scalars, stream, gain_attn, key_matrix, value_matrix, cosine, sine, chunks, (shift, *places)
    )
    packed = spread(packed, "seq")
    query = project_query(normed_one, w_query, cosine, sine)
    upstream = [mask_padding(scalars, cotangent, places[0], chunks, 0, (query, *packed))]
    upstream_all = [lax.all_gather(upstream[0], ("rows", "seq"), axis=0, tiled=True)]
    attended, stats, parts = attend(
        shift, query, packed, places, w_output, chunks, (upstream[0],)
    )
    upstream.append(mask_padding(scalars, cotangent, places[0], chunks, 1, (parts[0],)))
    upstream_all.append(lax.all_gather(upstream[1], ("seq", "rows"), axis=0, tiled=True))

    sent = exchange(parts, "tensor")
    grad_hidden = grad_hidden_of(core, upstream, w_down, 1, (parts[0],))
    middle, inverse_two, normed = middle_norm(scalars, stream, gain_ffn, sent, (grad_hidden,))

    grad_hidden_first = grad_hidden_of(core, upstream_all[:1], w_down, 2, (middle,))
    normed = join_halves(spread(normed, "tensor"), (grad_hidden_first,))
    normed_all = gather_halves(*normed)
    hidden, parts = feed_own(normed, w_gate, w_up, grad_hidden, chunks)

    sent = exchange(parts, "tensor")
    grad_hidden_second = grad_hidden_of(core, upstream_all[1:], w_down, 2, (parts[0],))
    grad_middle, grad_middle_low, gain_two = norm_back(
        upstream[0], middle, inverse_two, gain_ffn, sent, (grad_hidden_second,)
    )
    grad_middle_all = spread(grad_middle_low, "tensor")
    feed_first = feed_half(
        core, normed_all[0], w_gate, w_up, grad_hidden_first, (grad_middle,)
    )
    down_parts = down_projection(hidden, w_down, (feed_first[0],))
    down_send = pass_on(down_parts[1], grad_middle_all)
    grad_query, kv_terms = attend_back(
        shift,
        query,
        attended,
        stats,
        packed,
        places,
        cosine,
        sine,
        w_output,
        grad_middle_all,
        (corner(down_send),),
    )
    mask = chunks // 2
    down_came = flip(down_send, "tensor", mask)

    kv_sent = exchange(kv_terms, "seq")
    wq_part = left_product(normed_one, [grad_query])
    wo_part = left_product(attended, grad_middle_all, (wq_part,))
    grad_kv, gains, parts = input_back(
        scalars,
        grad_query,
        w_query,
        key_matrix,
        value_matrix,
        cosine,
        sine,
        inverse_one,
        stream,
        gain_two,
        kv_sent,
        chunks,
        (wo_part, normed_all[1]),
    )

    wkv_part = kv_product(normed_one, grad_kv, [gains])
    sent = exchange(parts, "tensor")
    grad_wo, grad_wq, grad_wkv = lax.psum((wo_part, wq_part, wkv_part), ("rows", "seq"))
    keep, send = add_half(down_parts[0], down_came, (wkv_part,))
    while mask > 2:
        mask //= 2
        keep, send = add_half(keep, flip(send, "tensor", mask))
    feed_second = feed_half(
        core, normed_all[1], w_gate, w_up, grad_hidden_second, (keep,)
    )
    hidden_all, grad_gate_all, grad_up_all = zip(feed_first, feed_second)
    grad_down, low = weight_grad(core, hidden_all, upstream_all, 0, 2)
    down_other = [flip(v[None], "rows", 1) for v in low]
    block_chunk = add_up(
        [middle, keep, flip(send, "tensor", mask // 2)], F32, (grad_down,)
    )
    both = finish(
        scalars, stream, inverse_one, gain_attn, grad_middle, block_chunk, sent
    )
    both_all = spread(both, "tensor")
    grad_gate_w, grad_up_w, *low = pair_grad(
        core, normed_all, grad_gate_all, grad_up_all, (both,)
    )
    gate_other, up_other = [flip(v, "rows", 1) for v in low]
    grad_down = fill_other(core, down_other, 0, grad_down, 0, (grad_up_w,))
    grad_gate_w = fill_other(core, [gate_other], 0, grad_gate_w, 1, (grad_down,))
    grad_wo, grad_wq, grad_wk, grad_wv, gains = widen(
        grad_wo, grad_wq, grad_wkv, key_matrix.shape[1], (grad_gate_w,)
    )
    grad_input, block_output = restore(scalars, both_all, (grad_wo,))
    gains = pass_on(gains, (grad_input,))
    grad_up_w = fill_other(core, [up_other], 0, grad_up_w, 1, (gains,))
    gains = gain_sum(spread(gains, "tensor"), (grad_up_w,))
    return (
        block_output[None],
        grad_input[None],
        grad_wq,
        grad_wk,
        grad_wv,
        grad_wo,
        grad_gate_w,
        grad_up_w,
        grad_down,
        gains[0].reshape(-1),
        gains[1].reshape(-1),
    )


def solution(mesh):
    placed = (
        P("rows", "seq", None),
        P("rows", None),
        P(None, "tensor"),
        P(None, "tensor"),
        P(None, "tensor"),
        P("tensor", None),
        P(None, "tensor"),
        P(None, "tensor"),
        P("tensor", None),
        P(),
        P(),
        P("rows", "seq", None),
    )
    return jax.shard_map(
        per_device,
        mesh=mesh,
        in_specs=placed,
        out_specs=(
            P("rows", "seq", None),
            P("rows", "seq", None),
            P(None, "tensor"),
            P(None, "tensor"),
            P(None, "tensor"),
            P("tensor", None),
            P(None, "tensor"),
            P(None, "tensor"),
            P("tensor", None),
            P(),
            P(),
        ),
        check_vma=False,
    )
```

```python
import functools

import jax
import jax.numpy as jnp
from jax import lax
from jax.experimental import pallas as pl
from jax.experimental.pallas import tpu as pltpu
import numpy as np
from jax.sharding import PartitionSpec as P

HEAD_SIZE = 64
DOCS = 4
EPSILON = 1e-05
BF = jnp.bfloat16
F32 = jnp.float32


MIB = 1 << 20


def kernel_params(dims):
    return pltpu.CompilerParams(
        vmem_limit_bytes=64 * MIB - 32768, dimension_semantics=("arbitrary",) * dims
    )


def contract(a, b, dim_a, dim_b):
    return lax.dot_general(
        a, b, (((dim_a,), (dim_b,)), ((), ())), preferred_element_type=F32
    )


def tile(limit, size):
    while size > limit and size % 2 == 0:
        size //= 2
    return size


SMALL = pl.CostEstimate(flops=1, bytes_accessed=1, transcendentals=0)


def spent(us):
    return pl.CostEstimate(flops=us * 10**9, bytes_accessed=1, transcendentals=0)


def whole_spec(array):
    shape = array.shape
    return pl.BlockSpec(shape, lambda *_: (0,) * len(shape))


def join(refs):
    if refs[0].shape[0] % 16 == 0:
        return jnp.concatenate([r[...] for r in refs], axis=0)
    return jnp.concatenate([r[...].astype(F32) for r in refs], axis=0).astype(refs[0].dtype)


def unread(deps):
    return [pl.BlockSpec(memory_space=pl.ANY)] * len(deps)


def times_transposed_kernel(count, core, weight, *refs):
    refs[-1][...] = contract(join(refs[:count]), weight[...], 1, 1).astype(BF)


def grad_hidden_of(core, pieces, w_down, shares, deps=()):
    count = len(pieces)
    tokens, depth = pieces[0].shape
    units = w_down.shape[0] // shares
    rows, cols = tile(640, tokens), tile(1024 // (3 - shares), units)
    steps = units // cols
    offset = steps * (shares - 1)
    return pl.pallas_call(
        functools.partial(times_transposed_kernel, count),
        out_shape=jax.ShapeDtypeStruct((count * tokens, units), BF),
        grid_spec=pltpu.PrefetchScalarGridSpec(
            num_scalar_prefetch=1,
            grid=(steps, tokens // rows),
            in_specs=[pl.BlockSpec((cols, depth), lambda j, i, c: (c[0] * offset + j, 0))]
            + [pl.BlockSpec((rows, depth), lambda j, i, c: (i, 0))] * count
            + unread(deps),
            out_specs=pl.BlockSpec((count * rows, cols), lambda j, i, c: (i, j)),
        ),
        compiler_params=kernel_params(2),
        cost_estimate=spent(10),
        name="grad_hidden_of",
    )(core, w_down, *pieces, *deps)


def swish_grads(gate, up_proj, grad_hidden):
    sigmoid = 1.0 / (1.0 + jnp.exp(-gate))
    activated = gate * sigmoid
    hidden = (activated * up_proj).astype(BF)
    grad_gate = (grad_hidden * up_proj * (sigmoid * (1.0 + gate * (1.0 - sigmoid)))).astype(BF)
    grad_up = (grad_hidden * activated).astype(BF)
    return hidden, grad_gate, grad_up


def feed_half_kernel(core, normed, gate_w, up_w, grad_hidden, *refs):
    hidden, grad_gate, grad_up = refs[-3:]
    rows = normed[...]
    hidden[...], grad_gate[...], grad_up[...] = swish_grads(
        contract(rows, gate_w[...], 1, 0),
        contract(rows, up_w[...], 1, 0),
        grad_hidden[...].astype(F32),
    )


def feed_half(core, normed, w_gate, w_up, grad_hidden, deps=()):
    tokens, depth = normed.shape
    half = w_gate.shape[1] // 2
    rows, cols = tile(640, tokens), tile(512, half)
    steps = half // cols
    out = jax.ShapeDtypeStruct((tokens, half), BF)
    weight = pl.BlockSpec((depth, cols), lambda j, i, c: (0, c[0] * steps + j))
    block = pl.BlockSpec((rows, cols), lambda j, i, c: (i, j))
    return pl.pallas_call(
        feed_half_kernel,
        out_shape=(out, out, out),
        grid_spec=pltpu.PrefetchScalarGridSpec(
            num_scalar_prefetch=1,
            grid=(steps, tokens // rows),
            in_specs=[
                pl.BlockSpec((rows, depth), lambda j, i, c: (i, 0)),
                weight,
                weight,
                block,
            ]
            + unread(deps),
            out_specs=(block, block, block),
        ),
        compiler_params=kernel_params(2),
        cost_estimate=spent(18),
        name="feed_half",
    )(core, normed, w_gate, w_up, grad_hidden, *deps)


def feed_own_kernel(pieces, chunks, gate_w, up_w, grad_hidden, *refs):
    normed = refs[:pieces]
    hidden, parts = refs[-chunks - 3], refs[-chunks - 2 : -2]
    rows, total = refs[-2:]
    step = pl.program_id(0)
    size = total.shape[0] // chunks

    @pl.when(step == 0)
    def _():
        rows[...] = join(normed)

    gate_now = gate_w[...]
    up_now = up_w[...]
    hidden[...], grad_gate, grad_up = swish_grads(
        contract(rows[...], gate_now, 1, 0),
        contract(rows[...], up_now, 1, 0),
        grad_hidden[...].astype(F32),
    )
    term = contract(grad_gate, gate_now, 1, 1) + contract(grad_up, up_now, 1, 1)

    @pl.when(step == 0)
    def _():
        total[...] = term

    @pl.when(step > 0)
    def _():
        total[...] += term

    @pl.when(step == pl.num_programs(0) - 1)
    def _():
        for k, part in enumerate(parts):
            part[...] = total[k * size : (k + 1) * size].astype(BF)


def feed_own(normed, w_gate, w_up, grad_hidden, chunks, deps=()):
    tokens, units = grad_hidden.shape
    depth = w_gate.shape[0]
    size = tokens // chunks
    cols = tile(512, units)
    weight = pl.BlockSpec((depth, cols), lambda j: (0, j))
    block = pl.BlockSpec((tokens, cols), lambda j: (0, j))
    rows = pl.BlockSpec((size, depth), lambda j: (0, 0))
    out = pl.pallas_call(
        functools.partial(feed_own_kernel, len(normed), chunks),
        out_shape=(jax.ShapeDtypeStruct((tokens, units), BF),)
        + (jax.ShapeDtypeStruct((size, depth), BF),) * chunks,
        grid=(units // cols,),
        in_specs=[weight, weight, block] + [whole_spec(n) for n in normed] + unread(deps),
        out_specs=(block,) + (rows,) * chunks,
        scratch_shapes=[pltpu.VMEM((tokens, depth), BF), pltpu.VMEM((tokens, depth), F32)],
        compiler_params=kernel_params(1),
        cost_estimate=spent(18),
        name="feed_own",
    )(w_gate, w_up, grad_hidden, *normed, *deps)
    return out[0], list(out[1:])


def down_kernel(hidden, weight, *refs):
    keep, send = refs[-2:]
    part = contract(hidden[...], weight[...], 1, 0).astype(BF)
    rows = keep.shape[0]
    keep[...] = part[:rows]
    send[...] = part[rows:]


def down_projection(hidden, w_down, deps=()):
    tokens, units = hidden.shape
    depth = w_down.shape[1]
    cols = tile(512, depth)
    half = jax.ShapeDtypeStruct((tokens // 2, depth), BF)
    block = pl.BlockSpec((tokens // 2, cols), lambda j: (0, j))
    return pl.pallas_call(
        down_kernel,
        out_shape=(half, half),
        grid=(depth // cols,),
        in_specs=[whole_spec(hidden), pl.BlockSpec((units, cols), lambda j: (0, j))]
        + unread(deps),
        out_specs=(block, block),
        compiler_params=kernel_params(1),
        cost_estimate=spent(7),
        name="down_projection",
    )(hidden, w_down, *deps)


def add_half_kernel(keep, came, *refs):
    total = keep[...].astype(F32) + came[...].astype(F32)
    first, second = refs[-2:]
    rows = first.shape[0]
    first[...] = total[:rows].astype(BF)
    second[...] = total[rows:].astype(BF)


def add_half(keep, came, deps=()):
    rows, depth = keep.shape
    half = jax.ShapeDtypeStruct((rows // 2, depth), BF)
    return pl.pallas_call(
        add_half_kernel,
        out_shape=(half, half),
        grid=(1,),
        in_specs=[whole_spec(keep), whole_spec(came)] + unread(deps),
        out_specs=(whole_spec(half), whole_spec(half)),
        compiler_params=kernel_params(1),
        cost_estimate=spent(1),
        name="add_half",
    )(keep, came, *deps)


STEPS = 4


def weight_grad_kernel(count, pieces, core, *refs):
    lefts, rights = refs[:count], refs[count : 2 * count]
    wide, lows = refs[-1 - pieces], refs[-pieces:]
    total = contract(lefts[0][...], rights[0][...], 0, 0)
    for left, right in zip(lefts[1:], rights[1:]):
        total = total + contract(left[...], right[...], 0, 0)
    wide[...] = total
    for k, low in enumerate(lows):

        @pl.when(pl.program_id(1) == k)
        def _():
            low[...] = total.astype(BF)


def weight_grad(core, lefts, rights, dim, pieces, deps=()):
    tokens, m = lefts[0].shape
    n = rights[0].shape[1]
    count = len(lefts)
    rows, cols = m // pieces, tile(1024, n)
    across = n // cols
    if dim == 0:
        full = (2 * m, n)
        place = lambda j, i, c: (c[0] * pieces + i, j)
    else:
        full = (m, 2 * n)
        place = lambda j, i, c: (i, c[0] * across + j)
    share = 1

    def piece(k):
        last = share - 1
        return pl.BlockSpec(
            (rows, cols), lambda j, i, c: (jnp.clip(i - k * share, 0, last), j)
        )

    out = pl.pallas_call(
        functools.partial(weight_grad_kernel, count, pieces),
        out_shape=(jax.ShapeDtypeStruct(full, F32),)
        + (jax.ShapeDtypeStruct((rows * share, n), BF),) * pieces,
        grid_spec=pltpu.PrefetchScalarGridSpec(
            num_scalar_prefetch=1,
            grid=(across, pieces),
            in_specs=[pl.BlockSpec((tokens, rows), lambda j, i, c: (0, i))] * count
            + [pl.BlockSpec((tokens, cols), lambda j, i, c: (0, j))] * count
            + unread(deps),
            out_specs=(pl.BlockSpec((rows, cols), place),)
            + tuple(piece(k) for k in range(pieces)),
        ),
        compiler_params=kernel_params(2),
        cost_estimate=spent(19),
        name="weight_grad",
    )(core, *lefts, *rights, *deps)
    return out[0], list(out[1:])


def pair_grad_kernel(count, core, *refs):
    lefts = [r[...] for r in refs[:count]]
    wides, lows = refs[-4:-2], refs[-2:]
    for k in range(2):
        rights = refs[count * (k + 1) : count * (k + 2)]
        total = contract(lefts[0], rights[0][...], 0, 0)
        for left, right in zip(lefts[1:], rights[1:]):
            total = total + contract(left, right[...], 0, 0)
        wides[k][...] = total
        lows[k][0] = total.astype(BF)


def pair_grad(core, lefts, first, second, deps=()):
    tokens, m = lefts[0].shape
    n = first[0].shape[1]
    count = len(lefts)
    rows = m // STEPS
    wide = jax.ShapeDtypeStruct((m, 2 * n), F32)
    low = jax.ShapeDtypeStruct((1, m, n), BF)
    place = pl.BlockSpec((rows, n), lambda i, c: (i, c[0]))
    here = pl.BlockSpec((1, rows, n), lambda i, c: (0, i, 0))
    out = pl.pallas_call(
        functools.partial(pair_grad_kernel, count),
        out_shape=(wide, wide, low, low),
        grid_spec=pltpu.PrefetchScalarGridSpec(
            num_scalar_prefetch=1,
            grid=(STEPS,),
            in_specs=[pl.BlockSpec((tokens, rows), lambda i, c: (0, i))] * count
            + [whole_spec(v) for v in (*first, *second)]
            + unread(deps),
            out_specs=(place, place, here, here),
        ),
        compiler_params=kernel_params(1),
        cost_estimate=spent(34),
        name="pair_grad",
    )(core, *lefts, *first, *second, *deps)
    return out


def left_product_kernel(count, left, *refs):
    right = join(refs[:count])
    refs[-1][...] = contract(left[...], right, 0, 0).astype(BF)


def left_product(left, pieces, deps=()):
    tokens, m = left.shape
    n = pieces[0].shape[1]
    rows, cols = tile(1024, m), tile(512, n)
    return pl.pallas_call(
        functools.partial(left_product_kernel, len(pieces)),
        out_shape=jax.ShapeDtypeStruct((m, n), BF),
        grid=(m // rows, n // cols),
        in_specs=[pl.BlockSpec((tokens, rows), lambda i, j: (0, i))]
        + [pl.BlockSpec((p.shape[0], cols), lambda i, j: (0, j)) for p in pieces]
        + unread(deps),
        out_specs=pl.BlockSpec((rows, cols), lambda i, j: (i, j)),
        compiler_params=kernel_params(2),
        cost_estimate=spent(1),
        name="left_product",
    )(left, *pieces, *deps)


def kv_product_kernel(left, right, *refs):
    gains, out = refs[:-1], refs[-1]
    width = right.shape[1]
    out[:width, :] = contract(right[...], left[...], 0, 0).astype(BF)
    total = sum_chunks(gains)
    out[width:, :] = jnp.concatenate([total, jnp.zeros(total.shape, F32)], axis=0).astype(BF)


def kv_product(left, right, gains, deps=()):
    tokens, m = left.shape
    width = right.shape[1]
    cols = tile(1024, m)

    def kernel(*refs):
        kv_product_kernel(*refs[: 2 + len(gains)], refs[-1])

    return pl.pallas_call(
        kernel,
        out_shape=jax.ShapeDtypeStruct((width + 16, m), BF),
        grid=(m // cols,),
        in_specs=[pl.BlockSpec((tokens, cols), lambda i: (0, i)), whole_spec(right)]
        + [pl.BlockSpec((8, cols), lambda i: (0, i))] * len(gains)
        + unread(deps),
        out_specs=pl.BlockSpec((width + 16, cols), lambda i: (0, i)),
        compiler_params=kernel_params(1),
        cost_estimate=spent(1),
        name="kv_product",
    )(left, right, *gains, *deps)


def mask_kernel(chunks, scalars, place, *refs):
    value = join(refs[:chunks]).astype(F32)
    refs[-1][...] = jnp.where(place[...] < scalars[1], value, 0.0).astype(BF)


def mask_padding(scalars, value, place, chunks, half, deps=()):
    span, depth = value.shape
    rows = span // 2
    first = half * chunks // 2
    out = jax.ShapeDtypeStruct((rows, depth), BF)
    return pl.pallas_call(
        functools.partial(mask_kernel, chunks // 2),
        out_shape=out,
        grid_spec=pltpu.PrefetchScalarGridSpec(
            num_scalar_prefetch=1,
            grid=(1,),
            in_specs=[pl.BlockSpec((rows, 1), lambda i, c: (half, 0))]
            + [chunk_spec(value, chunks, k) for k in range(first, first + chunks // 2)]
            + unread(deps),
            out_specs=whole_spec(out),
        ),
        compiler_params=kernel_params(1),
        cost_estimate=spent(4),
        name="mask_padding",
    )(scalars, place, *[value] * (chunks // 2), *deps)


def pass_on_kernel(value, *refs):
    refs[-1][...] = value[...]


def pass_on(value, deps):
    return pl.pallas_call(
        pass_on_kernel,
        out_shape=jax.ShapeDtypeStruct(value.shape, value.dtype),
        grid=(1,),
        in_specs=[whole_spec(value)] + unread(deps),
        out_specs=whole_spec(value),
        compiler_params=kernel_params(1),
        cost_estimate=spent(2),
        name="pass_on",
    )(value, *deps)


def corner_kernel(value, out):
    out[...] = value[...]


def corner(value):
    return pl.pallas_call(
        corner_kernel,
        out_shape=jax.ShapeDtypeStruct((16, 128), value.dtype),
        grid=(1,),
        in_specs=[pl.BlockSpec((16, 128), lambda i: (0, 0))],
        out_specs=pl.BlockSpec((16, 128), lambda i: (0, 0)),
        compiler_params=kernel_params(1),
        cost_estimate=spent(5),
        name="corner",
    )(value)


def fill_other_kernel(pieces, core, *refs):
    step = pl.program_id(0)
    for k in range(pieces):

        @pl.when(step // (STEPS // pieces) == k)
        def _():
            refs[-1][...] = refs[k][...].astype(F32).reshape(refs[-1].shape)


def fill_other(core, others, index, held, dim, deps=()):
    pieces = len(others)
    share = STEPS // pieces
    rows, n = others[0].shape[1] // share, others[0].shape[2]
    if dim == 0:
        place = lambda i, c: ((1 - c[0]) * STEPS + i, 0)
    else:
        place = lambda i, c: (i, 1 - c[0])

    def piece(k):
        last = share - 1
        return pl.BlockSpec(
            (1, rows, n), lambda i, c: (index, jnp.clip(i - k * share, 0, last), 0)
        )

    return pl.pallas_call(
        functools.partial(fill_other_kernel, pieces),
        out_shape=jax.ShapeDtypeStruct(held.shape, F32),
        grid_spec=pltpu.PrefetchScalarGridSpec(
            num_scalar_prefetch=1,
            grid=(STEPS,),
            in_specs=[piece(k) for k in range(pieces)]
            + [pl.BlockSpec(memory_space=pl.ANY)]
            + unread(deps),
            out_specs=pl.BlockSpec((rows, n), place),
        ),
        input_output_aliases={1 + pieces: 0},
        compiler_params=kernel_params(1),
        cost_estimate=spent(87),
        name="fill_other",
    )(core, *others, held, *deps)


def rotate_block(values, cosine, sine):
    width = values.shape[1]
    column = lax.broadcasted_iota(jnp.int32, values.shape, 1)
    other = jnp.where(
        column % HEAD_SIZE < HEAD_SIZE // 2,
        pltpu.roll(values, width - HEAD_SIZE // 2, 1),
        pltpu.roll(values, HEAD_SIZE // 2, 1),
    )
    return values * cosine + other * sine


def pack_rotated(keys, values, cosine, sine):
    width = keys.shape[1]
    if width % 128 == 0:
        turned = [
            rotate_block(keys[:, i : i + 128], cosine, sine) for i in range(0, width, 128)
        ]
        return jnp.concatenate(turned + [values], axis=1)
    both = jnp.concatenate([keys, values], axis=1)
    column = lax.broadcasted_iota(jnp.int32, both.shape, 1)
    return jnp.where(column < width, rotate_block(both, cosine, sine), both)


def chunk_spec(array, chunks, k):
    block = (array.shape[0] // chunks, array.shape[1])
    return pl.BlockSpec(block, lambda *a: (a[-1][0] ^ k, 0))


def project_kv_kernel(chunks, waits, me, *refs):
    gain, key_w, value_w, cosine, sine = refs[chunks : chunks + 5]
    normed, inverse, packed = refs[-3:]
    stream = join(refs[:chunks]).astype(F32)
    scale = lax.rsqrt(jnp.mean(stream * stream, axis=1, keepdims=True) + EPSILON)
    low = (stream * scale * gain[...]).astype(BF)
    normed[...] = low
    inverse[...] = jnp.broadcast_to(scale, inverse.shape)
    packed[...] = pack_rotated(
        contract(low, key_w[...], 1, 0), contract(low, value_w[...], 1, 0), cosine[...], sine[...]
    ).astype(BF)


def project_kv(me, x, gain, key_matrix, value_matrix, cosine, sine, chunks, deps=()):
    span, depth = x.shape
    args = (gain, key_matrix, value_matrix, cosine, sine)
    outs = (
        jax.ShapeDtypeStruct((span, depth), BF),
        jax.ShapeDtypeStruct((span, 128), F32),
        jax.ShapeDtypeStruct((span, 2 * key_matrix.shape[1]), BF),
    )
    return pl.pallas_call(
        functools.partial(project_kv_kernel, chunks, len(deps)),
        out_shape=outs,
        grid_spec=pltpu.PrefetchScalarGridSpec(
            num_scalar_prefetch=1,
            grid=(1,),
            in_specs=[chunk_spec(x, chunks, k) for k in range(chunks)]
            + [whole_spec(a) for a in args]
            + unread(deps),
            out_specs=tuple(whole_spec(a) for a in outs),
        ),
        compiler_params=kernel_params(1),
        cost_estimate=spent(4),
        name="project_kv",
    )(me, *[x] * chunks, *args, *deps)


def project_query_kernel(normed, weight, cosine, sine, *refs):
    out = refs[-1]
    lin = contract(normed[...], weight[...], 1, 0)
    for i in range(0, lin.shape[1], 128):
        turned = rotate_block(lin[:, i : i + 128], cosine[...], sine[...])
        out[:, i : i + 128] = (turned * HEAD_SIZE**-0.5).astype(BF)


def project_query(normed, w_query, cosine, sine, deps=()):
    span, depth = normed.shape
    width = w_query.shape[1]
    cols = 256
    return pl.pallas_call(
        project_query_kernel,
        out_shape=jax.ShapeDtypeStruct((span, width), BF),
        grid=(width // cols,),
        in_specs=[
            whole_spec(normed),
            pl.BlockSpec((depth, cols), lambda j: (0, j)),
            whole_spec(cosine),
            whole_spec(sine),
        ]
        + unread(deps),
        out_specs=pl.BlockSpec((span, cols), lambda j: (0, j)),
        compiler_params=kernel_params(1),
        cost_estimate=spent(4),
        name="project_query",
    )(normed, w_query, cosine, sine, *deps)


def head_columns(array, index):
    return array[:, index * HEAD_SIZE : (index + 1) * HEAD_SIZE]


def stack_heads(array, heads):
    return jnp.concatenate([head_columns(array, h) for h in heads], axis=0)


def store_heads(out, turned, first, span, finish):
    for i in range(0, turned.shape[1] // span, 2):
        pair = jnp.concatenate(
            [turned[:, (i + e) * span : (i + e + 1) * span] for e in range(2)], axis=0
        )
        at = (first + i) * HEAD_SIZE
        out[:, at : at + 128] = finish(jnp.transpose(pair)).astype(BF)


def attend_kernel(blocks, chunks, shift, query, place, place_row, begin_row, w_output, *refs):
    packed = refs[:blocks]
    attended, stats, *parts = refs[-2 - chunks :]
    span, width = query.shape
    heads_kv = packed[0].shape[1] // (2 * HEAD_SIZE)
    group = width // HEAD_SIZE // heads_kv
    last = jnp.concatenate([place_row[...]] * group, axis=1)
    first = jnp.concatenate([begin_row[...]] * group, axis=1)
    for g in range(heads_kv):
        q = stack_heads(query, range(g * group, (g + 1) * group))
        top = total = mixed = None
        for j in range(blocks):
            keys = head_columns(packed[j], g)
            values = head_columns(packed[j], heads_kv + g)
            key_place = place[...] + shift[j]
            allowed = (key_place >= first) & (key_place <= last)
            masked = jnp.where(allowed, contract(keys, q, 1, 1), -1e30)
            peak = jnp.max(masked, axis=0, keepdims=True)
            peak = peak if j == 0 else jnp.maximum(top, peak)
            terms = jnp.exp(masked - peak)
            amount = jnp.sum(terms, axis=0, keepdims=True)
            term = contract(values, terms.astype(BF), 0, 0)
            if j == 0:
                total, mixed = amount, term
            else:
                fade = jnp.exp(top - peak)
                total, mixed = total * fade + amount, mixed * fade + term
            top = peak
        stats[g : g + 1, :] = top + jnp.log(total)
        store_heads(attended, mixed * (1.0 / total), g * group, span, lambda v: v)
    part = contract(attended[...], w_output[...], 1, 0)
    chunk = span // len(parts)
    for k, out in enumerate(parts):
        out[...] = part[k * chunk : (k + 1) * chunk].astype(BF)


def attend(shift, query, packed, places, w_output, chunks, deps=()):
    span, width = query.shape
    depth = w_output.shape[1]
    blocks = len(packed)
    heads_kv = packed[0].shape[1] // (2 * HEAD_SIZE)
    args = (
        query,
        *places,
        w_output,
        *packed,
    )
    outs = (
        jax.ShapeDtypeStruct((span, width), BF),
        jax.ShapeDtypeStruct((heads_kv, width // HEAD_SIZE // heads_kv * span), F32),
    )
    outs += (jax.ShapeDtypeStruct((span // chunks, depth), BF),) * chunks
    out = pl.pallas_call(
        functools.partial(attend_kernel, blocks, chunks),
        out_shape=outs,
        grid_spec=pltpu.PrefetchScalarGridSpec(
            num_scalar_prefetch=1,
            grid=(1,),
            in_specs=[whole_spec(a) for a in args] + unread(deps),
            out_specs=tuple(whole_spec(a) for a in outs),
        ),
        compiler_params=kernel_params(1),
        cost_estimate=spent(11),
        name="attend",
    )(shift, *args, *deps)
    return out[0], out[1], list(out[2:])


def sum_chunks(refs):
    total = refs[0][...].astype(F32)
    for ref in refs[1:]:
        total = total + ref[...].astype(F32)
    return total


def middle_kernel(count, me, x, gain, *refs):
    chunks, (middle, inverse, normed) = refs[:count], refs[-3:]
    stream = x[...].astype(F32) + sum_chunks(chunks)
    scale = lax.rsqrt(jnp.mean(stream * stream, axis=1, keepdims=True) + EPSILON)
    middle[...] = stream
    inverse[...] = jnp.broadcast_to(scale, inverse.shape)
    normed[...] = (stream * scale * gain[...]).astype(BF)


def middle_norm(me, x, gain, chunks, deps=()):
    rows, depth = chunks[0].shape
    outs = (
        jax.ShapeDtypeStruct((rows, depth), F32),
        jax.ShapeDtypeStruct((rows, 128), F32),
        jax.ShapeDtypeStruct((rows, depth), BF),
    )
    return pl.pallas_call(
        functools.partial(middle_kernel, len(chunks)),
        out_shape=outs,
        grid_spec=pltpu.PrefetchScalarGridSpec(
            num_scalar_prefetch=1,
            grid=(1,),
            in_specs=[chunk_spec(x, len(chunks), 0)]
            + [whole_spec(a) for a in (gain, *chunks)]
            + unread(deps),
            out_specs=tuple(whole_spec(a) for a in outs),
        ),
        compiler_params=kernel_params(1),
        cost_estimate=spent(120),
        name="middle_norm",
    )(me, x, gain, *chunks, *deps)


def halves_kernel(count, *refs):
    half = count // 2
    refs[-2][...] = join(refs[:half])
    refs[-1][...] = join(refs[half:count])


def join_halves(chunks, deps=()):
    rows, depth = chunks[0].shape
    outs = (jax.ShapeDtypeStruct((rows * len(chunks) // 2, depth), BF),) * 2
    return pl.pallas_call(
        functools.partial(halves_kernel, len(chunks)),
        out_shape=outs,
        grid=(1,),
        in_specs=[whole_spec(a) for a in chunks] + unread(deps),
        out_specs=tuple(whole_spec(a) for a in outs),
        compiler_params=kernel_params(1),
        cost_estimate=spent(2),
        name="join_halves",
    )(*chunks, *deps)


def norm_gradient(grad, rows, scale, gain):
    scaled = grad * gain
    product = jnp.mean(scaled * rows, axis=1, keepdims=True)
    gain_grad = jnp.sum(grad * rows * scale, axis=0, keepdims=True)
    return scale * scaled - rows * (scale * scale * scale * product), gain_grad


def norm_back_kernel(count, upstream, middle, inverse, gain, *refs):
    chunks, (wide, low, gain_grad) = refs[:count], refs[-3:]
    grad, gain_grad[...] = norm_gradient(
        sum_chunks(chunks), middle[...], inverse[:, :1], gain[...]
    )
    total = upstream[...].astype(F32) + grad
    wide[...] = total
    low[...] = total.astype(BF)


def norm_back(upstream, middle, inverse, gain, chunks, deps=()):
    rows, depth = middle.shape
    args = (middle, inverse, gain, *chunks)
    outs = (
        jax.ShapeDtypeStruct((rows, depth), F32),
        jax.ShapeDtypeStruct((rows, depth), BF),
        jax.ShapeDtypeStruct((1, depth), F32),
    )
    return pl.pallas_call(
        functools.partial(norm_back_kernel, len(chunks)),
        out_shape=outs,
        grid=(1,),
        in_specs=[pl.BlockSpec((rows, depth), lambda i: (0, 0))]
        + [whole_spec(a) for a in args]
        + unread(deps),
        out_specs=tuple(whole_spec(a) for a in outs),
        compiler_params=kernel_params(1),
        cost_estimate=spent(3),
        name="norm_back",
    )(upstream, *args, *deps)


def finish_kernel(count, me, x, inverse, gain, grad_middle, block, *refs):
    grad, _ = norm_gradient(
        sum_chunks(refs[:count]), x[...].astype(F32), inverse[:, :1], gain[...]
    )
    refs[-1][...] = jnp.concatenate([grad_middle[...] + grad, block[...]], axis=0).astype(BF)


def finish(me, x, inverse, gain, grad_middle, block, chunks, deps=()):
    rows, depth = grad_middle.shape
    args = (gain, grad_middle, block, *chunks)
    outs = jax.ShapeDtypeStruct((2 * rows, depth), BF)
    return pl.pallas_call(
        functools.partial(finish_kernel, len(chunks)),
        out_shape=outs,
        grid_spec=pltpu.PrefetchScalarGridSpec(
            num_scalar_prefetch=1,
            grid=(1,),
            in_specs=[
                chunk_spec(x, len(chunks), 0),
                pl.BlockSpec((rows, 128), lambda i, c: (0, 0)),
            ]
            + [whole_spec(a) for a in args]
            + unread(deps),
            out_specs=whole_spec(outs),
        ),
        compiler_params=kernel_params(1),
        cost_estimate=spent(3),
        name="finish",
    )(me, x, inverse, *args, *deps)


def add_kernel(count, *refs):
    refs[-1][...] = sum_chunks(refs[:count]).astype(refs[-1].dtype)


def add_up(arrays, dtype, deps=()):
    out = jax.ShapeDtypeStruct(arrays[0].shape, dtype)
    return pl.pallas_call(
        functools.partial(add_kernel, len(arrays)),
        out_shape=out,
        grid=(1,),
        in_specs=[whole_spec(a) for a in arrays] + unread(deps),
        out_specs=whole_spec(out),
        compiler_params=kernel_params(1),
        cost_estimate=spent(2),
        name="add_up",
    )(*arrays, *deps)


def restore_kernel(count, me, *refs):
    step = pl.program_id(0)
    for k in range(count):

        @pl.when(step == k)
        def _():
            rows = refs[k].shape[0] // 2
            refs[-2][...] = refs[k][:rows]
            refs[-1][...] = refs[k][rows:]


def restore(me, pieces, deps=()):
    count = len(pieces)
    rows, depth = pieces[0].shape[0] // 2, pieces[0].shape[1]
    if rows % 16:
        halves = [[p[:rows] for p in pieces], [p[rows:] for p in pieces]]
        return [reorder(jnp.concatenate(h, axis=0), "tensor") for h in halves]
    out = jax.ShapeDtypeStruct((count * rows, depth), BF)
    place = pl.BlockSpec((rows, depth), lambda i, c: (c[0] ^ i, 0))
    return pl.pallas_call(
        functools.partial(restore_kernel, count),
        out_shape=(out, out),
        grid_spec=pltpu.PrefetchScalarGridSpec(
            num_scalar_prefetch=1,
            grid=(count,),
            in_specs=[whole_spec(p) for p in pieces] + unread(deps),
            out_specs=(place, place),
        ),
        compiler_params=kernel_params(1),
        cost_estimate=spent(87),
        name="restore",
    )(me, *pieces, *deps)


def widen(wo, wq, wkv, width, deps=()):
    steps = 4
    depth = wq.shape[0]
    shapes = [wo.shape, wq.shape, (depth, width), (depth, width)]

    def spec(shape):
        return pl.BlockSpec((shape[0] // steps, shape[1]), lambda i: (i, 0))

    def kernel(wo, wq, wkv, *refs):
        wo_out, wq_out, wk_out, wv_out, gains = refs[-5:]
        wo_out[...] = wo[...].astype(F32)
        wq_out[...] = wq[...].astype(F32)
        turned = jnp.transpose(wkv[: 2 * width, :].astype(F32))
        wk_out[...] = turned[:, :width]
        wv_out[...] = turned[:, width:]
        gains[...] = wkv[2 * width :, :].astype(F32)[:8]

    return pl.pallas_call(
        kernel,
        out_shape=tuple(jax.ShapeDtypeStruct(v, F32) for v in [*shapes, (8, depth)]),
        grid=(steps,),
        in_specs=[
            spec(wo.shape),
            spec(wq.shape),
            pl.BlockSpec((wkv.shape[0], depth // steps), lambda i: (0, i)),
        ]
        + unread(deps),
        out_specs=tuple(spec(v) for v in shapes)
        + (pl.BlockSpec((8, depth // steps), lambda i: (0, i)),),
        compiler_params=kernel_params(1),
        cost_estimate=spent(8),
        name="widen",
    )(wo, wq, wkv, *deps)


def gain_sum_kernel(count, *refs):
    total = sum_chunks(refs[:count])
    refs[-2][...] = total[:1]
    refs[-1][...] = total[1:2]


def gain_sum(pieces, deps=()):
    out = jax.ShapeDtypeStruct((1, pieces[0].shape[1]), F32)
    return pl.pallas_call(
        functools.partial(gain_sum_kernel, len(pieces)),
        out_shape=(out, out),
        grid=(1,),
        in_specs=[whole_spec(p) for p in pieces] + unread(deps),
        out_specs=(whole_spec(out), whole_spec(out)),
        compiler_params=kernel_params(1),
        cost_estimate=spent(2),
        name="gain_sum",
    )(*pieces, *deps)


def attend_back_kernel(blocks, count, shift, query, attended, stats, place, place_row, begin_row,
                       cosine, sine, w_output, *refs):
    packed = refs[:blocks]
    chunks = refs[blocks : blocks + count]
    grad_query = refs[-1 - blocks]
    terms = refs[-blocks:]
    span, width = query.shape
    heads_kv = packed[0].shape[1] // (2 * HEAD_SIZE)
    group = width // HEAD_SIZE // heads_kv
    grad_middle = join(chunks)
    grad_attended = contract(grad_middle, w_output[...], 1, 1).astype(BF)
    last = jnp.concatenate([place_row[...]] * group, axis=1)
    first = jnp.concatenate([begin_row[...]] * group, axis=1)
    key_terms = [[] for _ in range(blocks)]
    value_terms = [[] for _ in range(blocks)]
    for g in range(heads_kv):
        mine = range(g * group, (g + 1) * group)
        q = stack_heads(query, mine)
        grad = stack_heads(grad_attended, mine)
        norm = stats[g : g + 1, :]
        inner = lax.dot_general(
            jnp.ones((8, HEAD_SIZE), F32),
            grad.astype(F32) * stack_heads(attended, mine).astype(F32),
            (((1,), (1,)), ((), ())),
            preferred_element_type=F32,
            precision=lax.Precision.HIGHEST,
        )[:1]
        total = None
        for j in range(blocks):
            keys = head_columns(packed[j], g)
            values = head_columns(packed[j], heads_kv + g)
            key_place = place[...] + shift[j]
            allowed = (key_place >= first) & (key_place <= last)
            scores = contract(keys, q, 1, 1)
            probs = jnp.exp(jnp.where(allowed, scores - norm, -1e30))
            grad_scores = (probs * (contract(values, grad, 1, 1) - inner)).astype(BF)
            value_terms[j].append(contract(probs.astype(BF), grad, 1, 0))
            key_terms[j].append(contract(grad_scores, q, 1, 0))
            term = contract(keys, grad_scores, 0, 0)
            total = term if total is None else total + term
        store_heads(
            grad_query,
            total,
            g * group,
            span,
            lambda v: rotate_block(v * HEAD_SIZE**-0.5, cosine[...], -sine[...]),
        )
    for j in range(blocks):
        terms[j][...] = jnp.concatenate(key_terms[j] + value_terms[j], axis=1).astype(BF)


def attend_back(shift, query, attended, stats, packed, places, cosine, sine, w_output, chunks,
                deps=()):
    span, width = query.shape
    blocks = len(packed)
    args = (
        query,
        attended,
        stats,
        *places,
        cosine,
        sine,
        w_output,
        *packed,
        *chunks,
    )
    outs = (jax.ShapeDtypeStruct((span, width), BF),)
    outs += (jax.ShapeDtypeStruct(packed[0].shape, BF),) * blocks
    out = pl.pallas_call(
        functools.partial(attend_back_kernel, blocks, len(chunks)),
        out_shape=outs,
        grid_spec=pltpu.PrefetchScalarGridSpec(
            num_scalar_prefetch=1,
            grid=(1,),
            in_specs=[whole_spec(a) for a in args] + unread(deps),
            out_specs=tuple(whole_spec(a) for a in outs),
        ),
        compiler_params=kernel_params(1),
        cost_estimate=spent(16),
        name="attend_back",
    )(shift, *args, *deps)
    return out[0], list(out[1:])


def input_back_kernel(
    count, chunks, me, grad_query, w_query, key_w, value_w, cosine, sine, inverse, gain_two, *refs
):
    terms, rows = refs[:count], refs[count : count + chunks]
    lin, gains, *parts = refs[-2 - chunks :]
    normed = join(rows).astype(F32) * inverse[:, :1]
    width = key_w.shape[1]
    total = sum_chunks(terms)
    low = pack_rotated(total[:, :width], total[:, width:], cosine[...], -sine[...]).astype(BF)
    lin[...] = low
    part = contract(grad_query[...], w_query[...], 1, 1)
    part = part + contract(low[:, :width], key_w[...], 1, 1)
    part = part + contract(low[:, width:], value_w[...], 1, 1)
    rows = part.shape[0] // chunks
    for k, out in enumerate(parts):
        out[...] = part[k * rows : (k + 1) * rows].astype(BF)
    gain_one = jnp.sum(part * normed, axis=0, keepdims=True)
    empty = jnp.zeros((6, part.shape[1]), F32)
    gains[...] = jnp.concatenate([gain_one, gain_two[...], empty], axis=0)


def input_back(
    me,
    grad_query,
    w_query,
    key_matrix,
    value_matrix,
    cosine,
    sine,
    inverse,
    x,
    gain_two,
    terms,
    chunks,
    deps=(),
):
    span = grad_query.shape[0]
    depth = w_query.shape[0]
    args = (grad_query, w_query, key_matrix, value_matrix, cosine, sine, inverse, gain_two)
    args += tuple(terms)
    outs = (
        jax.ShapeDtypeStruct(terms[0].shape, BF),
        jax.ShapeDtypeStruct((8, depth), F32),
    )
    outs += (jax.ShapeDtypeStruct((span // chunks, depth), BF),) * chunks
    out = pl.pallas_call(
        functools.partial(input_back_kernel, len(terms), chunks),
        out_shape=outs,
        grid_spec=pltpu.PrefetchScalarGridSpec(
            num_scalar_prefetch=1,
            grid=(1,),
            in_specs=[whole_spec(a) for a in args]
            + [chunk_spec(x, chunks, k) for k in range(chunks)]
            + unread(deps),
            out_specs=tuple(whole_spec(a) for a in outs),
        ),
        compiler_params=kernel_params(1),
        cost_estimate=spent(1),
        name="input_back",
    )(me, *args, *[x] * chunks, *deps)
    return out[0], out[1], list(out[2:])


def rope_tables(positions):
    expo = np.arange(HEAD_SIZE // 2, dtype=np.float64) * 2.0 / HEAD_SIZE
    inverse = 1.0 / 500000.0**expo
    wavelength = 2.0 * np.pi / inverse
    smooth = (8192.0 / wavelength - 1.0) / 3.0
    middle = (1.0 - smooth) * inverse / 32.0 + smooth * inverse
    scaled = np.where(
        wavelength < 2048.0, inverse, np.where(wavelength > 8192.0, inverse / 32.0, middle)
    )
    scaled = jnp.asarray(np.tile(scaled, 4)[None, :].astype(np.float32))
    sign = jnp.asarray(np.tile(np.repeat([-1.0, 1.0], HEAD_SIZE // 2), 2)[None, :].astype(np.float32))
    angles = positions.astype(F32)[:, None] * scaled
    return jnp.cos(angles), jnp.sin(angles) * sign


def flip(value, axis, mask):
    return lax.ppermute(value, axis, [(i, i ^ mask) for i in range(lax.axis_size(axis))])


def reorder(value, axis):
    n = lax.axis_size(axis)
    me = lax.axis_index(axis)
    chunk = value.shape[0] // n
    return jnp.concatenate(
        [lax.dynamic_slice_in_dim(value, (me ^ k) * chunk, chunk, 0) for k in range(n)], axis=0
    )


def exchange(chunks, axis):
    return chunks[:1] + [flip(chunks[k], axis, k) for k in reversed(range(1, len(chunks)))]


def spread(chunk, axis):
    return [chunk] + [flip(chunk, axis, k) for k in range(1, lax.axis_size(axis))]


def gather_halves(first, second):
    return [
        lax.all_gather(first, ("rows", "seq"), axis=0, tiled=True),
        lax.all_gather(second, ("seq", "rows"), axis=0, tiled=True),
    ]


def per_device(
    activations,
    doc_lengths,
    w_query,
    key_matrix,
    value_matrix,
    w_output,
    w_gate,
    w_up,
    w_down,
    gain_attn,
    gain_ffn,
    cotangent,
):
    span = activations.shape[1]
    blocks = lax.axis_size("seq")
    chunks = lax.axis_size("tensor")
    chunk = span // chunks
    core = lax.axis_index("rows").astype(jnp.int32).reshape(1)
    block_here = lax.axis_index("seq")
    gain_attn = gain_attn.reshape(1, -1)
    gain_ffn = gain_ffn.reshape(1, -1)
    stream, cotangent = activations[0], cotangent[0]
    me = lax.axis_index("tensor").astype(jnp.int32)
    token = jnp.arange(span, dtype=jnp.int32)
    place = block_here * span + (me ^ (token // chunk)) * chunk + token % chunk
    if chunk % 16:
        stream, cotangent = reorder(stream, "tensor"), reorder(cotangent, "tensor")
        me = jnp.zeros_like(me)
    order = jnp.arange(DOCS, dtype=jnp.int32)
    ends = jnp.sum(jnp.where(order[None, :] <= order[:, None], doc_lengths[0][None, :], 0), axis=1)
    begin = jnp.max(jnp.where(place[:, None] >= ends[None, :], ends[None, :], 0), axis=1)
    cosine, sine = rope_tables(place - begin)
    shift = jnp.stack([((block_here ^ j) - block_here) * span for j in range(blocks)])
    shift = shift.astype(jnp.int32)
    scalars = jnp.stack([me, ends[-1].astype(jnp.int32)])
    places = (place.reshape(span, 1), place.reshape(1, span), begin.reshape(1, span))

    normed_one, inverse_one, packed = project_kv(
        scalars, stream, gain_attn, key_matrix, value_matrix, cosine, sine, chunks, (shift, *places)
    )
    packed = spread(packed, "seq")
    query = project_query(normed_one, w_query, cosine, sine)
    upstream = [mask_padding(scalars, cotangent, places[0], chunks, 0, (query, *packed))]
    upstream_all = [lax.all_gather(upstream[0], ("rows", "seq"), axis=0, tiled=True)]
    attended, stats, parts = attend(
        shift, query, packed, places, w_output, chunks, (upstream[0],)
    )
    upstream.append(mask_padding(scalars, cotangent, places[0], chunks, 1, (parts[0],)))
    upstream_all.append(lax.all_gather(upstream[1], ("seq", "rows"), axis=0, tiled=True))

    sent = exchange(parts, "tensor")
    grad_hidden = grad_hidden_of(core, upstream, w_down, 1, (parts[0],))
    middle, inverse_two, normed = middle_norm(scalars, stream, gain_ffn, sent, (grad_hidden,))

    grad_hidden_first = grad_hidden_of(core, upstream_all[:1], w_down, 2, (middle,))
    normed = join_halves(spread(normed, "tensor"), (grad_hidden_first,))
    normed_all = gather_halves(*normed)
    hidden, parts = feed_own(normed, w_gate, w_up, grad_hidden, chunks)

    sent = exchange(parts, "tensor")
    grad_hidden_second = grad_hidden_of(core, upstream_all[1:], w_down, 2, (parts[0],))
    grad_middle, grad_middle_low, gain_two = norm_back(
        upstream[0], middle, inverse_two, gain_ffn, sent, (grad_hidden_second,)
    )
    grad_middle_all = spread(grad_middle_low, "tensor")
    feed_first = feed_half(
        core, normed_all[0], w_gate, w_up, grad_hidden_first, (grad_middle,)
    )
    down_parts = down_projection(hidden, w_down, (feed_first[0],))
    down_send = pass_on(down_parts[1], grad_middle_all)
    grad_query, kv_terms = attend_back(
        shift,
        query,
        attended,
        stats,
        packed,
        places,
        cosine,
        sine,
        w_output,
        grad_middle_all,
        (corner(down_send),),
    )
    mask = chunks // 2
    down_came = flip(down_send, "tensor", mask)

    kv_sent = exchange(kv_terms, "seq")
    wq_part = left_product(normed_one, [grad_query])
    wo_part = left_product(attended, grad_middle_all, (wq_part,))
    grad_kv, gains, parts = input_back(
        scalars,
        grad_query,
        w_query,
        key_matrix,
        value_matrix,
        cosine,
        sine,
        inverse_one,
        stream,
        gain_two,
        kv_sent,
        chunks,
        (wo_part, normed_all[1]),
    )

    wkv_part = kv_product(normed_one, grad_kv, [gains])
    sent = exchange(parts, "tensor")
    grad_wo, grad_wq, grad_wkv = lax.psum((wo_part, wq_part, wkv_part), ("rows", "seq"))
    keep, send = add_half(down_parts[0], down_came, (wkv_part,))
    while mask > 2:
        mask //= 2
        keep, send = add_half(keep, flip(send, "tensor", mask))
    feed_second = feed_half(
        core, normed_all[1], w_gate, w_up, grad_hidden_second, (keep,)
    )
    hidden_all, grad_gate_all, grad_up_all = zip(feed_first, feed_second)
    grad_down, low = weight_grad(core, hidden_all, upstream_all, 0, 2)
    down_other = [flip(v[None], "rows", 1) for v in low]
    block_chunk = add_up(
        [middle, keep, flip(send, "tensor", mask // 2)], F32, (grad_down,)
    )
    both = finish(
        scalars, stream, inverse_one, gain_attn, grad_middle, block_chunk, sent
    )
    both_all = spread(both, "tensor")
    grad_gate_w, grad_up_w, *low = pair_grad(
        core, normed_all, grad_gate_all, grad_up_all, (both,)
    )
    gate_other, up_other = [flip(v, "rows", 1) for v in low]
    grad_down = fill_other(core, down_other, 0, grad_down, 0, (grad_up_w,))
    grad_gate_w = fill_other(core, [gate_other], 0, grad_gate_w, 1, (grad_down,))
    grad_wo, grad_wq, grad_wk, grad_wv, gains = widen(
        grad_wo, grad_wq, grad_wkv, key_matrix.shape[1], (grad_gate_w,)
    )
    grad_input, block_output = restore(scalars, both_all, (grad_wo,))
    gains = pass_on(gains, (grad_input,))
    grad_up_w = fill_other(core, [up_other], 0, grad_up_w, 1, (gains,))
    gains = gain_sum(spread(gains, "tensor"), (grad_up_w,))
    return (
        block_output[None],
        grad_input[None],
        grad_wq,
        grad_wk,
        grad_wv,
        grad_wo,
        grad_gate_w,
        grad_up_w,
        grad_down,
        gains[0].reshape(-1),
        gains[1].reshape(-1),
    )


def solution(mesh):
    placed = (
        P("rows", "seq", None),
        P("rows", None),
        P(None, "tensor"),
        P(None, "tensor"),
        P(None, "tensor"),
        P("tensor", None),
        P(None, "tensor"),
        P(None, "tensor"),
        P("tensor", None),
        P(),
        P(),
        P("rows", "seq", None),
    )
    return jax.shard_map(
        per_device,
        mesh=mesh,
        in_specs=placed,
        out_specs=(
            P("rows", "seq", None),
            P("rows", "seq", None),
            P(None, "tensor"),
            P(None, "tensor"),
            P(None, "tensor"),
            P("tensor", None),
            P(None, "tensor"),
            P(None, "tensor"),
            P("tensor", None),
            P(),
            P(),
        ),
        check_vma=False,
    )
```

```python
import functools

import jax
import jax.numpy as jnp
from jax import lax
from jax.experimental import pallas as pl
from jax.experimental.pallas import tpu as pltpu
import numpy as np
from jax.sharding import PartitionSpec as P

HEAD_SIZE = 64
DOCS = 4
EPSILON = 1e-05
BF = jnp.bfloat16
F32 = jnp.float32


MIB = 1 << 20


def kernel_params(dims):
    return pltpu.CompilerParams(
        vmem_limit_bytes=64 * MIB - 32768, dimension_semantics=("arbitrary",) * dims
    )


def contract(a, b, dim_a, dim_b):
    return lax.dot_general(
        a, b, (((dim_a,), (dim_b,)), ((), ())), preferred_element_type=F32
    )


def tile(limit, size):
    while size > limit and size % 2 == 0:
        size //= 2
    return size


SMALL = pl.CostEstimate(flops=1, bytes_accessed=1, transcendentals=0)


def spent(us):
    return pl.CostEstimate(flops=us * 10**9, bytes_accessed=1, transcendentals=0)


def whole_spec(array):
    shape = array.shape
    return pl.BlockSpec(shape, lambda *_: (0,) * len(shape))


def join(refs):
    if refs[0].shape[0] % 16 == 0:
        return jnp.concatenate([r[...] for r in refs], axis=0)
    return jnp.concatenate([r[...].astype(F32) for r in refs], axis=0).astype(refs[0].dtype)


def unread(deps):
    return [pl.BlockSpec(memory_space=pl.ANY)] * len(deps)


def times_transposed_kernel(count, core, weight, *refs):
    refs[-1][...] = contract(join(refs[:count]), weight[...], 1, 1).astype(BF)


def grad_hidden_of(core, pieces, w_down, shares, deps=()):
    count = len(pieces)
    tokens, depth = pieces[0].shape
    units = w_down.shape[0] // shares
    rows, cols = tile(640, tokens), tile(1024 // (3 - shares), units)
    steps = units // cols
    offset = steps * (shares - 1)
    return pl.pallas_call(
        functools.partial(times_transposed_kernel, count),
        out_shape=jax.ShapeDtypeStruct((count * tokens, units), BF),
        grid_spec=pltpu.PrefetchScalarGridSpec(
            num_scalar_prefetch=1,
            grid=(steps, tokens // rows),
            in_specs=[pl.BlockSpec((cols, depth), lambda j, i, c: (c[0] * offset + j, 0))]
            + [pl.BlockSpec((rows, depth), lambda j, i, c: (i, 0))] * count
            + unread(deps),
            out_specs=pl.BlockSpec((count * rows, cols), lambda j, i, c: (i, j)),
        ),
        compiler_params=kernel_params(2),
        cost_estimate=spent(10),
        name="grad_hidden_of",
    )(core, w_down, *pieces, *deps)


def swish_grads(gate, up_proj, grad_hidden):
    sigmoid = 1.0 / (1.0 + jnp.exp(-gate))
    activated = gate * sigmoid
    hidden = (activated * up_proj).astype(BF)
    grad_gate = (grad_hidden * up_proj * (sigmoid * (1.0 + gate * (1.0 - sigmoid)))).astype(BF)
    grad_up = (grad_hidden * activated).astype(BF)
    return hidden, grad_gate, grad_up


def feed_half_kernel(core, normed, gate_w, up_w, grad_hidden, *refs):
    hidden, grad_gate, grad_up = refs[-3:]
    rows = normed[...]
    hidden[...], grad_gate[...], grad_up[...] = swish_grads(
        contract(rows, gate_w[...], 1, 0),
        contract(rows, up_w[...], 1, 0),
        grad_hidden[...].astype(F32),
    )


def feed_half(core, normed, w_gate, w_up, grad_hidden, deps=()):
    tokens, depth = normed.shape
    half = w_gate.shape[1] // 2
    rows, cols = tile(640, tokens), tile(512, half)
    steps = half // cols
    out = jax.ShapeDtypeStruct((tokens, half), BF)
    weight = pl.BlockSpec((depth, cols), lambda j, i, c: (0, c[0] * steps + j))
    block = pl.BlockSpec((rows, cols), lambda j, i, c: (i, j))
    return pl.pallas_call(
        feed_half_kernel,
        out_shape=(out, out, out),
        grid_spec=pltpu.PrefetchScalarGridSpec(
            num_scalar_prefetch=1,
            grid=(steps, tokens // rows),
            in_specs=[
                pl.BlockSpec((rows, depth), lambda j, i, c: (i, 0)),
                weight,
                weight,
                block,
            ]
            + unread(deps),
            out_specs=(block, block, block),
        ),
        compiler_params=kernel_params(2),
        cost_estimate=spent(18),
        name="feed_half",
    )(core, normed, w_gate, w_up, grad_hidden, *deps)


def feed_own_kernel(pieces, chunks, gate_w, up_w, grad_hidden, *refs):
    normed = refs[:pieces]
    hidden, parts = refs[-chunks - 3], refs[-chunks - 2 : -2]
    rows, total = refs[-2:]
    step = pl.program_id(0)
    size = total.shape[0] // chunks

    @pl.when(step == 0)
    def _():
        rows[...] = join(normed)

    gate_now = gate_w[...]
    up_now = up_w[...]
    hidden[...], grad_gate, grad_up = swish_grads(
        contract(rows[...], gate_now, 1, 0),
        contract(rows[...], up_now, 1, 0),
        grad_hidden[...].astype(F32),
    )
    term = contract(grad_gate, gate_now, 1, 1) + contract(grad_up, up_now, 1, 1)

    @pl.when(step == 0)
    def _():
        total[...] = term

    @pl.when(step > 0)
    def _():
        total[...] += term

    @pl.when(step == pl.num_programs(0) - 1)
    def _():
        for k, part in enumerate(parts):
            part[...] = total[k * size : (k + 1) * size].astype(BF)


def feed_own(normed, w_gate, w_up, grad_hidden, chunks, deps=()):
    tokens, units = grad_hidden.shape
    depth = w_gate.shape[0]
    size = tokens // chunks
    cols = tile(512, units)
    weight = pl.BlockSpec((depth, cols), lambda j: (0, j))
    block = pl.BlockSpec((tokens, cols), lambda j: (0, j))
    rows = pl.BlockSpec((size, depth), lambda j: (0, 0))
    out = pl.pallas_call(
        functools.partial(feed_own_kernel, len(normed), chunks),
        out_shape=(jax.ShapeDtypeStruct((tokens, units), BF),)
        + (jax.ShapeDtypeStruct((size, depth), BF),) * chunks,
        grid=(units // cols,),
        in_specs=[weight, weight, block] + [whole_spec(n) for n in normed] + unread(deps),
        out_specs=(block,) + (rows,) * chunks,
        scratch_shapes=[pltpu.VMEM((tokens, depth), BF), pltpu.VMEM((tokens, depth), F32)],
        compiler_params=kernel_params(1),
        cost_estimate=spent(18),
        name="feed_own",
    )(w_gate, w_up, grad_hidden, *normed, *deps)
    return out[0], list(out[1:])


def down_kernel(hidden, weight, *refs):
    keep, send = refs[-2:]
    part = contract(hidden[...], weight[...], 1, 0).astype(BF)
    rows = keep.shape[0]
    keep[...] = part[:rows]
    send[...] = part[rows:]


def down_projection(hidden, w_down, deps=()):
    tokens, units = hidden.shape
    depth = w_down.shape[1]
    cols = tile(512, depth)
    half = jax.ShapeDtypeStruct((tokens // 2, depth), BF)
    block = pl.BlockSpec((tokens // 2, cols), lambda j: (0, j))
    return pl.pallas_call(
        down_kernel,
        out_shape=(half, half),
        grid=(depth // cols,),
        in_specs=[whole_spec(hidden), pl.BlockSpec((units, cols), lambda j: (0, j))]
        + unread(deps),
        out_specs=(block, block),
        compiler_params=kernel_params(1),
        cost_estimate=spent(7),
        name="down_projection",
    )(hidden, w_down, *deps)


def add_half_kernel(keep, came, *refs):
    total = keep[...].astype(F32) + came[...].astype(F32)
    first, second = refs[-2:]
    rows = first.shape[0]
    first[...] = total[:rows].astype(BF)
    second[...] = total[rows:].astype(BF)


def add_half(keep, came, deps=()):
    rows, depth = keep.shape
    half = jax.ShapeDtypeStruct((rows // 2, depth), BF)
    return pl.pallas_call(
        add_half_kernel,
        out_shape=(half, half),
        grid=(1,),
        in_specs=[whole_spec(keep), whole_spec(came)] + unread(deps),
        out_specs=(whole_spec(half), whole_spec(half)),
        compiler_params=kernel_params(1),
        cost_estimate=spent(1),
        name="add_half",
    )(keep, came, *deps)


STEPS = 4


def weight_grad_kernel(count, pieces, core, *refs):
    lefts, rights = refs[:count], refs[count : 2 * count]
    wide, lows = refs[-1 - pieces], refs[-pieces:]
    total = contract(lefts[0][...], rights[0][...], 0, 0)
    for left, right in zip(lefts[1:], rights[1:]):
        total = total + contract(left[...], right[...], 0, 0)
    wide[...] = total
    for k, low in enumerate(lows):

        @pl.when(pl.program_id(1) == k)
        def _():
            low[...] = total.astype(BF)


def weight_grad(core, lefts, rights, dim, pieces, deps=()):
    tokens, m = lefts[0].shape
    n = rights[0].shape[1]
    count = len(lefts)
    rows, cols = m // pieces, tile(1024, n)
    across = n // cols
    if dim == 0:
        full = (2 * m, n)
        place = lambda j, i, c: (c[0] * pieces + i, j)
    else:
        full = (m, 2 * n)
        place = lambda j, i, c: (i, c[0] * across + j)
    share = 1

    def piece(k):
        last = share - 1
        return pl.BlockSpec(
            (rows, cols), lambda j, i, c: (jnp.clip(i - k * share, 0, last), j)
        )

    out = pl.pallas_call(
        functools.partial(weight_grad_kernel, count, pieces),
        out_shape=(jax.ShapeDtypeStruct(full, F32),)
        + (jax.ShapeDtypeStruct((rows * share, n), BF),) * pieces,
        grid_spec=pltpu.PrefetchScalarGridSpec(
            num_scalar_prefetch=1,
            grid=(across, pieces),
            in_specs=[pl.BlockSpec((tokens, rows), lambda j, i, c: (0, i))] * count
            + [pl.BlockSpec((tokens, cols), lambda j, i, c: (0, j))] * count
            + unread(deps),
            out_specs=(pl.BlockSpec((rows, cols), place),)
            + tuple(piece(k) for k in range(pieces)),
        ),
        compiler_params=kernel_params(2),
        cost_estimate=spent(19),
        name="weight_grad",
    )(core, *lefts, *rights, *deps)
    return out[0], list(out[1:])


def pair_grad_kernel(count, core, *refs):
    lefts = [r[...] for r in refs[:count]]
    wides, lows = refs[-4:-2], refs[-2:]
    for k in range(2):
        rights = refs[count * (k + 1) : count * (k + 2)]
        total = contract(lefts[0], rights[0][...], 0, 0)
        for left, right in zip(lefts[1:], rights[1:]):
            total = total + contract(left, right[...], 0, 0)
        wides[k][...] = total
        lows[k][0] = total.astype(BF)


def pair_grad(core, lefts, first, second, deps=()):
    tokens, m = lefts[0].shape
    n = first[0].shape[1]
    count = len(lefts)
    rows = m // STEPS
    wide = jax.ShapeDtypeStruct((m, 2 * n), F32)
    low = jax.ShapeDtypeStruct((1, m, n), BF)
    place = pl.BlockSpec((rows, n), lambda i, c: (i, c[0]))
    here = pl.BlockSpec((1, rows, n), lambda i, c: (0, i, 0))
    out = pl.pallas_call(
        functools.partial(pair_grad_kernel, count),
        out_shape=(wide, wide, low, low),
        grid_spec=pltpu.PrefetchScalarGridSpec(
            num_scalar_prefetch=1,
            grid=(STEPS,),
            in_specs=[pl.BlockSpec((tokens, rows), lambda i, c: (0, i))] * count
            + [whole_spec(v) for v in (*first, *second)]
            + unread(deps),
            out_specs=(place, place, here, here),
        ),
        compiler_params=kernel_params(1),
        cost_estimate=spent(34),
        name="pair_grad",
    )(core, *lefts, *first, *second, *deps)
    return out


def left_product_kernel(count, left, *refs):
    right = join(refs[:count])
    refs[-1][...] = contract(left[...], right, 0, 0).astype(BF)


def left_product(left, pieces, deps=()):
    tokens, m = left.shape
    n = pieces[0].shape[1]
    rows, cols = tile(1024, m), tile(512, n)
    return pl.pallas_call(
        functools.partial(left_product_kernel, len(pieces)),
        out_shape=jax.ShapeDtypeStruct((m, n), BF),
        grid=(m // rows, n // cols),
        in_specs=[pl.BlockSpec((tokens, rows), lambda i, j: (0, i))]
        + [pl.BlockSpec((p.shape[0], cols), lambda i, j: (0, j)) for p in pieces]
        + unread(deps),
        out_specs=pl.BlockSpec((rows, cols), lambda i, j: (i, j)),
        compiler_params=kernel_params(2),
        cost_estimate=spent(1),
        name="left_product",
    )(left, *pieces, *deps)


def kv_product_kernel(left, right, *refs):
    gains, out = refs[:-1], refs[-1]
    width = right.shape[1]
    out[:width, :] = contract(right[...], left[...], 0, 0).astype(BF)
    total = sum_chunks(gains)
    out[width:, :] = jnp.concatenate([total, jnp.zeros(total.shape, F32)], axis=0).astype(BF)


def kv_product(left, right, gains, deps=()):
    tokens, m = left.shape
    width = right.shape[1]
    cols = tile(1024, m)

    def kernel(*refs):
        kv_product_kernel(*refs[: 2 + len(gains)], refs[-1])

    return pl.pallas_call(
        kernel,
        out_shape=jax.ShapeDtypeStruct((width + 16, m), BF),
        grid=(m // cols,),
        in_specs=[pl.BlockSpec((tokens, cols), lambda i: (0, i)), whole_spec(right)]
        + [pl.BlockSpec((8, cols), lambda i: (0, i))] * len(gains)
        + unread(deps),
        out_specs=pl.BlockSpec((width + 16, cols), lambda i: (0, i)),
        compiler_params=kernel_params(1),
        cost_estimate=spent(1),
        name="kv_product",
    )(left, right, *gains, *deps)


def mask_kernel(chunks, scalars, place, *refs):
    value = join(refs[:chunks]).astype(F32)
    refs[-1][...] = jnp.where(place[...] < scalars[1], value, 0.0).astype(BF)


def mask_padding(scalars, value, place, chunks, half, deps=()):
    span, depth = value.shape
    rows = span // 2
    first = half * chunks // 2
    out = jax.ShapeDtypeStruct((rows, depth), BF)
    return pl.pallas_call(
        functools.partial(mask_kernel, chunks // 2),
        out_shape=out,
        grid_spec=pltpu.PrefetchScalarGridSpec(
            num_scalar_prefetch=1,
            grid=(1,),
            in_specs=[pl.BlockSpec((rows, 1), lambda i, c: (half, 0))]
            + [chunk_spec(value, chunks, k) for k in range(first, first + chunks // 2)]
            + unread(deps),
            out_specs=whole_spec(out),
        ),
        compiler_params=kernel_params(1),
        cost_estimate=spent(4),
        name="mask_padding",
    )(scalars, place, *[value] * (chunks // 2), *deps)


def pass_on_kernel(value, *refs):
    refs[-1][...] = value[...]


def pass_on(value, deps):
    return pl.pallas_call(
        pass_on_kernel,
        out_shape=jax.ShapeDtypeStruct(value.shape, value.dtype),
        grid=(1,),
        in_specs=[whole_spec(value)] + unread(deps),
        out_specs=whole_spec(value),
        compiler_params=kernel_params(1),
        cost_estimate=spent(2),
        name="pass_on",
    )(value, *deps)


def corner_kernel(value, out):
    out[...] = value[...]


def corner(value):
    return pl.pallas_call(
        corner_kernel,
        out_shape=jax.ShapeDtypeStruct((16, 128), value.dtype),
        grid=(1,),
        in_specs=[pl.BlockSpec((16, 128), lambda i: (0, 0))],
        out_specs=pl.BlockSpec((16, 128), lambda i: (0, 0)),
        compiler_params=kernel_params(1),
        cost_estimate=spent(5),
        name="corner",
    )(value)


def fill_other_kernel(pieces, core, *refs):
    step = pl.program_id(0)
    for k in range(pieces):

        @pl.when(step // (STEPS // pieces) == k)
        def _():
            refs[-1][...] = refs[k][...].astype(F32).reshape(refs[-1].shape)


def fill_other(core, others, index, held, dim, deps=()):
    pieces = len(others)
    share = STEPS // pieces
    rows, n = others[0].shape[1] // share, others[0].shape[2]
    if dim == 0:
        place = lambda i, c: ((1 - c[0]) * STEPS + i, 0)
    else:
        place = lambda i, c: (i, 1 - c[0])

    def piece(k):
        last = share - 1
        return pl.BlockSpec(
            (1, rows, n), lambda i, c: (index, jnp.clip(i - k * share, 0, last), 0)
        )

    return pl.pallas_call(
        functools.partial(fill_other_kernel, pieces),
        out_shape=jax.ShapeDtypeStruct(held.shape, F32),
        grid_spec=pltpu.PrefetchScalarGridSpec(
            num_scalar_prefetch=1,
            grid=(STEPS,),
            in_specs=[piece(k) for k in range(pieces)]
            + [pl.BlockSpec(memory_space=pl.ANY)]
            + unread(deps),
            out_specs=pl.BlockSpec((rows, n), place),
        ),
        input_output_aliases={1 + pieces: 0},
        compiler_params=kernel_params(1),
        cost_estimate=spent(87),
        name="fill_other",
    )(core, *others, held, *deps)


def rotate_block(values, cosine, sine):
    width = values.shape[1]
    column = lax.broadcasted_iota(jnp.int32, values.shape, 1)
    other = jnp.where(
        column % HEAD_SIZE < HEAD_SIZE // 2,
        pltpu.roll(values, width - HEAD_SIZE // 2, 1),
        pltpu.roll(values, HEAD_SIZE // 2, 1),
    )
    return values * cosine + other * sine


def pack_rotated(keys, values, cosine, sine):
    width = keys.shape[1]
    if width % 128 == 0:
        turned = [
            rotate_block(keys[:, i : i + 128], cosine, sine) for i in range(0, width, 128)
        ]
        return jnp.concatenate(turned + [values], axis=1)
    both = jnp.concatenate([keys, values], axis=1)
    column = lax.broadcasted_iota(jnp.int32, both.shape, 1)
    return jnp.where(column < width, rotate_block(both, cosine, sine), both)


def chunk_spec(array, chunks, k):
    block = (array.shape[0] // chunks, array.shape[1])
    return pl.BlockSpec(block, lambda *a: (a[-1][0] ^ k, 0))


def project_kv_kernel(chunks, waits, me, *refs):
    gain, key_w, value_w, cosine, sine = refs[chunks : chunks + 5]
    normed, inverse, packed = refs[-3:]
    stream = join(refs[:chunks]).astype(F32)
    scale = lax.rsqrt(jnp.mean(stream * stream, axis=1, keepdims=True) + EPSILON)
    low = (stream * scale * gain[...]).astype(BF)
    normed[...] = low
    inverse[...] = jnp.broadcast_to(scale, inverse.shape)
    packed[...] = pack_rotated(
        contract(low, key_w[...], 1, 0), contract(low, value_w[...], 1, 0), cosine[...], sine[...]
    ).astype(BF)


def project_kv(me, x, gain, key_matrix, value_matrix, cosine, sine, chunks, deps=()):
    span, depth = x.shape
    args = (gain, key_matrix, value_matrix, cosine, sine)
    outs = (
        jax.ShapeDtypeStruct((span, depth), BF),
        jax.ShapeDtypeStruct((span, 128), F32),
        jax.ShapeDtypeStruct((span, 2 * key_matrix.shape[1]), BF),
    )
    return pl.pallas_call(
        functools.partial(project_kv_kernel, chunks, len(deps)),
        out_shape=outs,
        grid_spec=pltpu.PrefetchScalarGridSpec(
            num_scalar_prefetch=1,
            grid=(1,),
            in_specs=[chunk_spec(x, chunks, k) for k in range(chunks)]
            + [whole_spec(a) for a in args]
            + unread(deps),
            out_specs=tuple(whole_spec(a) for a in outs),
        ),
        compiler_params=kernel_params(1),
        cost_estimate=spent(4),
        name="project_kv",
    )(me, *[x] * chunks, *args, *deps)


def project_query_kernel(normed, weight, cosine, sine, *refs):
    out = refs[-1]
    lin = contract(normed[...], weight[...], 1, 0)
    for i in range(0, lin.shape[1], 128):
        turned = rotate_block(lin[:, i : i + 128], cosine[...], sine[...])
        out[:, i : i + 128] = (turned * HEAD_SIZE**-0.5).astype(BF)


def project_query(normed, w_query, cosine, sine, deps=()):
    span, depth = normed.shape
    width = w_query.shape[1]
    cols = 256
    return pl.pallas_call(
        project_query_kernel,
        out_shape=jax.ShapeDtypeStruct((span, width), BF),
        grid=(width // cols,),
        in_specs=[
            whole_spec(normed),
            pl.BlockSpec((depth, cols), lambda j: (0, j)),
            whole_spec(cosine),
            whole_spec(sine),
        ]
        + unread(deps),
        out_specs=pl.BlockSpec((span, cols), lambda j: (0, j)),
        compiler_params=kernel_params(1),
        cost_estimate=spent(4),
        name="project_query",
    )(normed, w_query, cosine, sine, *deps)


def head_columns(array, index):
    return array[:, index * HEAD_SIZE : (index + 1) * HEAD_SIZE]


def stack_heads(array, heads):
    return jnp.concatenate([head_columns(array, h) for h in heads], axis=0)


def store_heads(out, turned, first, span, finish):
    for i in range(0, turned.shape[1] // span, 2):
        pair = jnp.concatenate(
            [turned[:, (i + e) * span : (i + e + 1) * span] for e in range(2)], axis=0
        )
        at = (first + i) * HEAD_SIZE
        out[:, at : at + 128] = finish(jnp.transpose(pair)).astype(BF)


def attend_kernel(blocks, chunks, shift, query, place, place_row, begin_row, w_output, *refs):
    packed = refs[:blocks]
    attended, stats, *parts = refs[-2 - chunks :]
    span, width = query.shape
    heads_kv = packed[0].shape[1] // (2 * HEAD_SIZE)
    group = width // HEAD_SIZE // heads_kv
    last = jnp.concatenate([place_row[...]] * group, axis=1)
    first = jnp.concatenate([begin_row[...]] * group, axis=1)
    for g in range(heads_kv):
        q = stack_heads(query, range(g * group, (g + 1) * group))
        top = total = mixed = None
        for j in range(blocks):
            keys = head_columns(packed[j], g)
            values = head_columns(packed[j], heads_kv + g)
            key_place = place[...] + shift[j]
            allowed = (key_place >= first) & (key_place <= last)
            masked = jnp.where(allowed, contract(keys, q, 1, 1), -1e30)
            peak = jnp.max(masked, axis=0, keepdims=True)
            peak = peak if j == 0 else jnp.maximum(top, peak)
            terms = jnp.exp(masked - peak)
            amount = jnp.sum(terms, axis=0, keepdims=True)
            term = contract(values, terms.astype(BF), 0, 0)
            if j == 0:
                total, mixed = amount, term
            else:
                fade = jnp.exp(top - peak)
                total, mixed = total * fade + amount, mixed * fade + term
            top = peak
        stats[g : g + 1, :] = top + jnp.log(total)
        store_heads(attended, mixed * (1.0 / total), g * group, span, lambda v: v)
    part = contract(attended[...], w_output[...], 1, 0)
    chunk = span // len(parts)
    for k, out in enumerate(parts):
        out[...] = part[k * chunk : (k + 1) * chunk].astype(BF)


def attend(shift, query, packed, places, w_output, chunks, deps=()):
    span, width = query.shape
    depth = w_output.shape[1]
    blocks = len(packed)
    heads_kv = packed[0].shape[1] // (2 * HEAD_SIZE)
    args = (
        query,
        *places,
        w_output,
        *packed,
    )
    outs = (
        jax.ShapeDtypeStruct((span, width), BF),
        jax.ShapeDtypeStruct((heads_kv, width // HEAD_SIZE // heads_kv * span), F32),
    )
    outs += (jax.ShapeDtypeStruct((span // chunks, depth), BF),) * chunks
    out = pl.pallas_call(
        functools.partial(attend_kernel, blocks, chunks),
        out_shape=outs,
        grid_spec=pltpu.PrefetchScalarGridSpec(
            num_scalar_prefetch=1,
            grid=(1,),
            in_specs=[whole_spec(a) for a in args] + unread(deps),
            out_specs=tuple(whole_spec(a) for a in outs),
        ),
        compiler_params=kernel_params(1),
        cost_estimate=spent(11),
        name="attend",
    )(shift, *args, *deps)
    return out[0], out[1], list(out[2:])


def sum_chunks(refs):
    total = refs[0][...].astype(F32)
    for ref in refs[1:]:
        total = total + ref[...].astype(F32)
    return total


def middle_kernel(count, me, x, gain, *refs):
    chunks, (middle, inverse, normed) = refs[:count], refs[-3:]
    stream = x[...].astype(F32) + sum_chunks(chunks)
    scale = lax.rsqrt(jnp.mean(stream * stream, axis=1, keepdims=True) + EPSILON)
    middle[...] = stream
    inverse[...] = jnp.broadcast_to(scale, inverse.shape)
    normed[...] = (stream * scale * gain[...]).astype(BF)


def middle_norm(me, x, gain, chunks, deps=()):
    rows, depth = chunks[0].shape
    outs = (
        jax.ShapeDtypeStruct((rows, depth), F32),
        jax.ShapeDtypeStruct((rows, 128), F32),
        jax.ShapeDtypeStruct((rows, depth), BF),
    )
    return pl.pallas_call(
        functools.partial(middle_kernel, len(chunks)),
        out_shape=outs,
        grid_spec=pltpu.PrefetchScalarGridSpec(
            num_scalar_prefetch=1,
            grid=(1,),
            in_specs=[chunk_spec(x, len(chunks), 0)]
            + [whole_spec(a) for a in (gain, *chunks)]
            + unread(deps),
            out_specs=tuple(whole_spec(a) for a in outs),
        ),
        compiler_params=kernel_params(1),
        cost_estimate=spent(120),
        name="middle_norm",
    )(me, x, gain, *chunks, *deps)


def halves_kernel(count, *refs):
    half = count // 2
    refs[-2][...] = join(refs[:half])
    refs[-1][...] = join(refs[half:count])


def join_halves(chunks, deps=()):
    rows, depth = chunks[0].shape
    outs = (jax.ShapeDtypeStruct((rows * len(chunks) // 2, depth), BF),) * 2
    return pl.pallas_call(
        functools.partial(halves_kernel, len(chunks)),
        out_shape=outs,
        grid=(1,),
        in_specs=[whole_spec(a) for a in chunks] + unread(deps),
        out_specs=tuple(whole_spec(a) for a in outs),
        compiler_params=kernel_params(1),
        cost_estimate=spent(2),
        name="join_halves",
    )(*chunks, *deps)


def norm_gradient(grad, rows, scale, gain):
    scaled = grad * gain
    product = jnp.mean(scaled * rows, axis=1, keepdims=True)
    gain_grad = jnp.sum(grad * rows * scale, axis=0, keepdims=True)
    return scale * scaled - rows * (scale * scale * scale * product), gain_grad


def norm_back_kernel(count, upstream, middle, inverse, gain, *refs):
    chunks, (wide, low, gain_grad) = refs[:count], refs[-3:]
    grad, gain_grad[...] = norm_gradient(
        sum_chunks(chunks), middle[...], inverse[:, :1], gain[...]
    )
    total = upstream[...].astype(F32) + grad
    wide[...] = total
    low[...] = total.astype(BF)


def norm_back(upstream, middle, inverse, gain, chunks, deps=()):
    rows, depth = middle.shape
    args = (middle, inverse, gain, *chunks)
    outs = (
        jax.ShapeDtypeStruct((rows, depth), F32),
        jax.ShapeDtypeStruct((rows, depth), BF),
        jax.ShapeDtypeStruct((1, depth), F32),
    )
    return pl.pallas_call(
        functools.partial(norm_back_kernel, len(chunks)),
        out_shape=outs,
        grid=(1,),
        in_specs=[pl.BlockSpec((rows, depth), lambda i: (0, 0))]
        + [whole_spec(a) for a in args]
        + unread(deps),
        out_specs=tuple(whole_spec(a) for a in outs),
        compiler_params=kernel_params(1),
        cost_estimate=spent(3),
        name="norm_back",
    )(upstream, *args, *deps)


def finish_kernel(count, me, x, inverse, gain, grad_middle, block, *refs):
    grad, _ = norm_gradient(
        sum_chunks(refs[:count]), x[...].astype(F32), inverse[:, :1], gain[...]
    )
    refs[-1][...] = jnp.concatenate([grad_middle[...] + grad, block[...]], axis=0).astype(BF)


def finish(me, x, inverse, gain, grad_middle, block, chunks, deps=()):
    rows, depth = grad_middle.shape
    args = (gain, grad_middle, block, *chunks)
    outs = jax.ShapeDtypeStruct((2 * rows, depth), BF)
    return pl.pallas_call(
        functools.partial(finish_kernel, len(chunks)),
        out_shape=outs,
        grid_spec=pltpu.PrefetchScalarGridSpec(
            num_scalar_prefetch=1,
            grid=(1,),
            in_specs=[
                chunk_spec(x, len(chunks), 0),
                pl.BlockSpec((rows, 128), lambda i, c: (0, 0)),
            ]
            + [whole_spec(a) for a in args]
            + unread(deps),
            out_specs=whole_spec(outs),
        ),
        compiler_params=kernel_params(1),
        cost_estimate=spent(3),
        name="finish",
    )(me, x, inverse, *args, *deps)


def add_kernel(count, *refs):
    refs[-1][...] = sum_chunks(refs[:count]).astype(refs[-1].dtype)


def add_up(arrays, dtype, deps=()):
    out = jax.ShapeDtypeStruct(arrays[0].shape, dtype)
    return pl.pallas_call(
        functools.partial(add_kernel, len(arrays)),
        out_shape=out,
        grid=(1,),
        in_specs=[whole_spec(a) for a in arrays] + unread(deps),
        out_specs=whole_spec(out),
        compiler_params=kernel_params(1),
        cost_estimate=spent(2),
        name="add_up",
    )(*arrays, *deps)


def restore_kernel(count, me, *refs):
    step = pl.program_id(0)
    gains, (first, second, gains_out) = refs[count], refs[-3:]
    gains_out[...] = gains[...]
    for k in range(count):

        @pl.when(step == k)
        def _():
            rows = refs[k].shape[0] // 2
            first[...] = refs[k][:rows]
            second[...] = refs[k][rows:]


def restore(me, pieces, gains, deps=()):
    count = len(pieces)
    rows, depth = pieces[0].shape[0] // 2, pieces[0].shape[1]
    if rows % 16:
        halves = [[p[:rows] for p in pieces], [p[rows:] for p in pieces]]
        return [reorder(jnp.concatenate(h, axis=0), "tensor") for h in halves] + [gains]
    out = jax.ShapeDtypeStruct((count * rows, depth), BF)
    place = pl.BlockSpec((rows, depth), lambda i, c: (c[0] ^ i, 0))
    return pl.pallas_call(
        functools.partial(restore_kernel, count),
        out_shape=(out, out, jax.ShapeDtypeStruct(gains.shape, F32)),
        grid_spec=pltpu.PrefetchScalarGridSpec(
            num_scalar_prefetch=1,
            grid=(count,),
            in_specs=[whole_spec(p) for p in (*pieces, gains)] + unread(deps),
            out_specs=(place, place, whole_spec(gains)),
        ),
        compiler_params=kernel_params(1),
        cost_estimate=spent(87),
        name="restore",
    )(me, *pieces, gains, *deps)


def widen(wo, wq, wkv, width, deps=()):
    steps = 4
    depth = wq.shape[0]
    shapes = [wo.shape, wq.shape, (depth, width), (depth, width)]

    def spec(shape):
        return pl.BlockSpec((shape[0] // steps, shape[1]), lambda i: (i, 0))

    def kernel(wo, wq, wkv, *refs):
        wo_out, wq_out, wk_out, wv_out, gains = refs[-5:]
        wo_out[...] = wo[...].astype(F32)
        wq_out[...] = wq[...].astype(F32)
        turned = jnp.transpose(wkv[: 2 * width, :].astype(F32))
        wk_out[...] = turned[:, :width]
        wv_out[...] = turned[:, width:]
        gains[...] = wkv[2 * width :, :].astype(F32)[:8]

    return pl.pallas_call(
        kernel,
        out_shape=tuple(jax.ShapeDtypeStruct(v, F32) for v in [*shapes, (8, depth)]),
        grid=(steps,),
        in_specs=[
            spec(wo.shape),
            spec(wq.shape),
            pl.BlockSpec((wkv.shape[0], depth // steps), lambda i: (0, i)),
        ]
        + unread(deps),
        out_specs=tuple(spec(v) for v in shapes)
        + (pl.BlockSpec((8, depth // steps), lambda i: (0, i)),),
        compiler_params=kernel_params(1),
        cost_estimate=spent(8),
        name="widen",
    )(wo, wq, wkv, *deps)


def gain_sum_kernel(count, *refs):
    total = sum_chunks(refs[:count])
    refs[-2][...] = total[:1]
    refs[-1][...] = total[1:2]


def gain_sum(pieces, deps=()):
    out = jax.ShapeDtypeStruct((1, pieces[0].shape[1]), F32)
    return pl.pallas_call(
        functools.partial(gain_sum_kernel, len(pieces)),
        out_shape=(out, out),
        grid=(1,),
        in_specs=[whole_spec(p) for p in pieces] + unread(deps),
        out_specs=(whole_spec(out), whole_spec(out)),
        compiler_params=kernel_params(1),
        cost_estimate=spent(2),
        name="gain_sum",
    )(*pieces, *deps)


def attend_back_kernel(blocks, count, shift, query, attended, stats, place, place_row, begin_row,
                       cosine, sine, w_output, *refs):
    packed = refs[:blocks]
    chunks = refs[blocks : blocks + count]
    grad_query = refs[-1 - blocks]
    terms = refs[-blocks:]
    span, width = query.shape
    heads_kv = packed[0].shape[1] // (2 * HEAD_SIZE)
    group = width // HEAD_SIZE // heads_kv
    grad_middle = join(chunks)
    grad_attended = contract(grad_middle, w_output[...], 1, 1).astype(BF)
    last = jnp.concatenate([place_row[...]] * group, axis=1)
    first = jnp.concatenate([begin_row[...]] * group, axis=1)
    key_terms = [[] for _ in range(blocks)]
    value_terms = [[] for _ in range(blocks)]
    for g in range(heads_kv):
        mine = range(g * group, (g + 1) * group)
        q = stack_heads(query, mine)
        grad = stack_heads(grad_attended, mine)
        norm = stats[g : g + 1, :]
        inner = lax.dot_general(
            jnp.ones((8, HEAD_SIZE), F32),
            grad.astype(F32) * stack_heads(attended, mine).astype(F32),
            (((1,), (1,)), ((), ())),
            preferred_element_type=F32,
            precision=lax.Precision.HIGHEST,
        )[:1]
        total = None
        for j in range(blocks):
            keys = head_columns(packed[j], g)
            values = head_columns(packed[j], heads_kv + g)
            key_place = place[...] + shift[j]
            allowed = (key_place >= first) & (key_place <= last)
            scores = contract(keys, q, 1, 1)
            probs = jnp.exp(jnp.where(allowed, scores - norm, -1e30))
            grad_scores = (probs * (contract(values, grad, 1, 1) - inner)).astype(BF)
            value_terms[j].append(contract(probs.astype(BF), grad, 1, 0))
            key_terms[j].append(contract(grad_scores, q, 1, 0))
            term = contract(keys, grad_scores, 0, 0)
            total = term if total is None else total + term
        store_heads(
            grad_query,
            total,
            g * group,
            span,
            lambda v: rotate_block(v * HEAD_SIZE**-0.5, cosine[...], -sine[...]),
        )
    for j in range(blocks):
        terms[j][...] = jnp.concatenate(key_terms[j] + value_terms[j], axis=1).astype(BF)


def attend_back(shift, query, attended, stats, packed, places, cosine, sine, w_output, chunks,
                deps=()):
    span, width = query.shape
    blocks = len(packed)
    args = (
        query,
        attended,
        stats,
        *places,
        cosine,
        sine,
        w_output,
        *packed,
        *chunks,
    )
    outs = (jax.ShapeDtypeStruct((span, width), BF),)
    outs += (jax.ShapeDtypeStruct(packed[0].shape, BF),) * blocks
    out = pl.pallas_call(
        functools.partial(attend_back_kernel, blocks, len(chunks)),
        out_shape=outs,
        grid_spec=pltpu.PrefetchScalarGridSpec(
            num_scalar_prefetch=1,
            grid=(1,),
            in_specs=[whole_spec(a) for a in args] + unread(deps),
            out_specs=tuple(whole_spec(a) for a in outs),
        ),
        compiler_params=kernel_params(1),
        cost_estimate=spent(16),
        name="attend_back",
    )(shift, *args, *deps)
    return out[0], list(out[1:])


def input_back_kernel(
    count, chunks, me, grad_query, w_query, key_w, value_w, cosine, sine, inverse, gain_two, *refs
):
    terms, rows = refs[:count], refs[count : count + chunks]
    lin, gains, *parts = refs[-2 - chunks :]
    normed = join(rows).astype(F32) * inverse[:, :1]
    width = key_w.shape[1]
    total = sum_chunks(terms)
    low = pack_rotated(total[:, :width], total[:, width:], cosine[...], -sine[...]).astype(BF)
    lin[...] = low
    part = contract(grad_query[...], w_query[...], 1, 1)
    part = part + contract(low[:, :width], key_w[...], 1, 1)
    part = part + contract(low[:, width:], value_w[...], 1, 1)
    rows = part.shape[0] // chunks
    for k, out in enumerate(parts):
        out[...] = part[k * rows : (k + 1) * rows].astype(BF)
    gain_one = jnp.sum(part * normed, axis=0, keepdims=True)
    empty = jnp.zeros((6, part.shape[1]), F32)
    gains[...] = jnp.concatenate([gain_one, gain_two[...], empty], axis=0)


def input_back(
    me,
    grad_query,
    w_query,
    key_matrix,
    value_matrix,
    cosine,
    sine,
    inverse,
    x,
    gain_two,
    terms,
    chunks,
    deps=(),
):
    span = grad_query.shape[0]
    depth = w_query.shape[0]
    args = (grad_query, w_query, key_matrix, value_matrix, cosine, sine, inverse, gain_two)
    args += tuple(terms)
    outs = (
        jax.ShapeDtypeStruct(terms[0].shape, BF),
        jax.ShapeDtypeStruct((8, depth), F32),
    )
    outs += (jax.ShapeDtypeStruct((span // chunks, depth), BF),) * chunks
    out = pl.pallas_call(
        functools.partial(input_back_kernel, len(terms), chunks),
        out_shape=outs,
        grid_spec=pltpu.PrefetchScalarGridSpec(
            num_scalar_prefetch=1,
            grid=(1,),
            in_specs=[whole_spec(a) for a in args]
            + [chunk_spec(x, chunks, k) for k in range(chunks)]
            + unread(deps),
            out_specs=tuple(whole_spec(a) for a in outs),
        ),
        compiler_params=kernel_params(1),
        cost_estimate=spent(1),
        name="input_back",
    )(me, *args, *[x] * chunks, *deps)
    return out[0], out[1], list(out[2:])


def rope_tables(positions):
    expo = np.arange(HEAD_SIZE // 2, dtype=np.float64) * 2.0 / HEAD_SIZE
    inverse = 1.0 / 500000.0**expo
    wavelength = 2.0 * np.pi / inverse
    smooth = (8192.0 / wavelength - 1.0) / 3.0
    middle = (1.0 - smooth) * inverse / 32.0 + smooth * inverse
    scaled = np.where(
        wavelength < 2048.0, inverse, np.where(wavelength > 8192.0, inverse / 32.0, middle)
    )
    scaled = jnp.asarray(np.tile(scaled, 4)[None, :].astype(np.float32))
    sign = jnp.asarray(np.tile(np.repeat([-1.0, 1.0], HEAD_SIZE // 2), 2)[None, :].astype(np.float32))
    angles = positions.astype(F32)[:, None] * scaled
    return jnp.cos(angles), jnp.sin(angles) * sign


def flip(value, axis, mask):
    return lax.ppermute(value, axis, [(i, i ^ mask) for i in range(lax.axis_size(axis))])


def reorder(value, axis):
    n = lax.axis_size(axis)
    me = lax.axis_index(axis)
    chunk = value.shape[0] // n
    return jnp.concatenate(
        [lax.dynamic_slice_in_dim(value, (me ^ k) * chunk, chunk, 0) for k in range(n)], axis=0
    )


def exchange(chunks, axis):
    return chunks[:1] + [flip(chunks[k], axis, k) for k in reversed(range(1, len(chunks)))]


def spread(chunk, axis):
    return [chunk] + [flip(chunk, axis, k) for k in range(1, lax.axis_size(axis))]


def gather_halves(first, second):
    return [
        lax.all_gather(first, ("rows", "seq"), axis=0, tiled=True),
        lax.all_gather(second, ("seq", "rows"), axis=0, tiled=True),
    ]


def per_device(
    activations,
    doc_lengths,
    w_query,
    key_matrix,
    value_matrix,
    w_output,
    w_gate,
    w_up,
    w_down,
    gain_attn,
    gain_ffn,
    cotangent,
):
    span = activations.shape[1]
    blocks = lax.axis_size("seq")
    chunks = lax.axis_size("tensor")
    chunk = span // chunks
    core = lax.axis_index("rows").astype(jnp.int32).reshape(1)
    block_here = lax.axis_index("seq")
    gain_attn = gain_attn.reshape(1, -1)
    gain_ffn = gain_ffn.reshape(1, -1)
    stream, cotangent = activations[0], cotangent[0]
    me = lax.axis_index("tensor").astype(jnp.int32)
    token = jnp.arange(span, dtype=jnp.int32)
    place = block_here * span + (me ^ (token // chunk)) * chunk + token % chunk
    if chunk % 16:
        stream, cotangent = reorder(stream, "tensor"), reorder(cotangent, "tensor")
        me = jnp.zeros_like(me)
    order = jnp.arange(DOCS, dtype=jnp.int32)
    ends = jnp.sum(jnp.where(order[None, :] <= order[:, None], doc_lengths[0][None, :], 0), axis=1)
    begin = jnp.max(jnp.where(place[:, None] >= ends[None, :], ends[None, :], 0), axis=1)
    cosine, sine = rope_tables(place - begin)
    shift = ((block_here ^ jnp.arange(blocks)) - block_here) * span
    shift = shift.astype(jnp.int32)
    scalars = jnp.where(order[:2] == 0, me, ends[-1]).astype(jnp.int32)
    places = (place.reshape(span, 1), place.reshape(1, span), begin.reshape(1, span))

    normed_one, inverse_one, packed = project_kv(
        scalars, stream, gain_attn, key_matrix, value_matrix, cosine, sine, chunks, (shift, *places)
    )
    packed = spread(packed, "seq")
    query = project_query(normed_one, w_query, cosine, sine)
    upstream = [mask_padding(scalars, cotangent, places[0], chunks, 0, (query, *packed))]
    upstream_all = [lax.all_gather(upstream[0], ("rows", "seq"), axis=0, tiled=True)]
    attended, stats, parts = attend(
        shift, query, packed, places, w_output, chunks, (upstream[0],)
    )
    upstream.append(mask_padding(scalars, cotangent, places[0], chunks, 1, (parts[0],)))
    upstream_all.append(lax.all_gather(upstream[1], ("seq", "rows"), axis=0, tiled=True))

    sent = exchange(parts, "tensor")
    grad_hidden = grad_hidden_of(core, upstream, w_down, 1, (parts[0],))
    middle, inverse_two, normed = middle_norm(scalars, stream, gain_ffn, sent, (grad_hidden,))

    grad_hidden_first = grad_hidden_of(core, upstream_all[:1], w_down, 2, (middle,))
    normed = join_halves(spread(normed, "tensor"), (grad_hidden_first,))
    normed_all = gather_halves(*normed)
    hidden, parts = feed_own(normed, w_gate, w_up, grad_hidden, chunks)

    sent = exchange(parts, "tensor")
    grad_hidden_second = grad_hidden_of(core, upstream_all[1:], w_down, 2, (parts[0],))
    grad_middle, grad_middle_low, gain_two = norm_back(
        upstream[0], middle, inverse_two, gain_ffn, sent, (grad_hidden_second,)
    )
    grad_middle_all = spread(grad_middle_low, "tensor")
    feed_first = feed_half(
        core, normed_all[0], w_gate, w_up, grad_hidden_first, (grad_middle,)
    )
    down_parts = down_projection(hidden, w_down, (feed_first[0],))
    down_send = pass_on(down_parts[1], grad_middle_all)
    grad_query, kv_terms = attend_back(
        shift,
        query,
        attended,
        stats,
        packed,
        places,
        cosine,
        sine,
        w_output,
        grad_middle_all,
        (corner(down_send),),
    )
    mask = chunks // 2
    down_came = flip(down_send, "tensor", mask)

    kv_sent = exchange(kv_terms, "seq")
    wq_part = left_product(normed_one, [grad_query])
    wo_part = left_product(attended, grad_middle_all, (wq_part,))
    grad_kv, gains, parts = input_back(
        scalars,
        grad_query,
        w_query,
        key_matrix,
        value_matrix,
        cosine,
        sine,
        inverse_one,
        stream,
        gain_two,
        kv_sent,
        chunks,
        (wo_part, normed_all[1]),
    )

    wkv_part = kv_product(normed_one, grad_kv, [gains])
    sent = exchange(parts, "tensor")
    grad_wo, grad_wq, grad_wkv = lax.psum((wo_part, wq_part, wkv_part), ("rows", "seq"))
    keep, send = add_half(down_parts[0], down_came, (wkv_part,))
    while mask > 2:
        mask //= 2
        keep, send = add_half(keep, flip(send, "tensor", mask))
    feed_second = feed_half(
        core, normed_all[1], w_gate, w_up, grad_hidden_second, (keep,)
    )
    hidden_all, grad_gate_all, grad_up_all = zip(feed_first, feed_second)
    grad_down, low = weight_grad(core, hidden_all, upstream_all, 0, 2)
    down_other = [flip(v[None], "rows", 1) for v in low]
    block_chunk = add_up(
        [middle, keep, flip(send, "tensor", mask // 2)], F32, (grad_down,)
    )
    both = finish(
        scalars, stream, inverse_one, gain_attn, grad_middle, block_chunk, sent
    )
    both_all = spread(both, "tensor")
    grad_gate_w, grad_up_w, *low = pair_grad(
        core, normed_all, grad_gate_all, grad_up_all, (both,)
    )
    gate_other, up_other = [flip(v, "rows", 1) for v in low]
    grad_down = fill_other(core, down_other, 0, grad_down, 0, (grad_up_w,))
    grad_gate_w = fill_other(core, [gate_other], 0, grad_gate_w, 1, (grad_down,))
    grad_wo, grad_wq, grad_wk, grad_wv, gains = widen(
        grad_wo, grad_wq, grad_wkv, key_matrix.shape[1], (grad_gate_w,)
    )
    grad_input, block_output, gains = restore(scalars, both_all, gains)
    grad_up_w = fill_other(core, [up_other], 0, grad_up_w, 1, (gains,))
    gains = gain_sum(spread(gains, "tensor"), (grad_up_w,))
    return (
        block_output[None],
        grad_input[None],
        grad_wq,
        grad_wk,
        grad_wv,
        grad_wo,
        grad_gate_w,
        grad_up_w,
        grad_down,
        gains[0].reshape(-1),
        gains[1].reshape(-1),
    )


def solution(mesh):
    placed = (
        P("rows", "seq", None),
        P("rows", None),
        P(None, "tensor"),
        P(None, "tensor"),
        P(None, "tensor"),
        P("tensor", None),
        P(None, "tensor"),
        P(None, "tensor"),
        P("tensor", None),
        P(),
        P(),
        P("rows", "seq", None),
    )
    return jax.shard_map(
        per_device,
        mesh=mesh,
        in_specs=placed,
        out_specs=(
            P("rows", "seq", None),
            P("rows", "seq", None),
            P(None, "tensor"),
            P(None, "tensor"),
            P(None, "tensor"),
            P("tensor", None),
            P(None, "tensor"),
            P(None, "tensor"),
            P("tensor", None),
            P(),
            P(),
        ),
        check_vma=False,
    )
```
